32 devices in a mesh: pipe: 2 (over core), rows: 16 (over z, y, x).
Axes of the slice: x: 2, y: 2, z: 4, core: 2. Of those that a mesh axis runs over, the one named last changes fastest.
Arguments:
- image_tokens: bfloat16 [2, 224, 112, 384], P(None, 'rows'), may hold values from -6 to 6
- out_grad: bfloat16 [2, 224, 112, 384], P(None, 'rows'), may hold values from -6 to 6
- first_gain: bfloat16 [2, 384], P('pipe'), may hold values from 0.099609375 to 1.8984375
- first_shift: bfloat16 [2, 384], P('pipe'), may hold values from -3 to 3
- triple_weight: bfloat16 [2, 384, 1152], P('pipe'), may hold values from -0.3125 to 0.3125
- query_bias: bfloat16 [2, 384], P('pipe'), may hold values from -3 to 3
- value_bias: bfloat16 [2, 384], P('pipe'), may hold values from -3 to 3
- bias_table: bfloat16 [2, 169, 12], P('pipe'), may hold values from -4 to 4
- attend_weight: bfloat16 [2, 384, 384], P('pipe'), may hold values from -2 to 2
- attend_bias: bfloat16 [2, 384], P('pipe'), may hold values from -3 to 3
- second_gain: bfloat16 [2, 384], P('pipe'), may hold values from 0.099609375 to 1.8984375
- second_shift: bfloat16 [2, 384], P('pipe'), may hold values from -3 to 3
- widen_weight: bfloat16 [2, 384, 1536], P('pipe'), may hold values from -0.3125 to 0.3125
- widen_bias: bfloat16 [2, 1536], P('pipe'), may hold values from -3 to 3
- narrow_weight: bfloat16 [2, 1536, 384], P('pipe'), may hold values from -0.15625 to 0.15625
- narrow_bias: bfloat16 [2, 384], P('pipe'), may hold values from -3 to 3
Outputs:
- block_outputs: bfloat16 [2, 2, 224, 112, 384], P('pipe', None, 'rows')
- input_grads: bfloat16 [2, 2, 224, 112, 384], P('pipe', None, 'rows')
- slope_first_gain: float32 [2, 384], P('pipe')
- slope_first_shift: float32 [2, 384], P('pipe')
- slope_triple_weight: float32 [2, 384, 1152], P('pipe')
- slope_query_bias: float32 [2, 384], P('pipe')
- slope_value_bias: float32 [2, 384], P('pipe')
- slope_bias_table: float32 [2, 169, 12], P('pipe')
- slope_attend_weight: float32 [2, 384, 384], P('pipe')
- slope_attend_bias: float32 [2, 384], P('pipe')
- slope_second_gain: float32 [2, 384], P('pipe')
- slope_second_shift: float32 [2, 384], P('pipe')
- slope_widen_weight: float32 [2, 384, 1536], P('pipe')
- slope_widen_bias: float32 [2, 1536], P('pipe')
- slope_narrow_weight: float32 [2, 1536, 384], P('pipe')
- slope_narrow_bias: float32 [2, 384], P('pipe')
The draws below stay inside these ranges and needn't reach their ends.
All inputs are finite; a program needn't handle non-finite values.
Results may differ from the reference program's by a relative error of at most 0.015.
Values may be sent and summed in bfloat16 or wider, within the bound.
No kernel may reach another device: no remote copies, remote signals or barrier semaphores. Data moves between devices by JAX's collectives and lax.ppermute only.
A program may use at most 448 MiB of HBM per device.

```python
from functools import partial
import jax
import jax.numpy as jnp
from jax import lax

C = 384
HEADS = 12
HIDDEN_SIZE = 1536
WID = 112
MICRO = 2
HGT = 224


def level_of(key, extent, cuts, smallest, high):
    def one(position, shards_of):
        draws = jax.random.uniform(jax.random.fold_in(jax.random.fold_in(key, 6), position), (shards_of,), jnp.float32, smallest / len(cuts), high / len(cuts))
        return jnp.repeat(jnp.exp(draws), extent[position] // shards_of).reshape((-1,) + (1,) * (len(extent) - position - 1))

    level = one(*cuts[0])
    for cut in cuts[1:]:
        level = level * one(*cut)
    return level


def normal_values(rng, dims, width, bound, pieces=(), kind=jnp.bfloat16):
    level = level_of(rng, dims, pieces, -0.22, 0.18) if pieces else 1.0
    drawn = jax.random.normal(rng, dims, jnp.float32) * width * level
    return jnp.minimum(jnp.maximum(drawn, -bound), bound).astype(kind)


def setup_inputs(seed: int = 0) -> dict:
    key_of = jax.random.split(jax.random.key(seed), 17)
    return {
        "image_tokens": normal_values(key_of[0], (MICRO, HGT, WID, C), 1.0, 6.0, ((1, 16),)),
        "out_grad": normal_values(key_of[1], (MICRO, HGT, WID, C), 1.0, 6.0, ((1, 16),)),
        "first_gain": jnp.clip(1.0 + 0.18 * jax.random.normal(key_of[2], (2, C), jnp.float32), 0.099609375, 1.8984375).astype(jnp.bfloat16),
        "first_shift": normal_values(key_of[3], (2, C), 0.5, 3.0, ((0, 2),)),
        "triple_weight": normal_values(key_of[4], (2, C, 3 * C), C ** -0.5, 0.3125, ((0, 2),)),
        "query_bias": normal_values(key_of[5], (2, C), 0.5, 3.0, ((0, 2),)),
        "value_bias": normal_values(key_of[6], (2, C), 0.5, 3.0, ((0, 2),)),
        "bias_table": normal_values(key_of[7], (2, 169, HEADS), 1.0, 4.0, ((0, 2),)),
        "attend_weight": normal_values(key_of[8], (2, C, C), (max(C // 49, 1)) ** -0.5, 2.0, ((0, 2),)),
        "attend_bias": normal_values(key_of[9], (2, C), 0.3, 3.0, ((0, 2),)),
        "second_gain": jnp.clip(1.0 + 0.18 * jax.random.normal(key_of[10], (2, C), jnp.float32), 0.099609375, 1.8984375).astype(jnp.bfloat16),
        "second_shift": normal_values(key_of[11], (2, C), 0.5, 3.0, ((0, 2),)),
        "widen_weight": normal_values(key_of[12], (2, C, HIDDEN_SIZE), C ** -0.5, 0.3125, ((0, 2),)),
        "widen_bias": normal_values(key_of[13], (2, HIDDEN_SIZE), 0.5, 3.0, ((0, 2),)),
        "narrow_weight": normal_values(key_of[14], (2, HIDDEN_SIZE, C), HIDDEN_SIZE ** -0.5, 0.15625, ((0, 2),)),
        "narrow_bias": normal_values(key_of[15], (2, C), 0.3, 3.0, ((0, 2),)),
    }


masked_score = -1e+30
highest = lax.Precision.HIGHEST

@jax.custom_vjp
def low(v):
    return lax.optimization_barrier(v.astype(jnp.bfloat16)).astype(jnp.float32)

@jax.custom_vjp
def low_back(v):
    return v

def low_keep(v):
    return (low(v), None)

def low_pass(kept, grad):
    return (grad,)

def back_keep(v):
    return (v, None)

def back_low(kept, grad):
    return (low(grad),)
low.defvjp(low_keep, low_pass)
low_back.defvjp(back_keep, back_low)

def norm_rows(values, gain, offset):
    center = values - lax.optimization_barrier(jnp.mean(values, -1, keepdims=True))
    spread = lax.optimization_barrier(jnp.mean(center * center, -1, keepdims=True))
    return center * lax.rsqrt(spread + 1e-05) * gain + offset

def split_windows(tensor):
    row_count, col_count, features = tensor.shape
    tensor = tensor.reshape(row_count // 7, 7, col_count // 7, 7, features).transpose(0, 2, 1, 3, 4)
    return tensor.reshape(-1, 49, features)

def join_windows(tensor, row_count, col_count):
    features = tensor.shape[-1]
    tensor = tensor.reshape(row_count // 7, col_count // 7, 7, 7, features).transpose(0, 2, 1, 3, 4)
    return tensor.reshape(row_count, col_count, features)

def offset_index():
    places = jnp.arange(49, dtype=jnp.int32)
    downs = places // 7
    acrosses = places % 7
    return (downs[:, None] - downs[None, :] + 6) * 13 + (acrosses[:, None] - acrosses[None, :] + 6)

def region_codes(row_count, col_count):
    downs = jnp.arange(row_count, dtype=jnp.int32)
    acrosses = jnp.arange(col_count, dtype=jnp.int32)
    vertical = (downs >= row_count - 7).astype(jnp.int32) + (downs >= row_count - 3).astype(jnp.int32)
    horizontal = (acrosses >= col_count - 7).astype(jnp.int32) + (acrosses >= col_count - 3).astype(jnp.int32)
    return vertical[:, None] * 3 + horizontal[None, :]

def swin_block(tokens, params, shifted):
    first_gain, first_shift, triple_weight, query_bias, value_bias, bias_table, attend_weight, attend_bias, second_gain, second_shift, widen_weight, widen_bias, narrow_weight, narrow_bias = params
    row_count, col_count, features = tokens.shape
    head_count = bias_table.shape[1]
    head_depth = features // head_count
    roll_by = 3 * shifted
    rolled = jnp.roll(tokens, (-roll_by, -roll_by), (0, 1))
    normed = low(norm_rows(rolled, first_gain, first_shift))
    offsets = jnp.concatenate([query_bias, jnp.zeros_like(query_bias), value_bias])
    triple = jnp.dot(normed.reshape(-1, features), triple_weight, precision=highest) + offsets
    triple = low(low_back(triple))
    parts = split_windows(triple.reshape(row_count, col_count, 3 * features)).reshape(-1, 49, 3, head_count, head_depth)
    relative = bias_table[offset_index()].transpose(2, 0, 1)
    scores = jnp.einsum('nqhd,nkhd->nhqk', parts[:, :, 0], parts[:, :, 1], precision=highest) * head_depth ** (-0.5) + relative[None]
    if shifted:
        region_ids = jnp.roll(region_codes(row_count, col_count), (-roll_by, -roll_by), (0, 1))
        region_ids = split_windows(region_ids[:, :, None])[:, :, 0]
        alike = region_ids[:, :, None] == region_ids[:, None, :]
        scores = jnp.where(alike[:, None], scores, masked_score)
    scores = low_back(scores)
    weights = jax.nn.softmax(scores, axis=-1)
    mixed = jnp.einsum('nhqk,nkhd->nqhd', low(weights), parts[:, :, 2], precision=highest)
    mixed = low(low_back(mixed.reshape(-1, features)))
    branch = low_back(jnp.dot(mixed, attend_weight, precision=highest) + attend_bias)
    branch = join_windows(branch.reshape(-1, 49, features), row_count, col_count)
    middle = tokens + jnp.roll(branch, (roll_by, roll_by), (0, 1))
    second_normed = low(norm_rows(middle, second_gain, second_shift)).reshape(-1, features)
    widened = low_back(jnp.dot(second_normed, widen_weight, precision=highest) + widen_bias)
    activated = low(jax.nn.gelu(widened, approximate=False))
    narrowed = low_back(jnp.dot(activated, narrow_weight, precision=highest) + narrow_bias)
    return middle + narrowed.reshape(row_count, col_count, features)

def reference(image_tokens, out_grad, first_gain, first_shift, triple_weight, query_bias, value_bias, bias_table, attend_weight, attend_bias, second_gain, second_shift, widen_weight, widen_bias, narrow_weight, narrow_bias):
    params = tuple((item.astype(jnp.float32) for item in (first_gain, first_shift, triple_weight, query_bias, value_bias, bias_table, attend_weight, attend_bias, second_gain, second_shift, widen_weight, widen_bias, narrow_weight, narrow_bias)))
    inputs = image_tokens.astype(jnp.float32)
    probe = jnp.zeros_like(inputs)

    def forward(inputs, probe, params):
        first_set = tuple((item[0] for item in params))
        second_set = tuple((item[1] for item in params))

        def one_micro(pair):
            tokens, probe_part = pair
            hidden = low(jax.checkpoint(partial(swin_block, shifted=0))(tokens, first_set))
            entry = low_back(hidden) + probe_part
            final = low(jax.checkpoint(partial(swin_block, shifted=1))(entry, second_set))
            return (hidden, final)
        return lax.map(one_micro, (inputs, probe))
    (hidden, final), pullback = jax.vjp(forward, inputs, probe, params)
    input_grad, entry_grad, slopes = pullback((jnp.zeros_like(hidden), out_grad.astype(jnp.float32)))
    block_outputs = jnp.stack([hidden, final]).astype(jnp.bfloat16)
    input_grads = jnp.stack([input_grad, entry_grad]).astype(jnp.bfloat16)
    return (block_outputs, input_grads, slopes[0], slopes[1], slopes[2], slopes[3], slopes[4], slopes[5], slopes[6], slopes[7], slopes[8], slopes[9], slopes[10], slopes[11], slopes[12], slopes[13])
```

```python
from functools import partial

import jax
import jax.numpy as jnp
import numpy as np
from jax import lax
from jax.experimental import pallas as pl
from jax.experimental.pallas import tpu as pltpu
from jax.sharding import PartitionSpec as P

f32 = jnp.float32
bf16 = jnp.bfloat16
epsilon = 1e-05
masked_score = -1e30
chunk = 256
vmem_bytes = 60 * 1024 * 1024


def mm(left, right):
    return lax.dot_general(left, right, (((1,), (0,)), ((), ())), preferred_element_type=f32)


def mm_t(left, right):
    return lax.dot_general(left, right, (((1,), (1,)), ((), ())), preferred_element_type=f32)


def t_mm(left, right):
    return lax.dot_general(left, right, (((0,), (0,)), ((), ())), preferred_element_type=f32)


def normed_parts(values):
    center = values - jnp.mean(values, -1, keepdims=True)
    spread = jnp.mean(center * center, -1, keepdims=True)
    scale = lax.rsqrt(spread + epsilon)
    return center * scale, scale


def norm_back(grad, hat, scale, gain):
    pulled = grad * gain
    return scale * (
        pulled
        - jnp.mean(pulled, -1, keepdims=True)
        - hat * jnp.mean(pulled * hat, -1, keepdims=True)
    )


def gelu_parts(value):
    near = jnp.abs(value)
    t = 1.0 / (1.0 + (0.3275911 * 0.5**0.5) * near)
    series = t * (
        0.5 * 0.254829592
        + t
        * (
            0.5 * -0.284496736
            + t * (0.5 * 1.421413741 + t * (0.5 * -1.453152027 + t * (0.5 * 1.061405429)))
        )
    )
    bell = jnp.exp(-0.5 * value * value)
    tail = series * bell
    below = jnp.where(value >= 0, 1.0 - tail, tail)
    return value * below, below + value * bell * (2.0 * np.pi) ** -0.5


def row_sum(values):
    return jnp.sum(values, 0, keepdims=True)


def head_masks(depth):
    place = lax.broadcasted_iota(jnp.int32, (1, 128), 1) // depth
    return [(place == h) for h in range(128 // depth)]


def spread_heads(part, masks):
    return jnp.concatenate([part * m.astype(bf16) for m in masks], 0)


def collect_heads(tall, masks):
    rows = tall.shape[0] // len(masks)
    out = tall[:rows]
    for h in range(1, len(masks)):
        out = jnp.where(masks[h], tall[h * rows : (h + 1) * rows], out)
    return out


def pad_rows(values, rows):
    return jnp.concatenate(
        [values, jnp.zeros((rows - values.shape[0], values.shape[1]), values.dtype)], 0
    )


def image_to_windows(image_ref, spread, store):
    for u in range(7):
        cells = mm(spread, image_ref[u])
        store(u, cells.reshape(-1, 8, cells.shape[-1]))


def windows_to_image(windows_ref, spread, image_ref):
    wins = windows_ref.shape[0]
    feats = windows_ref.shape[-1]
    for u in range(7):
        cells = windows_ref[:, u * 8 : (u + 1) * 8, :].reshape(wins * 8, feats).astype(bf16)
        image_ref[u] = t_mm(spread, cells).astype(bf16)


def stage_front(x_ref, spread, gain, shift, triple, triple_bias, xs, n1, n1t, qkv):
    wins, cells, feats = xs.shape

    def put(u, part):
        xs[:, u * 8 : (u + 1) * 8, :] = part

    image_to_windows(x_ref, spread, put)

    def norm_step(i, carry):
        span = pl.ds(i * 4, 4)
        hat, _ = normed_parts(xs[span].reshape(4 * cells, feats))
        n1[pl.ds(pl.multiple_of(i * 4 * cells, 4 * cells), 4 * cells), :] = (
            hat * gain + shift
        ).astype(bf16)
        return carry

    lax.fori_loop(0, wins // 4, norm_step, 0)
    qkv[:, cells:, :] = jnp.zeros((wins, qkv.shape[1] - cells, qkv.shape[2]), bf16)
    for j in range(3):
        lanes = slice(j * feats, (j + 1) * feats)
        part = mm(n1[...], triple[:, lanes]) + triple_bias[:, lanes]
        qkv[:, :cells, lanes] = part.reshape(wins, cells, feats).astype(bf16)
    n1t[...] = n1[...].T


def stage_attend(qkv, bias, probs, mixed, depth):
    wins, tall, width = qkv.shape
    feats = width // 3
    cells = mixed.shape[1]
    masks = head_masks(depth)
    scale = depth**-0.5

    def step(w, carry):
        kind = jnp.maximum(w - (wins - 3), 0)
        for g in range(feats // 128):
            at = g * 128
            q = qkv[w, :, at : at + 128]
            k = qkv[w, :, feats + at : feats + at + 128]
            v = qkv[w, :, 2 * feats + at : 2 * feats + at + 128]
            scores = mm_t(k, spread_heads(q, masks))[:cells] * scale + bias[0, kind, g]
            powers = jnp.exp(scores - jnp.max(scores, 0, keepdims=True))
            weights = powers * (1.0 / jnp.sum(powers, 0, keepdims=True))
            low = pad_rows(weights, tall).astype(bf16)
            probs[w, g] = low
            mixed[w, :, at : at + 128] = collect_heads(t_mm(low, v), masks)[:cells]
        return carry

    lax.fori_loop(0, wins, step, 0)


def stage_feed(mixed, attend, attend_bias, gain, shift, widen, widen_bias, narrow, narrow_bias,
               xs, ot, x1, n2, n2t, act, slope, total):
    wins, cells, feats = xs.shape
    rows = wins * cells
    low = mixed[...].reshape(rows, feats).astype(bf16)
    ot[...] = low.T
    x1[...] = xs[...].reshape(rows, feats) + mm(low, attend[...]) + attend_bias

    def norm_step(i, carry):
        span = pl.ds(pl.multiple_of(i * 4 * cells, 4 * cells), 4 * cells)
        hat, _ = normed_parts(x1[span, :])
        n2[span, :] = (hat * gain + shift).astype(bf16)
        return carry

    lax.fori_loop(0, wins // 4, norm_step, 0)
    n2t[...] = n2[...].T
    total[...] = x1[...] + narrow_bias

    def hidden_step(j, carry):
        lanes = pl.ds(pl.multiple_of(j * chunk, chunk), chunk)
        h1 = mm(n2[...], widen[:, lanes]) + widen_bias[:, lanes]
        value, pull = gelu_parts(h1)
        low_act = value.astype(bf16)
        act[j] = low_act
        slope[j] = pull.astype(bf16)
        total[...] += mm(low_act, narrow[lanes, :])
        return carry

    lax.fori_loop(0, act.shape[0], hidden_step, 0)


def stage_feed_back(dy, dyt, x1, n2t, act, slope, gain, widen, narrow, dn2, gx1,
                    s_gain, s_shift, s_widen, s_widen_b, s_narrow_t, s_narrow_b):
    rows, feats = x1.shape
    part = rows // 4
    dyt[...] = dy[...].T
    s_narrow_b[...] += row_sum(dy[...].astype(f32))
    dn2[...] = jnp.zeros_like(dn2)

    def hidden_step(j, carry):
        lanes = pl.ds(pl.multiple_of(j * chunk, chunk), chunk)
        dh = mm_t(dy[...], narrow[lanes, :]) * slope[j].astype(f32)
        s_widen_b[:, lanes] += row_sum(dh)
        dh = dh.astype(bf16)
        s_widen[j] += mm(n2t[...], dh)
        s_narrow_t[j] += mm(dyt[...], act[j])
        dn2[...] += mm_t(dh, widen[:, lanes])
        return carry

    lax.fori_loop(0, act.shape[0], hidden_step, 0)

    def norm_step(i, carry):
        span = pl.ds(pl.multiple_of(i * part, part), part)
        hat, scale = normed_parts(x1[span, :])
        grad = dn2[span, :]
        s_gain[...] += row_sum(grad * hat)
        s_shift[...] += row_sum(grad)
        gx1[span, :] = dy[span, :].astype(f32) + norm_back(grad, hat, scale, gain)
        return carry

    lax.fori_loop(0, 4, norm_step, 0)


def stage_attend_back(gx1, qkv, probs, ot, attend, da, gmix, gqkv, s_attend, s_attend_b, s_pair,
                      depth):
    wins, tall, width = qkv.shape
    feats = width // 3
    cells = gqkv.shape[1]
    masks = head_masks(depth)
    da[...] = gx1[...].astype(bf16)
    s_attend_b[...] += row_sum(gx1[...])
    s_attend[...] += mm(ot[...], da[...])
    gmix[:, cells:, :] = jnp.zeros((wins, tall - cells, feats), bf16)
    gmix[:, :cells, :] = mm_t(da[...], attend[...]).reshape(wins, cells, feats).astype(bf16)
    scale = depth**-0.5

    def step(w, carry):
        for g in range(feats // 128):
            at = g * 128
            q = qkv[w, :, at : at + 128]
            k = qkv[w, :, feats + at : feats + at + 128]
            v = qkv[w, :, 2 * feats + at : 2 * feats + at + 128]
            wide = spread_heads(gmix[w, :, at : at + 128], masks)
            low = probs[w, g]
            pulled = mm_t(v, wide)[:cells] * low.astype(f32)[:cells]
            ds = pulled - low.astype(f32)[:cells] * jnp.sum(pulled, 0, keepdims=True)
            s_pair[g] += ds
            ds = pad_rows(ds, tall).astype(bf16)
            gqkv[w, :, 2 * feats + at : 2 * feats + at + 128] = mm(low, wide)[:cells]
            gqkv[w, :, feats + at : feats + at + 128] = (
                mm(ds, spread_heads(q, masks))[:cells] * scale
            )
            gqkv[w, :, at : at + 128] = collect_heads(t_mm(ds, k), masks)[:cells] * scale
        return carry

    lax.fori_loop(0, wins, step, 0)


def stage_front_back(gqkv, gx1, xs, n1t, gain, triple, dq, dn1, s_gain, s_shift, s_triple,
                     s_triple_b):
    wins, cells, feats = xs.shape
    rows = wins * cells
    for j in range(3):
        lanes = slice(j * feats, (j + 1) * feats)
        part = gqkv[:, :, lanes].reshape(rows, feats)
        s_triple_b[:, lanes] += row_sum(part)
        dq[:, lanes] = part.astype(bf16)
        s_triple[:, lanes] += mm(n1t[...], dq[:, lanes])
    dn1[...] = mm_t(dq[...], triple[...])

    def norm_step(i, carry):
        span = pl.ds(pl.multiple_of(i * 4 * cells, 4 * cells), 4 * cells)
        wide = pl.ds(i * 4, 4)
        hat, scale = normed_parts(xs[wide].reshape(4 * cells, feats))
        grad = dn1[span, :]
        s_gain[...] += row_sum(grad * hat)
        s_shift[...] += row_sum(grad)
        out = gx1[span, :] + norm_back(grad, hat, scale, gain)
        xs[wide] = out.reshape(4, cells, feats)
        return carry

    lax.fori_loop(0, wins // 4, norm_step, 0)


def read(ref):
    return ref[...].astype(f32)


names = (
    "first_gain first_shift triple_weight triple_bias attend_weight attend_bias "
    "second_gain second_shift widen_weight widen_bias narrow_weight narrow_bias"
).split()


class Weights:
    def __init__(self, refs):
        for name, ref in zip(names, refs):
            setattr(self, name, ref)


def forward_kernel(depth, x_ref, spread_ref, bias, *rest):
    w = Weights(rest[:12])
    y_ref, xs, n1t, qkv, probs, ot, x1, n2t, act, slope = (
        r if place == 0 else r.at[0] for place, r in enumerate(rest[12:22])
    )
    n1, mixed, n2, total = rest[22:]
    spread = spread_ref[...]
    stage_front(x_ref, spread, read(w.first_gain), read(w.first_shift), w.triple_weight,
                read(w.triple_bias), xs, n1, n1t, qkv)
    stage_attend(qkv, bias, probs, mixed, depth)
    stage_feed(mixed, w.attend_weight, read(w.attend_bias), read(w.second_gain),
               read(w.second_shift), w.widen_weight, w.widen_bias, w.narrow_weight,
               read(w.narrow_bias), xs, ot, x1, n2, n2t, act, slope, total)
    mixed[...] = total[...].reshape(mixed.shape)
    windows_to_image(mixed, spread, y_ref)


def clear_first(refs):
    @pl.when(pl.program_id(0) == 0)
    def _():
        for ref in refs:
            ref[...] = jnp.zeros_like(ref)


def narrow_out(t_ref, out_ref):
    for j in range(t_ref.shape[0]):
        out_ref[:, j * chunk : (j + 1) * chunk] = t_ref[j].astype(bf16)


def both_kernel(depth, x_ref, dy_ref, spread_ref, bias, *rest):
    w = Weights(rest[:12])
    (y_ref, dx_ref, o_triple, o_attend, o_widen, o_narrow_t,
     s_gain1, s_shift1, s_triple_b, s_attend_b, s_gain2, s_shift2, s_widen_b, s_narrow_b,
     s_pair) = rest[12:27]
    (xs, n1t, qkv, probs, ot, x1, n2t, act, slope, n1, mixed, n2, total, dy, dyt, gx1, gmix, gqkv,
     dq, s_triple, s_attend, s_widen, s_narrow_t) = rest[27:]
    spread = spread_ref[...]
    clear_first((s_gain1, s_shift1, s_triple_b, s_attend_b, s_gain2, s_shift2, s_widen_b,
                 s_narrow_b, s_pair, s_triple, s_attend, s_widen, s_narrow_t))
    stage_front(x_ref, spread, read(w.first_gain), read(w.first_shift), w.triple_weight,
                read(w.triple_bias), xs, n1, n1t, qkv)
    stage_attend(qkv, bias, probs, mixed, depth)
    stage_feed(mixed, w.attend_weight, read(w.attend_bias), read(w.second_gain),
               read(w.second_shift), w.widen_weight, w.widen_bias, w.narrow_weight,
               read(w.narrow_bias), xs, ot, x1, n2, n2t, act, slope, total)
    mixed[...] = total[...].reshape(mixed.shape)
    windows_to_image(mixed, spread, y_ref)

    def put(u, part):
        mixed[:, u * 8 : (u + 1) * 8, :] = part

    image_to_windows(dy_ref, spread, put)
    dy[...] = mixed[...].reshape(dy.shape).astype(bf16)
    stage_feed_back(dy, dyt, x1, n2t, act, slope, read(w.second_gain), w.widen_weight,
                    w.narrow_weight, total, gx1, s_gain2, s_shift2, s_widen, s_widen_b, s_narrow_t,
                    s_narrow_b)
    stage_attend_back(gx1, qkv, probs, ot, w.attend_weight, n2, gmix, gqkv, s_attend, s_attend_b,
                      s_pair, depth)
    stage_front_back(gqkv, gx1, xs, n1t, read(w.first_gain), w.triple_weight, dq, total, s_gain1,
                     s_shift1, s_triple, s_triple_b)
    windows_to_image(xs, spread, dx_ref)

    @pl.when(pl.program_id(0) == pl.num_programs(0) - 1)
    def _():
        o_triple[...] = s_triple[...].astype(bf16)
        o_attend[...] = s_attend[...].astype(bf16)
        narrow_out(s_widen, o_widen)
        narrow_out(s_narrow_t, o_narrow_t)


def feed_back_kernel(dy_ref, spread_ref, x1, n2t, act, slope, gain, widen, narrow,
                     gx1, o_widen, o_narrow_t, s_gain2, s_shift2, s_widen_b, s_narrow_b,
                     mixed, dy, dyt, dn2, s_widen, s_narrow_t):
    clear_first((s_gain2, s_shift2, s_widen_b, s_narrow_b, s_widen, s_narrow_t))

    def put(u, part):
        mixed[:, u * 8 : (u + 1) * 8, :] = part

    image_to_windows(dy_ref, spread_ref[...], put)
    dy[...] = mixed[...].reshape(dy.shape).astype(bf16)
    stage_feed_back(dy, dyt, x1.at[0], n2t.at[0], act.at[0], slope.at[0], read(gain), widen,
                    narrow, dn2, gx1.at[0], s_gain2, s_shift2, s_widen, s_widen_b, s_narrow_t,
                    s_narrow_b)

    @pl.when(pl.program_id(0) == pl.num_programs(0) - 1)
    def _():
        narrow_out(s_widen, o_widen)
        narrow_out(s_narrow_t, o_narrow_t)


def attend_back_kernel(depth, gx1, spread_ref, xs, n1t, qkv, probs, ot, gain, triple, attend,
                       dx_ref, o_triple, o_attend, s_gain1, s_shift1, s_triple_b, s_attend_b,
                       s_pair, da, gmix, gqkv, dq, dn1, xw, s_triple, s_attend):
    clear_first((s_gain1, s_shift1, s_triple_b, s_attend_b, s_pair, s_triple, s_attend))
    stage_attend_back(gx1.at[0], qkv.at[0], probs.at[0], ot.at[0], attend, da, gmix, gqkv,
                      s_attend, s_attend_b, s_pair, depth)
    xw[...] = xs[0]
    stage_front_back(gqkv, gx1.at[0], xw, n1t.at[0], read(gain), triple, dq, dn1, s_gain1,
                     s_shift1, s_triple, s_triple_b)
    windows_to_image(xw, spread_ref[...], dx_ref)

    @pl.when(pl.program_id(0) == pl.num_programs(0) - 1)
    def _():
        o_triple[...] = s_triple[...].astype(bf16)
        o_attend[...] = s_attend[...].astype(bf16)


class Sizes:
    def __init__(self, own_rows, cols, feats, hidden, heads):
        self.steps = own_rows // 7
        self.cols = cols
        self.feats = feats
        self.hidden = hidden
        self.wins = cols // 7
        self.rows = self.wins * 56
        self.depth = feats // heads
        self.groups = feats // 128
        self.lanes = 128 // self.depth * 64
        self.parts = hidden // chunk


def whole(shape):
    return pl.BlockSpec(shape, lambda i: (0,) * len(shape), pipeline_mode=pl.Buffered(1))


def per_step(shape):
    return pl.BlockSpec((1,) + shape, lambda i: (i,) + (0,) * len(shape))


def summed(shape):
    return pl.BlockSpec(shape, lambda i: (0,) * len(shape))


def image_spec(z):
    return pl.BlockSpec((7, z.cols, z.feats), lambda i: (i, 0, 0))


def saved_shapes(z):
    return {
        "xs": ((z.wins, 56, z.feats), f32),
        "n1t": ((z.feats, z.rows), bf16),
        "qkv": ((z.wins, 64, 3 * z.feats), bf16),
        "probs": ((z.wins, z.groups, 64, z.lanes), bf16),
        "ot": ((z.feats, z.rows), bf16),
        "x1": ((z.rows, z.feats), f32),
        "n2t": ((z.feats, z.rows), bf16),
        "act": ((z.parts, z.rows, chunk), bf16),
        "slope": ((z.parts, z.rows, chunk), bf16),
    }


def weight_specs(weights):
    return [whole(item.shape) for item in weights]


def cost(z, passes):
    return pl.CostEstimate(
        flops=int(passes * 2 * z.steps * z.rows * z.feats * (4 * z.feats + 2 * z.hidden)),
        bytes_accessed=40_000_000,
        transcendentals=0,
    )


def params():
    return pltpu.CompilerParams(
        dimension_semantics=("arbitrary",), vmem_limit_bytes=vmem_bytes
    )


def bias_spec(bias):
    return pl.BlockSpec((1,) + bias.shape[1:], lambda i: (i, 0, 0, 0, 0))


def run_forward(z, image, spread, bias, weights):
    saved = saved_shapes(z)
    scratch = [
        pltpu.VMEM((z.rows, z.feats), bf16),
        pltpu.VMEM((z.wins, 56, z.feats), f32),
        pltpu.VMEM((z.rows, z.feats), bf16),
        pltpu.VMEM((z.rows, z.feats), f32),
    ]
    return pl.pallas_call(
        partial(forward_kernel, z.depth),
        grid=(z.steps,),
        in_specs=[image_spec(z), whole(spread.shape), bias_spec(bias)] + weight_specs(weights),
        out_specs=[image_spec(z)] + [per_step(shape) for shape, _ in saved.values()],
        out_shape=[jax.ShapeDtypeStruct(image.shape, bf16)]
        + [jax.ShapeDtypeStruct((z.steps,) + shape, kind) for shape, kind in saved.values()],
        scratch_shapes=scratch,
        compiler_params=params(),
        cost_estimate=cost(z, 1),
    )(image, spread, bias, *weights)


def run_both(z, image, grad, spread, bias, weights):
    saved = saved_shapes(z)
    sums = [
        (1, z.feats), (1, z.feats), (1, 3 * z.feats), (1, z.feats), (1, z.feats), (1, z.feats),
        (1, z.hidden), (1, z.feats), (z.groups, 56, z.lanes),
    ]
    mats = [(z.feats, 3 * z.feats), (z.feats, z.feats), (z.feats, z.hidden), (z.feats, z.hidden)]
    scratch = [pltpu.VMEM(shape, kind) for shape, kind in saved.values()] + [
        pltpu.VMEM((z.rows, z.feats), bf16),
        pltpu.VMEM((z.wins, 56, z.feats), f32),
        pltpu.VMEM((z.rows, z.feats), bf16),
        pltpu.VMEM((z.rows, z.feats), f32),
        pltpu.VMEM((z.rows, z.feats), bf16),
        pltpu.VMEM((z.feats, z.rows), bf16),
        pltpu.VMEM((z.rows, z.feats), f32),
        pltpu.VMEM((z.wins, 64, z.feats), bf16),
        pltpu.VMEM((z.wins, 56, 3 * z.feats), f32),
        pltpu.VMEM((z.rows, 3 * z.feats), bf16),
        pltpu.VMEM((z.feats, 3 * z.feats), f32),
        pltpu.VMEM((z.feats, z.feats), f32),
        pltpu.VMEM((z.parts, z.feats, chunk), f32),
        pltpu.VMEM((z.parts, z.feats, chunk), f32),
    ]
    return pl.pallas_call(
        partial(both_kernel, z.depth),
        grid=(z.steps,),
        in_specs=[image_spec(z), image_spec(z), whole(spread.shape), bias_spec(bias)]
        + weight_specs(weights),
        out_specs=[image_spec(z), image_spec(z)] + [whole(s) for s in mats + sums],
        out_shape=[jax.ShapeDtypeStruct(image.shape, bf16)] * 2
        + [jax.ShapeDtypeStruct(s, bf16) for s in mats]
        + [jax.ShapeDtypeStruct(s, f32) for s in sums],
        scratch_shapes=scratch,
        compiler_params=params(),
        cost_estimate=cost(z, 3),
    )(image, grad, spread, bias, *weights)


def run_feed_back(z, grad, spread, kept, gain, widen, narrow):
    saved = saved_shapes(z)
    wanted = ("x1", "n2t", "act", "slope")
    mats = [(z.feats, z.hidden), (z.feats, z.hidden)]
    sums = [(1, z.feats), (1, z.feats), (1, z.hidden), (1, z.feats)]
    return pl.pallas_call(
        feed_back_kernel,
        grid=(z.steps,),
        in_specs=[image_spec(z), whole(spread.shape)]
        + [per_step(saved[name][0]) for name in wanted]
        + weight_specs((gain, widen, narrow)),
        out_specs=[per_step((z.rows, z.feats))] + [whole(s) for s in mats + sums],
        out_shape=[jax.ShapeDtypeStruct((z.steps, z.rows, z.feats), f32)]
        + [jax.ShapeDtypeStruct(s, bf16) for s in mats]
        + [jax.ShapeDtypeStruct(s, f32) for s in sums],
        scratch_shapes=[
            pltpu.VMEM((z.wins, 56, z.feats), f32),
            pltpu.VMEM((z.rows, z.feats), bf16),
            pltpu.VMEM((z.feats, z.rows), bf16),
            pltpu.VMEM((z.rows, z.feats), f32),
            pltpu.VMEM((z.parts, z.feats, chunk), f32),
            pltpu.VMEM((z.parts, z.feats, chunk), f32),
        ],
        compiler_params=params(),
        cost_estimate=cost(z, 1.3),
    )(grad, spread, *(kept[name] for name in wanted), gain, widen, narrow)


def run_attend_back(z, gx1, spread, kept, gain, triple, attend):
    saved = saved_shapes(z)
    wanted = ("xs", "n1t", "qkv", "probs", "ot")
    mats = [(z.feats, 3 * z.feats), (z.feats, z.feats)]
    sums = [(1, z.feats), (1, z.feats), (1, 3 * z.feats), (1, z.feats), (z.groups, 56, z.lanes)]
    image = (z.steps * 7, z.cols, z.feats)
    return pl.pallas_call(
        partial(attend_back_kernel, z.depth),
        grid=(z.steps,),
        in_specs=[per_step((z.rows, z.feats)), whole(spread.shape)]
        + [per_step(saved[name][0]) for name in wanted]
        + weight_specs((gain, triple, attend)),
        out_specs=[image_spec(z)] + [whole(s) for s in mats + sums],
        out_shape=[jax.ShapeDtypeStruct(image, bf16)]
        + [jax.ShapeDtypeStruct(s, bf16) for s in mats]
        + [jax.ShapeDtypeStruct(s, f32) for s in sums],
        scratch_shapes=[
            pltpu.VMEM((z.rows, z.feats), bf16),
            pltpu.VMEM((z.wins, 64, z.feats), bf16),
            pltpu.VMEM((z.wins, 56, 3 * z.feats), f32),
            pltpu.VMEM((z.rows, 3 * z.feats), bf16),
            pltpu.VMEM((z.rows, z.feats), f32),
            pltpu.VMEM((z.wins, 56, z.feats), f32),
            pltpu.VMEM((z.feats, 3 * z.feats), f32),
            pltpu.VMEM((z.feats, z.feats), f32),
        ],
        compiler_params=params(),
        cost_estimate=cost(z, 1.3),
    )(gx1, spread, *(kept[name] for name in wanted), gain, triple, attend)


def spread_matrix(cols, roll_by):
    place = np.arange(cols // 7 * 8)
    target = (place // 8 * 7 + place % 8 + roll_by) % cols
    hit = (target[:, None] == np.arange(cols)[None, :]) & (place % 8 < 7)[:, None]
    return jnp.asarray(hit, bf16)


def pair_index():
    place = np.arange(64)
    u, w = place // 8, place % 8
    real = (u < 7) & (w < 7)
    index = (u[None, :] - u[:, None] + 6) * 13 + (w[None, :] - w[:, None] + 6)
    return np.where(real[:, None] & real[None, :], index, 169)


def score_bias(table, z, shifted, first_row, total_rows):
    heads = table.shape[1]
    index = pair_index()[:56]
    onehot = jnp.asarray(index.reshape(-1)[:, None] == np.arange(169)[None, :], bf16)
    base = lax.dot_general(
        onehot, table, (((1,), (0,)), ((), ())), preferred_element_type=f32
    ).reshape(56, 64, z.groups, heads // z.groups)
    base = base.transpose(2, 0, 3, 1)
    place = np.arange(64)
    key_real = ((place % 8 < 7) & (place < 56))[:56]
    base = jnp.where(key_real[None, :, None, None], base, masked_score)
    if not shifted:
        base = base.reshape(z.groups, 56, z.lanes)
        return jnp.broadcast_to(base[None, None], (z.steps, 3) + base.shape)
    u, w = place // 8, place % 8
    steps = []
    for step in range(z.steps):
        rows = jnp.mod(first_row + step * 7 + jnp.minimum(u, 6) + 3, total_rows)
        vertical = (rows >= total_rows - 7).astype(jnp.int32) + (rows >= total_rows - 3)
        kinds = []
        for column in (0, z.wins - 2, z.wins - 1):
            cols = np.mod(column * 7 + np.minimum(w, 6) + 3, z.cols)
            horizontal = (cols >= z.cols - 7).astype(np.int32) + (cols >= z.cols - 3)
            code = vertical * 3 + horizontal
            alike = code[:56, None] == code[None, :]
            kinds.append(jnp.where(alike[None, :, None, :], base, masked_score))
        steps.append(jnp.stack(kinds))
    return jnp.stack(steps).reshape(z.steps, 3, z.groups, 56, z.lanes)


def table_slope(pair, z, heads):
    index = pair_index()[:56]
    onehot = jnp.asarray(index.reshape(-1)[:, None] == np.arange(169)[None, :], bf16)
    pair = pair.reshape(z.groups, 56, heads // z.groups, 64).transpose(1, 3, 0, 2)
    pair = pair.reshape(56 * 64, heads)
    high = pair.astype(bf16)
    rest = (pair - high.astype(f32)).astype(bf16)
    both = t_mm(onehot, jnp.concatenate([high, rest], 1))
    return both[:, :heads] + both[:, heads:]


def swap_cores(item):
    return lax.ppermute(item, "pipe", [(0, 1), (1, 0)])


def take(pair, index):
    return lax.dynamic_index_in_dim(pair, index, 0, keepdims=False)


def sum_rows_axis(item):
    count = lax.axis_size("rows")
    me = lax.axis_index("rows")
    total = item.shape[0]
    order = []
    bit = 1
    while bit < count:
        order.append(bit)
        bit *= 2
    if bit != count:
        return lax.psum(item, "rows")
    for bit in order:
        route = [(i, i ^ bit) for i in range(count)]
        mine = (me // bit) % 2
        halves = item.reshape(2, -1, 128)
        arrived = lax.ppermute(take(halves, 1 - mine), "rows", route)
        item = (take(halves, mine).astype(f32) + arrived.astype(f32)).astype(bf16)
    for bit in order[::-1]:
        route = [(i, i ^ bit) for i in range(count)]
        mine = (me // bit) % 2
        arrived = lax.ppermute(item, "rows", route)
        item = jnp.where(
            mine == 0, jnp.concatenate([item, arrived]), jnp.concatenate([arrived, item])
        )
    return item.reshape(total, 128)


def reduce_block(mats, sums, owner):
    core = lax.axis_index("pipe")
    unit = 2 * 16 * 128 * lax.axis_size("rows")
    parts = [m.reshape(-1) for m in mats] + [s.astype(bf16).reshape(-1) for s in sums]
    flat = jnp.concatenate(parts)
    short = -flat.shape[0] % unit
    flat = jnp.concatenate([flat, jnp.zeros((short,), bf16)]).reshape(2, -1, 128)
    arrived = swap_cores(take(flat, 1 - core))
    half = (take(flat, core).astype(f32) + arrived.astype(f32)).astype(bf16)
    half = sum_rows_axis(half)
    other = swap_cores(half)
    done = jnp.where(core == 0, jnp.concatenate([half, other]), jnp.concatenate([other, half]))
    done = done.reshape(-1)
    out = []
    at = 0
    for item in list(mats) + list(sums):
        size = int(np.prod(item.shape))
        out.append(done[at : at + size].reshape(item.shape).astype(f32))
        at += size
    return out


def on_device(
    image_tokens,
    out_grad,
    first_gain,
    first_shift,
    triple_weight,
    query_bias,
    value_bias,
    bias_table,
    attend_weight,
    attend_bias,
    second_gain,
    second_shift,
    widen_weight,
    widen_bias,
    narrow_weight,
    narrow_bias,
):
    core = lax.axis_index("pipe")
    count = lax.axis_size("rows")
    place = lax.axis_index("rows")
    batches, own_rows, cols, feats = image_tokens.shape
    heads = bias_table.shape[2]
    hidden = widen_weight.shape[2]
    z = Sizes(own_rows, cols, feats, hidden, heads)
    total_rows = own_rows * count
    first_row = place * own_rows

    small = (first_gain, first_shift, query_bias, value_bias, bias_table, attend_bias,
             second_gain, second_shift, widen_bias, narrow_bias)
    big = (triple_weight, attend_weight, widen_weight, narrow_weight)
    flat = jnp.concatenate([item.reshape(-1) for item in small])
    flat_other = swap_cores(flat)
    big_other = [swap_cores(item) for item in big]
    blocks = []
    for b in range(2):
        mine = core == b
        chosen = jnp.where(mine, flat, flat_other)
        values = []
        at = 0
        for item in small:
            size = int(np.prod(item.shape))
            values.append(chosen[at : at + size].reshape(item.shape[1:]))
            at += size
        gain1, shift1, qb, vb, table, ab, gain2, shift2, wb, nb = values
        tw, aw, ww, nw = (jnp.where(mine, own, other)[0] for own, other in zip(big, big_other))
        tb = jnp.concatenate([qb, jnp.zeros_like(qb), vb])
        weights = [gain1[None], shift1[None], tw, tb[None], aw, ab[None], gain2[None],
                   shift2[None], ww, wb[None].astype(f32), nw, nb[None]]
        blocks.append((weights, table))

    image = take(image_tokens, core)
    grad = take(out_grad, core)
    to_previous = [((i + 1) % count, i) for i in range(count)]
    to_next = [(i, (i + 1) % count) for i in range(count)]

    def rolled_rows(item):
        return jnp.concatenate([item[3:], lax.ppermute(item[:3], "rows", to_previous)], 0)

    def unrolled_rows(item):
        return jnp.concatenate([lax.ppermute(item[-3:], "rows", to_next), item[:-3]], 0)

    spread0 = spread_matrix(cols, 0)
    spread1 = spread_matrix(cols, 3)
    weights0, table0 = blocks[0]
    weights1, table1 = blocks[1]
    bias0 = score_bias(table0, z, False, first_row, total_rows)
    bias1 = score_bias(table1, z, True, first_row, total_rows)
    grad_rolled = rolled_rows(grad)

    outcome = run_forward(z, image, spread0, bias0, weights0)
    hidden_out = outcome[0]
    kept = dict(zip(saved_shapes(z), outcome[1:]))
    entry = rolled_rows(hidden_out)
    outcome = run_both(z, entry, grad_rolled, spread1, bias1, weights1)
    final_rolled, entry_rolled = outcome[:2]
    mats1, sums1 = outcome[2:6], outcome[6:]
    final = unrolled_rows(final_rolled)
    entry_grad = unrolled_rows(entry_rolled)
    outcome = run_feed_back(z, entry_grad, spread0, kept, weights0[6], weights0[8], weights0[10])
    gx1 = outcome[0]
    feed_mats, feed_sums = outcome[1:3], outcome[3:]
    outcome = run_attend_back(z, gx1, spread0, kept, weights0[0], weights0[2], weights0[4])
    image_grad = outcome[0]
    attend_mats, attend_sums = outcome[1:3], outcome[3:]

    def arranged(mats, sums):
        return list(mats), list(sums[:-1]) + [table_slope(sums[-1], z, heads)]

    mats0 = list(attend_mats) + list(feed_mats)
    sums0 = list(attend_sums[:4]) + list(feed_sums) + [attend_sums[4]]
    totals0 = reduce_block(*arranged(mats0, sums0), 0)
    totals1 = reduce_block(*arranged(mats1, sums1), 1)
    totals = [jnp.where(core == 0, a, b) for a, b in zip(totals0, totals1)]
    (t_triple, t_attend, t_widen, t_narrow_t, t_gain1, t_shift1, t_triple_b, t_attend_b, t_gain2,
     t_shift2, t_widen_b, t_narrow_b, t_table) = totals

    def stacked(block0, block1):
        mine = jnp.where(core == 0, block0, block1)
        other = swap_cores(jnp.where(core == 0, block1, block0))
        return jnp.where(core == 0, jnp.stack([mine, other]), jnp.stack([other, mine]))[None]

    return (
        stacked(hidden_out, final),
        stacked(image_grad, entry_grad),
        t_gain1,
        t_shift1,
        t_triple[None],
        t_triple_b[:, :feats],
        t_triple_b[:, 2 * feats :],
        t_table[None],
        t_attend[None],
        t_attend_b,
        t_gain2,
        t_shift2,
        t_widen[None],
        t_widen_b,
        t_narrow_t.T[None],
        t_narrow_b,
    )


def solution(mesh):
    param_specs = [
        P("pipe", None),
        P("pipe", None),
        P("pipe", None, None),
        P("pipe", None),
        P("pipe", None),
        P("pipe", None, None),
        P("pipe", None, None),
        P("pipe", None),
        P("pipe", None),
        P("pipe", None),
        P("pipe", None, None),
        P("pipe", None),
        P("pipe", None, None),
        P("pipe", None),
    ]
    in_specs = (P(None, "rows", None, None),) * 2 + tuple(param_specs)
    out_specs = (P("pipe", None, "rows", None, None),) * 2 + tuple(param_specs)
    return jax.shard_map(
        on_device, mesh=mesh, in_specs=in_specs, out_specs=out_specs, check_vma=False
    )
```

```python
from functools import partial

import jax
import jax.numpy as jnp
import numpy as np
from jax import lax
from jax.experimental import pallas as pl
from jax.experimental.pallas import tpu as pltpu
from jax.sharding import PartitionSpec as P

f32 = jnp.float32
bf16 = jnp.bfloat16
epsilon = 1e-05
masked_score = -1e30
vmem_bytes = 60 * 1024 * 1024
cells = 56
tall = 64

gain1_row, shift1_row, query_bias_row, value_bias_row = 0, 1, 2, 4
attend_bias_row, gain2_row, shift2_row, narrow_bias_row, widen_bias_row = 5, 6, 7, 8, 9
s_gain1, s_shift1, s_attend_b, s_gain2, s_shift2, s_narrow_b, s_widen_b = 3, 4, 5, 6, 7, 8, 9
small_rows = 16


def mm(left, right):
    return lax.dot_general(left, right, (((1,), (0,)), ((), ())), preferred_element_type=f32)


def mm_t(left, right):
    return lax.dot_general(left, right, (((1,), (1,)), ((), ())), preferred_element_type=f32)


def t_mm(left, right):
    return lax.dot_general(left, right, (((0,), (0,)), ((), ())), preferred_element_type=f32)


def normed_parts(values):
    center = values - jnp.mean(values, -1, keepdims=True)
    spread = jnp.mean(center * center, -1, keepdims=True)
    scale = lax.rsqrt(spread + epsilon)
    return center * scale, scale


def norm_back(grad, hat, scale, gain):
    pulled = grad * gain
    return scale * (
        pulled
        - jnp.mean(pulled, -1, keepdims=True)
        - hat * jnp.mean(pulled * hat, -1, keepdims=True)
    )


def gelu_parts(value):
    below = 0.5 + 0.5 * lax.erf(value * 0.5**0.5)
    bell = jnp.exp(value * value * -0.5)
    return value * below, below + value * bell * (2.0 * np.pi) ** -0.5


def row_sum(values):
    return jnp.sum(values, 0, keepdims=True)


def head_masks(depth):
    place = lax.broadcasted_iota(jnp.int32, (1, 128), 1) // depth
    return [(place == h) for h in range(128 // depth)]


def spread_heads(part, masks):
    return jnp.concatenate([part * m.astype(bf16) for m in masks], 0)


def collect_heads(high, masks):
    rows = high.shape[0] // len(masks)
    out = high[:rows]
    for h in range(1, len(masks)):
        out = jnp.where(masks[h], high[h * rows : (h + 1) * rows], out)
    return out


def pad_rows(values, rows):
    return jnp.concatenate(
        [values, jnp.zeros((rows - values.shape[0], values.shape[1]), values.dtype)], 0
    )


def spread_matrix(cols, roll_by):
    place = lax.broadcasted_iota(jnp.int32, (cols // 7 * 8, cols), 0)
    column = lax.broadcasted_iota(jnp.int32, (cols // 7 * 8, cols), 1)
    w = place & 7
    target = (place >> 3) * 7 + w + roll_by
    target = jnp.where(target >= cols, target - cols, target)
    return jnp.where((target == column) & (w < 7), 1.0, 0.0).astype(bf16)


def image_to_windows(rows, spread, out):
    for u, row in enumerate(rows):
        part = mm(spread, row())
        out[:, u * 8 : (u + 1) * 8, :] = part.reshape(-1, 8, part.shape[-1])


def windows_to_image(windows, spread, image_ref):
    wins, _, feats = windows.shape
    for u in range(7):
        part = windows[:, u * 8 : (u + 1) * 8, :].reshape(wins * 8, feats).astype(bf16)
        image_ref[u] = t_mm(spread, part).astype(bf16)


def row_reader(ref, *index):
    return lambda: ref[index]


def by_rows(rows, parts, step):
    size = rows // parts

    def body(i, carry):
        step(i, pl.ds(pl.multiple_of(i * size, size), size))
        return carry

    lax.fori_loop(0, parts, body, 0)


class Loader:
    def __init__(self, core_ref, block, sems):
        self.mine = core_ref[0] == block
        self.sems = sems
        self.count = 0

    def start(self, own, other, target):
        sem = self.sems.at[self.count]
        self.count += 1

        @pl.when(self.mine)
        def _():
            pltpu.make_async_copy(own.at[0], target, sem).start()

        @pl.when(jnp.logical_not(self.mine))
        def _():
            pltpu.make_async_copy(other.at[0], target, sem).start()

        return pltpu.make_async_copy(own.at[0], target, sem)

    def small(self, own, other):
        return jnp.where(self.mine, own[...], other[...])


class Writer:
    def __init__(self, sems):
        self.sems = sems
        self.copies = []

    def start(self, source, target):
        copy = pltpu.make_async_copy(source, target, self.sems.at[len(self.copies)])
        copy.start()
        self.copies.append(copy)

    def finish(self):
        for copy in self.copies:
            copy.wait()


def stage_norm(xs, gain, shift, n1):
    wins, _, feats = xs.shape

    def step(i, span):
        hat, _ = normed_parts(xs[pl.ds(i * 4, 4)].reshape(4 * cells, feats))
        n1[span, :] = (hat * gain + shift).astype(bf16)

    by_rows(wins * cells, wins // 4, step)


def stage_triple(n1, triple, small, qkv):
    wins, _, width = qkv.shape
    feats = width // 3
    qkv[:, cells:, :] = jnp.zeros((wins, tall - cells, width), bf16)
    offsets = (query_bias_row, None, value_bias_row)
    for j in range(3):
        lanes = slice(j * feats, (j + 1) * feats)
        part = mm(n1[...], triple[:, lanes])
        if offsets[j] is not None:
            part = part + small[offsets[j] : offsets[j] + 1]
        qkv[:, :cells, lanes] = part.reshape(wins, cells, feats).astype(bf16)


def stage_attend(qkv, bias, probs, mixed, depth):
    wins, _, width = qkv.shape
    feats = width // 3
    masks = head_masks(depth)
    scale = depth**-0.5

    def step(w, carry):
        kind = jnp.maximum(w - (wins - 3), 0) if bias.shape[0] > 1 else 0
        for g in range(feats // 128):
            at = g * 128
            q = qkv[w, :, at : at + 128]
            k = qkv[w, :, feats + at : feats + at + 128]
            v = qkv[w, :, 2 * feats + at : 2 * feats + at + 128]
            scores = mm_t(k, spread_heads(q, masks))[:cells] * scale + bias[kind, g]
            powers = jnp.exp(scores - jnp.max(scores, 0, keepdims=True))
            weights = powers * (1.0 / jnp.sum(powers, 0, keepdims=True))
            low = pad_rows(weights, tall).astype(bf16)
            probs[w, g] = low
            mixed[w, :, at : at + 128] = collect_heads(t_mm(low, v), masks)[:cells]
        return carry

    lax.fori_loop(0, wins, step, 0, unroll=4)


def front_kernel(z, block, with_back, x_plan, dy_plan, n_x, n_dy, core_ref, *refs):
    refs = list(refs)
    x_refs = [refs.pop(0) for _ in range(n_x)]
    dy_refs = [refs.pop(0) for _ in range(n_dy)]
    small_own, small_other, base_ref = (refs.pop(0) for _ in range(3))
    mask = refs.pop(0) if block == 1 else None
    big = [(refs.pop(0), refs.pop(0)) for _ in range(4)]
    prev = refs.pop(0) if with_back == 2 else None
    prev_small = refs.pop(0) if with_back == 2 else None
    y_ref, o_qkv, o_probs, o_mix = (refs.pop(0) for _ in range(4))
    if with_back:
        o_gx1, o_mats, o_small = (refs.pop(0) for _ in range(3))
    else:
        o_x1, o_act, o_slope = (refs.pop(0) for _ in range(3))
    (triple, attend, widen, narrow, xs, n1, qkv, bias, probs, mixed, low_mix, x1, n2, act, slope,
     total, load_sems, write_sems) = refs[:18]
    rows, feats = x1.shape
    load = Loader(core_ref, block, load_sems)
    waits = [
        load.start(own, other, target)
        for (own, other), target in zip(big, (triple, attend, widen, narrow))
    ]
    write = Writer(write_sems)
    small = load.small(small_own, small_other)
    spread = spread_matrix(z.cols, 3 * block)
    base = base_ref[...].astype(f32)
    if block == 1:
        for kind in range(3):
            for g in range(z.groups):
                bias[kind, g] = base[g] + mask[kind]
    else:
        bias[0] = base
    image_to_windows([row_reader(x_refs[a], *at) for a, at in x_plan], spread, xs)
    stage_norm(xs, small[gain1_row : gain1_row + 1], small[shift1_row : shift1_row + 1], n1)
    waits[0].wait()
    stage_triple(n1, triple, small, qkv)
    write.start(qkv, o_qkv)
    stage_attend(qkv, bias, probs, mixed, z.depth)
    write.start(probs, o_probs)
    low_mix[...] = mixed[...].reshape(rows, feats).astype(bf16)
    write.start(low_mix, o_mix)
    waits[1].wait()
    x1[...] = (
        xs[...].reshape(rows, feats)
        + mm(low_mix[...], attend[...])
        + small[attend_bias_row : attend_bias_row + 1]
    )
    if not with_back:
        write.start(x1, o_x1)
    gain2 = small[gain2_row : gain2_row + 1]
    shift2 = small[shift2_row : shift2_row + 1]

    def norm_step(i, span):
        hat, _ = normed_parts(x1[span, :])
        n2[span, :] = (hat * gain2 + shift2).astype(bf16)

    by_rows(rows, 4, norm_step)
    waits[2].wait()
    part = z.hidden // z.parts
    for j in range(z.parts):
        lanes = slice(j * part, (j + 1) * part)
        offset = jnp.concatenate(
            [
                small[widen_bias_row + i : widen_bias_row + i + 1]
                for i in range(j * part // feats, (j + 1) * part // feats)
            ],
            1,
        )
        value, pull = gelu_parts(mm(n2[...], widen[:, lanes]) + offset)
        act[:, lanes] = value.astype(bf16)
        slope[:, lanes] = pull.astype(bf16)
    if not with_back:
        write.start(act, o_act)
        write.start(slope, o_slope)
    waits[3].wait()
    total[...] = (
        x1[...] + mm(act[...], narrow[...]) + small[narrow_bias_row : narrow_bias_row + 1]
    ).reshape(total.shape)
    windows_to_image(total, spread, y_ref)
    if with_back:
        dy, dh, dn2, gx1 = refs[18:22]
        feed_back(z, dy_refs, dy_plan, spread, total, x1, n2, act, slope, widen, narrow, gain2,
                  dy, dh, dn2, gx1, prev, prev_small, o_mats, o_small)
        write.start(gx1, o_gx1)
    write.finish()


def feed_back(z, dy_refs, dy_plan, spread, wide, x1, n2, act, slope, widen, narrow, gain2,
              dy, dh, dn2, gx1, prev, prev_small, o_mats, o_small):
    rows, feats = x1.shape
    image_to_windows([row_reader(dy_refs[a], *at) for a, at in dy_plan], spread, wide)
    dy[...] = wide[...].reshape(rows, feats).astype(bf16)
    zero = jnp.zeros((1, feats), f32)
    sums = {s_narrow_b: row_sum(wide[...].reshape(rows, feats))}
    part = z.hidden // z.parts

    def put(at, size, lanes, value):
        if prev is not None:
            value = value + prev[at : at + size, lanes].astype(f32)
        o_mats[at : at + size, lanes] = value.astype(bf16)

    for j in range(z.parts):
        lanes = slice(j * part, (j + 1) * part)
        grad = mm_t(dy[...], narrow[lanes, :]) * slope[:, lanes].astype(f32)
        total = row_sum(grad)
        for i in range(part // feats):
            sums[s_widen_b + j * part // feats + i] = total[:, i * feats : (i + 1) * feats]
        dh[:, lanes] = grad.astype(bf16)
    dn2[...] = mm_t(dh[...], widen[...])
    for j in range(z.hidden // feats):
        lanes = slice(j * feats, (j + 1) * feats)
        put(j * feats, feats, slice(None), t_mm(n2[...], dh[:, lanes]))
    for j in range(z.hidden // feats):
        lanes = slice(j * feats, (j + 1) * feats)
        put(z.hidden + j * feats, feats, slice(None), t_mm(act[:, lanes], dy[...]))
    o_small[...] = jnp.zeros_like(o_small) if prev_small is None else prev_small[...]
    for at, value in sums.items():
        o_small[at : at + 1] += value

    def norm_step(i, span):
        hat, scale = normed_parts(x1[span, :])
        grad = dn2[span, :]
        o_small[s_gain2 : s_gain2 + 1] += row_sum(grad * hat)
        o_small[s_shift2 : s_shift2 + 1] += row_sum(grad)
        gx1[span, :] = dy[span, :].astype(f32) + norm_back(grad, hat, scale, gain2)

    by_rows(rows, 4, norm_step)


def feed_back_kernel(z, block, dy_plan, n_dy, chained, core_ref, *refs):
    refs = list(refs)
    dy_refs = [refs.pop(0) for _ in range(n_dy)]
    small_own, small_other = refs.pop(0), refs.pop(0)
    big = [(refs.pop(0), refs.pop(0)) for _ in range(2)]
    x1, act, slope = (refs.pop(0) for _ in range(3))
    prev = refs.pop(0) if chained else None
    prev_small = refs.pop(0) if chained else None
    o_gx1, o_mats, o_small = (refs.pop(0) for _ in range(3))
    widen, narrow, wide, n2, dy, dh, dn2, load_sems = refs
    load = Loader(core_ref, block, load_sems)
    waits = [load.start(own, other, to) for (own, other), to in zip(big, (widen, narrow))]
    small = load.small(small_own, small_other)
    gain2 = small[gain2_row : gain2_row + 1]
    shift2 = small[shift2_row : shift2_row + 1]
    rows, feats = x1.shape

    def norm_step(i, span):
        hat, _ = normed_parts(x1[span, :])
        n2[span, :] = (hat * gain2 + shift2).astype(bf16)

    by_rows(rows, 4, norm_step)
    for wait in waits:
        wait.wait()
    feed_back(z, dy_refs, dy_plan, spread_matrix(z.cols, 3 * block), wide, x1, n2, act, slope,
              widen, narrow, gain2, dy, dh, dn2, o_gx1, prev, prev_small, o_mats, o_small)


def attend_back_kernel(z, block, x_plan, n_x, chained, finish, core_ref, *refs):
    refs = list(refs)
    x_refs = [refs.pop(0) for _ in range(n_x)]
    small_own, small_other = refs.pop(0), refs.pop(0)
    big = [(refs.pop(0), refs.pop(0)) for _ in range(2)]
    gx1, qkv, probs, low_mix, prev_small = (refs.pop(0) for _ in range(5))
    prev = refs.pop(0) if chained else None
    out, o_mats = refs.pop(0), refs.pop(0)
    triple, attend, xs, hat1, da, gmix, gqkv, dq, pair, load_sems = refs[:10]
    load = Loader(core_ref, block, load_sems)
    waits = [load.start(own, other, to) for (own, other), to in zip(big, (triple, attend))]
    small = load.small(small_own, small_other)
    wins, _, feats = xs.shape
    rows = wins * cells
    depth = z.depth
    masks = head_masks(depth)
    scale = depth**-0.5
    mats = 4 * feats

    def put(at, size, value):
        if prev is not None:
            value = value + prev[at : at + size, :].astype(f32)
        o_mats[at : at + size, :] = value.astype(bf16)

    da[...] = gx1[...].astype(bf16)
    attend_b = row_sum(gx1[...])
    waits[1].wait()
    gmix[:, cells:, :] = jnp.zeros((wins, tall - cells, feats), bf16)
    gmix[:, :cells, :] = mm_t(da[...], attend[...]).reshape(wins, cells, feats).astype(bf16)
    put(3 * feats, feats, t_mm(low_mix[...], da[...]))
    pair[...] = jnp.zeros_like(pair)

    def step(w, carry):
        for g in range(feats // 128):
            at = g * 128
            q = qkv[w, :, at : at + 128]
            k = qkv[w, :, feats + at : feats + at + 128]
            v = qkv[w, :, 2 * feats + at : 2 * feats + at + 128]
            wide = spread_heads(gmix[w, :, at : at + 128], masks)
            low = probs[w, g]
            high = low.astype(f32)[:cells]
            pulled = mm_t(v, wide)[:cells] * high
            ds = pulled - high * jnp.sum(pulled, 0, keepdims=True)
            pair[g] += ds
            ds = pad_rows(ds, tall).astype(bf16)
            gqkv[w, :, 2 * feats + at : 2 * feats + at + 128] = mm(low, wide)[:cells]
            gqkv[w, :, feats + at : feats + at + 128] = (
                mm(ds, spread_heads(q, masks))[:cells] * scale
            )
            gqkv[w, :, at : at + 128] = collect_heads(t_mm(ds, k), masks)[:cells] * scale
        return carry

    lax.fori_loop(0, wins, step, 0, unroll=4)
    spread = spread_matrix(z.cols, 3 * block)
    gain1 = small[gain1_row : gain1_row + 1]
    shift1 = small[shift1_row : shift1_row + 1]
    image_to_windows([row_reader(x_refs[a], *at) for a, at in x_plan], spread, xs)

    def hat_step(i, span):
        hat, _ = normed_parts(xs[pl.ds(i * 4, 4)].reshape(4 * cells, feats))
        hat1[span, :] = hat.astype(bf16)

    by_rows(rows, wins // 4, hat_step)
    waits[0].wait()
    columns = jnp.concatenate([gain1, shift1, jnp.zeros((6, feats), f32)], 0).T
    gain_column, shift_column = columns[:, 0:1], columns[:, 1:2]
    sums = []
    gain_grad = jnp.zeros((feats, 1), f32)
    shift_grad = jnp.zeros((8, feats), f32)
    for j in range(3):
        lanes = slice(j * feats, (j + 1) * feats)
        part = gqkv[:, :, lanes].reshape(rows, feats)
        total = row_sum(part)
        sums.append(total)
        dq[:, lanes] = part.astype(bf16)
        both = t_mm(hat1[...], dq[:, lanes])
        put(j * feats, feats, gain_column * both + shift_column * total)
        gain_grad += jnp.sum(both * triple[:, lanes].astype(f32), -1, keepdims=True)
        top = total.astype(bf16)
        rest = (total - top.astype(f32)).astype(bf16)
        shift_grad += mm_t(
            jnp.concatenate([top.astype(f32), rest.astype(f32), jnp.zeros((6, feats), f32)], 0)
            .astype(bf16),
            triple[:, lanes],
        )
    sums.append(jnp.broadcast_to(gain_grad, (feats, 8)).T[0:1])
    sums.append(shift_grad[0:1] + shift_grad[1:2])
    sums.append(attend_b)
    smalls = prev_small[...] + jnp.concatenate(
        sums + [jnp.zeros((small_rows - 6, feats), f32)], 0
    )
    put(mats, small_rows, smalls)
    flat = pair[...].reshape(z.groups * cells, z.lanes)
    cut = flat.shape[0] * z.lanes // feats
    more = flat[cut:]
    put(
        mats + small_rows,
        cut,
        jnp.concatenate(
            [flat[:cut], jnp.concatenate([more[:, :128], more[:, 128:]], 0)], 1
        ),
    )
    if finish:
        dn1 = refs[10]
        input_back(z, small, dq, triple, xs, gx1, dn1, spread, out)
    else:
        out[...] = dq[...]


def input_back(z, small, dq, triple, xs, gx1, dn1, spread, image_ref):
    wins, _, feats = xs.shape
    gain1 = small[gain1_row : gain1_row + 1]
    dn1[...] = mm_t(dq[...], triple[...])

    def norm_step(i, span):
        wide = pl.ds(i * 4, 4)
        hat, scale = normed_parts(xs[wide].reshape(4 * cells, feats))
        out = gx1[span, :] + norm_back(dn1[span, :], hat, scale, gain1)
        xs[wide] = out.reshape(4, cells, feats)

    by_rows(wins * cells, wins // 4, norm_step)
    windows_to_image(xs, spread, image_ref)


def input_kernel(z, block, x_plan, n_x, core_ref, *refs):
    refs = list(refs)
    x_refs = [refs.pop(0) for _ in range(n_x)]
    small_own, small_other, own, other, gx1, dq, out = (refs.pop(0) for _ in range(7))
    triple, xs, dn1, load_sems = refs
    load = Loader(core_ref, block, load_sems)
    wait = load.start(own, other, triple)
    small = load.small(small_own, small_other)
    spread = spread_matrix(z.cols, 3 * block)
    image_to_windows([row_reader(x_refs[a], *at) for a, at in x_plan], spread, xs)
    wait.wait()
    input_back(z, small, dq, triple, xs, gx1, dn1, spread, out)


class Sizes:
    def __init__(self, own_rows, cols, feats, hidden, heads):
        self.steps = own_rows // 7
        self.cols = cols
        self.feats = feats
        self.hidden = hidden
        self.wins = cols // 7
        self.rows = self.wins * cells
        self.depth = feats // heads
        self.groups = feats // 128
        self.lanes = 128 // self.depth * tall
        self.parts = 2
        self.feed_rows = 2 * hidden
        self.attend_rows = 4 * feats + small_rows + self.groups * cells * self.lanes // feats


def in_vmem(item):
    return pl.BlockSpec(item.shape, lambda i, c: (0,) * item.ndim)


hbm = pl.BlockSpec(memory_space=pl.ANY)


def of_core(item):
    return pl.BlockSpec((1,) + item.shape[1:], lambda i, c: (c[0], 0, 0, 0))


def shaped(shape, kind):
    return jax.ShapeDtypeStruct(shape, kind)


def call(kernel, z, core, inputs, outputs, scratch, passes):
    out_specs = [
        hbm if manual else pl.BlockSpec(shape, lambda i, c, n=len(shape): (0,) * n)
        for shape, _, manual in outputs
    ]
    return pl.pallas_call(
        kernel,
        grid_spec=pltpu.PrefetchScalarGridSpec(
            num_scalar_prefetch=1,
            grid=(1,),
            in_specs=[spec for _, spec in inputs],
            out_specs=out_specs,
            scratch_shapes=scratch,
        ),
        out_shape=[shaped(shape, kind) for shape, kind, _ in outputs],
        compiler_params=pltpu.CompilerParams(
            dimension_semantics=("arbitrary",), vmem_limit_bytes=vmem_bytes
        ),
        cost_estimate=pl.CostEstimate(
            flops=int(passes * 20 * z.rows * z.feats * (4 * z.feats + 2 * z.hidden)),
            bytes_accessed=int(passes * 300_000_000),
            transcendentals=0,
        ),
    )(core, *(item for item, _ in inputs))


def run_front(z, core, block, xs, x_plan, dys, dy_plan, params, base, mask, prev):
    with_back = 0 if dys is None else (1 if prev is None else 2)
    inputs = list(xs) + list(dys or [])
    inputs += [(a, in_vmem(a)) for a in params["small"] + [base]]
    if block == 1:
        inputs.append((mask, in_vmem(mask)))
    for own, other in params["big"]:
        inputs += [(own, hbm), (other, hbm)]
    if prev is not None:
        inputs += [(a, in_vmem(a)) for a in prev]
    feats, hidden, rows, wins = z.feats, z.hidden, z.rows, z.wins
    qkv = (wins, tall, 3 * feats)
    probs = (wins, z.groups, tall, z.lanes)
    outputs = [
        ((7, z.cols, feats), bf16, False),
        (qkv, bf16, True),
        (probs, bf16, True),
        ((rows, feats), bf16, True),
    ]
    if with_back:
        outputs += [
            ((rows, feats), f32, True),
            ((z.feed_rows, feats), bf16, False),
            ((small_rows, feats), f32, False),
        ]
    else:
        outputs += [
            ((rows, feats), f32, True),
            ((rows, hidden), bf16, True),
            ((rows, hidden), bf16, True),
        ]
    vm = pltpu.VMEM
    scratch = [
        vm((feats, 3 * feats), bf16),
        vm((feats, feats), bf16),
        vm((feats, hidden), bf16),
        vm((hidden, feats), bf16),
        vm((wins, cells, feats), f32),
        vm((rows, feats), bf16),
        vm(qkv, bf16),
        vm((3 if block else 1, z.groups, cells, z.lanes), f32),
        vm(probs, bf16),
        vm((wins, cells, feats), f32),
        vm((rows, feats), bf16),
        vm((rows, feats), f32),
        vm((rows, feats), bf16),
        vm((rows, hidden), bf16),
        vm((rows, hidden), bf16),
        vm((wins, cells, feats), f32),
        pltpu.SemaphoreType.DMA((4,)),
        pltpu.SemaphoreType.DMA((6,)),
    ]
    if with_back:
        scratch += [
            vm((rows, feats), bf16),
            vm((rows, hidden), bf16),
            vm((rows, feats), f32),
            vm((rows, feats), f32),
        ]
    kernel = partial(front_kernel, z, block, with_back, x_plan, dy_plan, len(xs), len(dys or []))
    return call(kernel, z, core, inputs, outputs, scratch, 2.5 if with_back else 1.2)


def run_feed_back(z, core, block, dys, dy_plan, params, kept, prev):
    inputs = list(dys) + [(a, in_vmem(a)) for a in params["small"]]
    for own, other in params["big"][2:]:
        inputs += [(own, hbm), (other, hbm)]
    inputs += [(a, in_vmem(a)) for a in kept + list(prev or [])]
    feats, hidden, rows = z.feats, z.hidden, z.rows
    outputs = [
        ((rows, feats), f32, False),
        ((z.feed_rows, feats), bf16, False),
        ((small_rows, feats), f32, False),
    ]
    vm = pltpu.VMEM
    scratch = [
        vm((feats, hidden), bf16),
        vm((hidden, feats), bf16),
        vm((z.wins, cells, feats), f32),
        vm((rows, feats), bf16),
        vm((rows, feats), bf16),
        vm((rows, hidden), bf16),
        vm((rows, feats), f32),
        pltpu.SemaphoreType.DMA((2,)),
    ]
    kernel = partial(feed_back_kernel, z, block, dy_plan, len(dys), prev is not None)
    return call(kernel, z, core, inputs, outputs, scratch, 1.2)


def run_attend_back(z, core, block, xs, x_plan, params, kept, prev, finish):
    inputs = list(xs) + [(a, in_vmem(a)) for a in params["small"]]
    for own, other in params["big"][:2]:
        inputs += [(own, hbm), (other, hbm)]
    inputs += [(a, in_vmem(a)) for a in kept]
    if prev is not None:
        inputs.append((prev, in_vmem(prev)))
    feats, rows, wins = z.feats, z.rows, z.wins
    outputs = [
        ((7, z.cols, feats), bf16, False) if finish else ((rows, 3 * feats), bf16, False),
        ((z.attend_rows, feats), bf16, False),
    ]
    vm = pltpu.VMEM
    scratch = [
        vm((feats, 3 * feats), bf16),
        vm((feats, feats), bf16),
        vm((wins, cells, feats), f32),
        vm((rows, feats), bf16),
        vm((rows, feats), bf16),
        vm((wins, tall, feats), bf16),
        vm((wins, cells, 3 * feats), f32),
        vm((rows, 3 * feats), bf16),
        vm((z.groups, cells, z.lanes), f32),
        pltpu.SemaphoreType.DMA((2,)),
    ]
    if finish:
        scratch.append(vm((rows, feats), f32))
    kernel = partial(attend_back_kernel, z, block, x_plan, len(xs), prev is not None, finish)
    return call(kernel, z, core, inputs, outputs, scratch, 1.5)


def run_input(z, core, block, xs, x_plan, params, kept):
    inputs = list(xs) + [(a, in_vmem(a)) for a in params["small"]]
    own, other = params["big"][0]
    inputs += [(own, hbm), (other, hbm)] + [(a, in_vmem(a)) for a in kept]
    vm = pltpu.VMEM
    scratch = [
        vm((z.feats, 3 * z.feats), bf16),
        vm((z.wins, cells, z.feats), f32),
        vm((z.rows, z.feats), f32),
        pltpu.SemaphoreType.DMA((1,)),
    ]
    kernel = partial(input_kernel, z, block, x_plan, len(xs))
    return call(kernel, z, core, inputs, [((7, z.cols, z.feats), bf16, False)], scratch, 0.4)[0]


def pair_index():
    place = np.arange(tall)
    u, w = place // 8, place % 8
    real = (u < 7) & (w < 7)
    index = (u[None, :] - u[:, None] + 6) * 13 + (w[None, :] - w[:, None] + 6)
    return np.where(real[:, None] & real[None, :], index, 169)[:cells]


def pair_onehot():
    return jnp.asarray(
        np.arange(169)[:, None] == pair_index().reshape(-1)[None, :], bf16
    )


def bias_base(table, z):
    spread = lax.dot_general(
        table, pair_onehot(), (((0,), (0,)), ((), ())), preferred_element_type=f32
    )
    spread = spread.reshape(z.groups, -1, cells, tall).transpose(0, 2, 1, 3)
    real = (np.arange(cells) % 8 < 7)[None, :, None, None]
    return (
        jnp.where(real, spread, masked_score).astype(bf16).reshape(z.groups, cells, z.lanes)
    )


def region_mask(z, step, first_row, total_rows):
    place = np.arange(tall)
    u, w = np.minimum(place // 8, 6), np.minimum(place % 8, 6)
    rows = jnp.mod(first_row + step * 7 + u + 3, total_rows)
    vertical = (rows >= total_rows - 7).astype(jnp.int32) + (rows >= total_rows - 3)
    kinds = []
    for column in (0, z.wins - 2, z.wins - 1):
        at = np.mod(column * 7 + w + 3, z.cols)
        horizontal = (at >= z.cols - 7).astype(np.int32) + (at >= z.cols - 3)
        code = vertical * 3 + horizontal
        alike = code[:cells, None] == code[None, :]
        kinds.append(jnp.where(alike, 0.0, masked_score).astype(f32))
    mask = jnp.stack(kinds)
    return jnp.tile(mask, (1, 1, z.lanes // tall))


def table_slope(pair, z, heads):
    pair = pair.reshape(z.groups, cells, -1, tall).transpose(1, 3, 0, 2).reshape(-1, heads)
    return mm(pair_onehot(), pair.astype(bf16))


def swap_cores(item):
    return lax.ppermute(item, "pipe", [(0, 1), (1, 0)])


def take(pair, index):
    return lax.dynamic_index_in_dim(pair, index, 0, keepdims=False)


def tie(item, *others):
    return lax.optimization_barrier((item,) + others)


class Reduction:
    near = 4

    def __init__(self, buf, owner):
        self.owner = owner
        self.count = lax.axis_size("rows")
        self.far = self.count // self.near
        self.place = lax.axis_index("rows")
        self.value = buf
        self.phase = 0

    def route(self, bit):
        base = self.owner * self.count
        return [(base + i, base + (i ^ bit)) for i in range(self.count)]

    def send(self, item, route):
        return lax.ppermute(item, ("pipe", "rows"), route)

    def scatter(self, value, size, unit, mine):
        value = value.reshape((size, -1) + value.shape[1:])
        arrived = [
            self.send(take(value, mine ^ d), self.route(d * unit)) for d in range(1, size)
        ]
        total = take(value, mine).astype(f32)
        for item in arrived:
            total = total + item.astype(f32)
        return total.astype(bf16)

    def gather(self, value, size, unit, mine):
        arrived = [self.send(value, self.route(d * unit)) for d in range(1, size)]
        out = jnp.zeros((size,) + value.shape, bf16)
        for d, item in enumerate([value] + arrived):
            out = lax.dynamic_update_index_in_dim(out, item, mine ^ d, 0)
        return out.reshape((-1,) + value.shape[1:])

    def advance(self):
        value = self.value
        if self.phase == 0:
            here, there = self.owner * self.count, (1 - self.owner) * self.count
            route = [(there + i, here + i) for i in range(self.count)]
            value = (value.astype(f32) + self.send(value, route).astype(f32)).astype(bf16)
        elif self.phase == 1:
            value = self.scatter(value, self.near, 1, self.place % self.near)
        elif self.phase == 2:
            value = self.scatter(value, self.far, self.near, self.place // self.near)
        elif self.phase == 3:
            value = self.gather(value, self.far, self.near, self.place // self.near)
        elif self.phase == 4:
            value = self.gather(value, self.near, 1, self.place % self.near)
        self.value = value
        self.phase += 1

    def join(self, other):
        joined = Reduction(jnp.concatenate([self.value, other.value], 0), self.owner)
        joined.phase = self.phase
        return joined

    def parted_whole(self, rows):
        return self.value[:rows], self.value[rows:]

    def parted(self, rows):
        pieces = self.value.reshape((self.near, -1) + self.value.shape[1:])
        return [
            part.reshape((-1,) + part.shape[2:]) for part in (pieces[:, :rows], pieces[:, rows:])
        ]


def on_device(
    image_tokens,
    out_grad,
    first_gain,
    first_shift,
    triple_weight,
    query_bias,
    value_bias,
    bias_table,
    attend_weight,
    attend_bias,
    second_gain,
    second_shift,
    widen_weight,
    widen_bias,
    narrow_weight,
    narrow_bias,
):
    core = lax.axis_index("pipe")
    core_id = core.astype(jnp.int32).reshape(1)
    count = lax.axis_size("rows")
    place = lax.axis_index("rows")
    batches, own_rows, cols, feats = image_tokens.shape
    heads = bias_table.shape[2]
    hidden = widen_weight.shape[2]
    z = Sizes(own_rows, cols, feats, hidden, heads)
    total_rows = own_rows * count
    first_row = place * own_rows

    small = jnp.concatenate(
        [
            first_gain,
            first_shift,
            query_bias,
            jnp.zeros_like(query_bias),
            value_bias,
            attend_bias,
            second_gain,
            second_shift,
            narrow_bias,
            widen_bias.reshape(-1, feats),
            jnp.zeros((small_rows - 9 - hidden // feats, feats), bf16),
        ],
        0,
    ).astype(f32)
    tables = [bias_table[0], swap_cores(bias_table[0])]
    first = core == 0
    big = (triple_weight, attend_weight, widen_weight, narrow_weight)
    params = {
        "small": [small, swap_cores(small)],
        "big": [(item, swap_cores(item)) for item in big],
    }
    to_previous = [((i + 1) % count, i) for i in range(count)]
    to_next = [(i, (i + 1) % count) for i in range(count)]
    base0 = bias_base(jnp.where(first, tables[0], tables[1]), z)

    def plain(item):
        return (item, in_vmem(item))

    image = (image_tokens, of_core(image_tokens))
    grad = (out_grad, of_core(out_grad))
    upper = [(0, (0, u)) for u in range(7)]
    lower = [(0, (0, u)) for u in range(7, 14)]

    y00, qkv00, probs00, mix00, x100, act00, slope00 = run_front(
        z, core_id, 0, [image], upper, None, None, params, base0, None, None
    )
    y0_halo = lax.ppermute(y00[:3], "rows", to_previous)
    late_grad, late_row, late_table, _ = tie(
        out_grad, first_row, jnp.where(first, tables[1], tables[0]), y00
    )
    grad_halo = lax.ppermute(take(late_grad, core)[:3], "rows", to_previous)
    masks = [region_mask(z, step, late_row, total_rows) for step in range(2)]
    base1 = bias_base(late_table, z)
    y01, qkv01, probs01, mix01, x101, act01, slope01 = run_front(
        z, core_id, 0, [image], lower, None, None, params, base0, None, None
    )

    entry0 = [plain(y00), plain(y01)]
    entry0_plan = [(0, (u,)) for u in range(3, 7)] + [(1, (u,)) for u in range(3)]
    entry1 = [plain(y01), plain(y0_halo)]
    entry1_plan = [(0, (u,)) for u in range(3, 7)] + [(1, (u,)) for u in range(3)]
    grad0_plan = [(0, (0, u)) for u in range(3, 10)]
    grad1_plan = [(0, (0, u)) for u in range(10, 14)] + [(1, (u,)) for u in range(3)]
    y10, qkv10, probs10, mix10, gx10, mats10, small10 = run_front(
        z, core_id, 1, entry0, entry0_plan, [grad], grad0_plan, params, base1, masks[0], None
    )
    y11, qkv11, probs11, mix11, gx11, mats11, small11 = run_front(
        z, core_id, 1, entry1, entry1_plan, [grad, plain(grad_halo)], grad1_plan, params,
        base1, masks[1], (mats10, small10),
    )
    feed1 = Reduction(mats11, 1)
    y1_halo = lax.ppermute(y11[4:], "rows", to_next)

    dx10, rest10 = run_attend_back(
        z, core_id, 1, entry0, entry0_plan, params,
        [gx10, qkv10, probs10, mix10, jnp.zeros((small_rows, feats), f32)], None, True,
    )
    dx11, rest11 = run_attend_back(
        z, core_id, 1, entry1, entry1_plan, params,
        [gx11, qkv11, probs11, mix11, small11], rest10, True,
    )
    dx1_halo = lax.ppermute(dx11[4:], "rows", to_next)
    attend1 = Reduction(rest11, 1)
    feed1.advance()

    attend1.advance()
    joined1 = feed1.join(attend1)
    gx01, mats01, small01 = run_feed_back(
        z, core_id, 0, [plain(dx10), plain(dx11)],
        [(0, (u,)) for u in range(4, 7)] + [(1, (u,)) for u in range(4)],
        params, [x101, act01, slope01], None,
    )
    dx1_halo, joined1.value = tie(dx1_halo, joined1.value)
    joined1.advance()
    gx00, mats00, small00 = run_feed_back(
        z, core_id, 0, [plain(dx1_halo), plain(dx10)],
        [(0, (u,)) for u in range(3)] + [(1, (u,)) for u in range(4)],
        params, [x100, act00, slope00], (mats01, small01),
    )
    feed0 = Reduction(mats00, 0)
    gx01, joined1.value = tie(gx01, joined1.value)
    joined1.advance()
    feed0.advance()
    dx01, rest01 = run_attend_back(
        z, core_id, 0, [image], lower, params,
        [gx01, qkv01, probs01, mix01, jnp.zeros((small_rows, feats), f32)], None, True,
    )
    gx00, feed0.value, joined1.value = tie(gx00, feed0.value, joined1.value)
    joined1.advance()
    feed0.advance()
    dq00, rest00 = run_attend_back(
        z, core_id, 0, [image], upper, params, [gx00, qkv00, probs00, mix00, small00], rest01,
        False,
    )
    rest00, feed0.value, joined1.value = tie(rest00, feed0.value, joined1.value)
    joined1.advance()
    attend0 = Reduction(rest00, 0)
    dx00 = run_input(z, core_id, 0, [image], upper, params, [gx00, dq00])
    attend0.advance()
    attend0.advance()
    joined = feed0.join(attend0)
    for _ in range(3):
        joined.advance()
    feed0, attend0 = joined.parted(feed0.value.shape[0])

    def exchanged(block0, block1):
        other = swap_cores(jnp.where(first, block1, block0))
        return jnp.where(first, jnp.stack([block0, other]), jnp.stack([other, block1]))[None]

    late_halo, _ = tie(y1_halo, rest00)
    final = jnp.concatenate([late_halo, y10, y11[:4]], 0)
    entry_grad = jnp.concatenate([dx1_halo, dx10, dx11[:4]], 0)
    block_outputs = exchanged(jnp.concatenate([y00, y01], 0), final)
    input_grads = exchanged(jnp.concatenate([dx00, dx01], 0), entry_grad)

    feed1, attend1 = joined1.parted_whole(hidden * 2)
    feed = jnp.where(first, feed0, feed1).astype(f32)
    rest = jnp.where(first, attend0, attend1).astype(f32)

    def blocks(item, at, number):
        return jnp.concatenate(
            [item[at + i * feats : at + (i + 1) * feats] for i in range(number)], 1
        )[None]

    sums = rest[4 * feats : 4 * feats + small_rows]
    flat = rest[4 * feats + small_rows :]
    cut = flat.shape[0]
    left = z.groups * cells - cut
    more = flat[:, z.lanes :]
    pair = jnp.concatenate(
        [flat[:, : z.lanes], jnp.concatenate([more[:left], more[left:]], 1)], 0
    )

    def line(at):
        return sums[at : at + 1]

    return (
        block_outputs,
        input_grads,
        line(s_gain1),
        line(s_shift1),
        blocks(rest, 0, 3),
        line(0),
        line(2),
        table_slope(pair, z, heads)[None],
        rest[3 * feats : 4 * feats][None],
        line(s_attend_b),
        line(s_gain2),
        line(s_shift2),
        blocks(feed, 0, hidden // feats),
        sums[s_widen_b : s_widen_b + hidden // feats].reshape(1, hidden),
        feed[hidden:][None],
        line(s_narrow_b),
    )


def solution(mesh):
    param_specs = [
        P("pipe", None),
        P("pipe", None),
        P("pipe", None, None),
        P("pipe", None),
        P("pipe", None),
        P("pipe", None, None),
        P("pipe", None, None),
        P("pipe", None),
        P("pipe", None),
        P("pipe", None),
        P("pipe", None, None),
        P("pipe", None),
        P("pipe", None, None),
        P("pipe", None),
    ]
    in_specs = (P(None, "rows", None, None),) * 2 + tuple(param_specs)
    out_specs = (P("pipe", None, "rows", None, None),) * 2 + tuple(param_specs)
    return jax.shard_map(
        on_device, mesh=mesh, in_specs=in_specs, out_specs=out_specs, check_vma=False
    )
```

```python
from functools import partial

import jax
import jax.numpy as jnp
import numpy as np
from jax import lax
from jax.experimental import pallas as pl
from jax.experimental.pallas import tpu as pltpu
from jax.sharding import PartitionSpec as P

f32 = jnp.float32
bf16 = jnp.bfloat16
epsilon = 1e-05
masked_score = -1e30
vmem_bytes = 60 * 1024 * 1024
cells = 56
tall = 64

gain1_row, shift1_row, query_bias_row, value_bias_row = 0, 1, 2, 4
attend_bias_row, gain2_row, shift2_row, narrow_bias_row, widen_bias_row = 5, 6, 7, 8, 9
s_gain1, s_shift1, s_attend_b, s_gain2, s_shift2, s_narrow_b, s_widen_b = 3, 4, 5, 6, 7, 8, 9
small_rows = 16


def mm(left, right):
    return lax.dot_general(left, right, (((1,), (0,)), ((), ())), preferred_element_type=f32)


def mm_t(left, right):
    return lax.dot_general(left, right, (((1,), (1,)), ((), ())), preferred_element_type=f32)


def t_mm(left, right):
    return lax.dot_general(left, right, (((0,), (0,)), ((), ())), preferred_element_type=f32)


def normed_parts(values):
    center = values - jnp.mean(values, -1, keepdims=True)
    spread = jnp.mean(center * center, -1, keepdims=True)
    scale = lax.rsqrt(spread + epsilon)
    return center * scale, scale


def norm_back(grad, hat, scale, gain):
    pulled = grad * gain
    return scale * (
        pulled
        - jnp.mean(pulled, -1, keepdims=True)
        - hat * jnp.mean(pulled * hat, -1, keepdims=True)
    )


def gelu_parts(value):
    below = 0.5 + 0.5 * lax.erf(value * 0.5**0.5)
    bell = jnp.exp(value * value * -0.5)
    return value * below, below + value * bell * (2.0 * np.pi) ** -0.5


def row_sum(values):
    return jnp.sum(values, 0, keepdims=True)


def head_masks(depth):
    place = lax.broadcasted_iota(jnp.int32, (1, 128), 1) // depth
    return [(place == h) for h in range(128 // depth)]


def spread_heads(part, masks):
    return jnp.concatenate([part * m.astype(bf16) for m in masks], 0)


def collect_heads(high, masks):
    rows = high.shape[0] // len(masks)
    out = high[:rows]
    for h in range(1, len(masks)):
        out = jnp.where(masks[h], high[h * rows : (h + 1) * rows], out)
    return out


def pad_rows(values, rows):
    return jnp.concatenate(
        [values, jnp.zeros((rows - values.shape[0], values.shape[1]), values.dtype)], 0
    )


def spread_matrix(cols, roll_by):
    place = lax.broadcasted_iota(jnp.int32, (cols // 7 * 8, cols), 0)
    column = lax.broadcasted_iota(jnp.int32, (cols // 7 * 8, cols), 1)
    w = place & 7
    target = (place >> 3) * 7 + w + roll_by
    target = jnp.where(target >= cols, target - cols, target)
    return jnp.where((target == column) & (w < 7), 1.0, 0.0).astype(bf16)


def image_to_windows(image, spread, out):
    for u in range(7):
        part = mm(spread, image[u])
        out[:, u * 8 : (u + 1) * 8, :] = part.reshape(-1, 8, part.shape[-1])


def windows_to_image(windows, spread, image, rim=None, first=0):
    wins, _, feats = windows.shape
    for u in range(7):
        part = windows[:, u * 8 : (u + 1) * 8, :].reshape(wins * 8, feats).astype(bf16)
        row = t_mm(spread, part).astype(bf16)
        image[u] = row
        if rim is not None and first <= u < first + 3:
            rim[u - first] = row


def by_rows(rows, parts, step):
    size = rows // parts

    def body(i, carry):
        step(i, pl.ds(pl.multiple_of(i * size, size), size))
        return carry

    lax.fori_loop(0, parts, body, 0)


class Copies:
    def __init__(self, core_ref, block, sems):
        self.core = core_ref[0]
        self.mine = self.core == block
        self.sems = sems
        self.count = 0
        self.writes = []

    def next(self):
        self.count += 1
        return self.sems.at[self.count - 1]

    def start(self, source, target):
        copy = pltpu.make_async_copy(source, target, self.next())
        copy.start()
        return copy

    def pick(self, pair, target):
        own, other = pair
        sem = self.next()

        @pl.when(self.mine)
        def _():
            pltpu.make_async_copy(own.at[0], target, sem).start()

        @pl.when(jnp.logical_not(self.mine))
        def _():
            pltpu.make_async_copy(other.at[0], target, sem).start()

        return pltpu.make_async_copy(own.at[0], target, sem)

    def rows(self, refs, plan, target):
        at = 0
        copies = []
        for which, batched, first, size in plan:
            source = refs[which].at[self.core] if batched else refs[which]
            copies.append(
                self.start(source.at[pl.ds(first, size)], target.at[pl.ds(at, size)])
            )
            at += size
        return copies

    def write(self, source, target):
        self.writes.append(self.start(source, target))

    def finish(self):
        for copy in self.writes:
            copy.wait()

    def small(self, own, other):
        return jnp.where(self.mine, own[...], other[...])


def wait_all(copies):
    for copy in copies:
        copy.wait()


def stage_norm(xs, gain, shift, n1):
    wins, _, feats = xs.shape

    def step(i, span):
        hat, _ = normed_parts(xs[pl.ds(i * 4, 4)].reshape(4 * cells, feats))
        n1[span, :] = (hat * gain + shift).astype(bf16)

    by_rows(wins * cells, wins // 4, step)


def stage_triple(n1, triple, small, qkv):
    wins, _, width = qkv.shape
    feats = width // 3
    qkv[:, cells:, :] = jnp.zeros((wins, tall - cells, width), bf16)
    offsets = (query_bias_row, None, value_bias_row)
    for j in range(3):
        lanes = slice(j * feats, (j + 1) * feats)
        part = mm(n1[...], triple[:, lanes])
        if offsets[j] is not None:
            part = part + small[offsets[j] : offsets[j] + 1]
        qkv[:, :cells, lanes] = part.reshape(wins, cells, feats).astype(bf16)


def stage_attend(qkv, bias, probs, mixed, depth, shifted):
    wins, _, width = qkv.shape
    feats = width // 3
    masks = head_masks(depth)
    scale = depth**-0.5

    def step(w, carry):
        kind = jnp.maximum(w - (wins - 3), 0) if shifted else 0
        for g in range(feats // 128):
            at = g * 128
            q = qkv[w, :, at : at + 128]
            k = qkv[w, :, feats + at : feats + at + 128]
            v = qkv[w, :, 2 * feats + at : 2 * feats + at + 128]
            scores = mm_t(k, spread_heads(q, masks))[:cells] * scale + bias[kind, g]
            powers = jnp.exp(scores - jnp.max(scores, 0, keepdims=True))
            weights = powers * (1.0 / jnp.sum(powers, 0, keepdims=True))
            low = pad_rows(weights, tall).astype(bf16)
            probs[w, g] = low
            mixed[w, :, at : at + 128] = collect_heads(t_mm(low, v), masks)[:cells]
        return carry

    lax.fori_loop(0, wins, step, 0, unroll=8)


def forward_stages(z, block, copies, c, small, bias_parts, picks, x_waits):
    rows, feats = c.x1.shape
    base, mask = bias_parts
    base = base[...].astype(f32)
    if block == 1:
        for kind in range(3):
            for g in range(z.groups):
                c.bias[kind, g] = base[g] + mask[kind]
    else:
        c.bias[0] = base
    wait_all(x_waits)
    image_to_windows(c.x_rows, c.spread, c.xs)
    stage_norm(c.xs, small[gain1_row : gain1_row + 1], small[shift1_row : shift1_row + 1], c.n1)
    picks[0].wait()
    stage_triple(c.n1, c.triple, small, c.qkv)
    yield
    stage_attend(c.qkv, c.bias, c.probs, c.mixed, z.depth, block == 1)
    c.low_mix[...] = c.mixed[...].reshape(rows, feats).astype(bf16)
    yield
    picks[1].wait()
    c.x1[...] = (
        c.xs[...].reshape(rows, feats)
        + mm(c.low_mix[...], c.attend[...])
        + small[attend_bias_row : attend_bias_row + 1]
    )
    yield
    second_norm(small, c)
    picks[2].wait()
    part = z.hidden // z.parts
    for j in range(z.parts):
        lanes = slice(j * part, (j + 1) * part)
        offset = jnp.concatenate(
            [
                small[widen_bias_row + i : widen_bias_row + i + 1]
                for i in range(j * part // feats, (j + 1) * part // feats)
            ],
            1,
        )
        value, pull = gelu_parts(mm(c.n2[...], c.widen[:, lanes]) + offset)
        c.act[:, lanes] = value.astype(bf16)
        c.slope[:, lanes] = pull.astype(bf16)
    yield
    picks[3].wait()
    c.total[...] = (
        c.x1[...]
        + mm(c.act[...], c.narrow[...])
        + small[narrow_bias_row : narrow_bias_row + 1]
    ).reshape(c.total.shape)


def second_norm(small, c):
    gain2 = small[gain2_row : gain2_row + 1]
    shift2 = small[shift2_row : shift2_row + 1]

    def norm_step(i, span):
        hat, _ = normed_parts(c.x1[span, :])
        c.n2[span, :] = (hat * gain2 + shift2).astype(bf16)

    by_rows(c.x1.shape[0], 4, norm_step)


def feed_back_stages(z, copies, c, small, waits, prev, o_mats, o_small):
    rows, feats = c.x1.shape
    w_dy, w_narrow, w_slope, w_widen, w_x1, w_act, w_prev = waits
    wait_all(w_dy)
    image_to_windows(c.dy_rows, c.spread, c.total)
    c.dy[...] = c.total[...].reshape(rows, feats).astype(bf16)
    sums = {s_narrow_b: row_sum(c.total[...].reshape(rows, feats))}
    part = z.hidden // z.parts
    wait_all(w_narrow + w_slope)
    for j in range(z.parts):
        lanes = slice(j * part, (j + 1) * part)
        grad = mm_t(c.dy[...], c.narrow[lanes, :]) * c.slope[:, lanes].astype(f32)
        total = row_sum(grad)
        for i in range(part // feats):
            sums[s_widen_b + j * part // feats + i] = total[:, i * feats : (i + 1) * feats]
        c.dh[:, lanes] = grad.astype(bf16)
    wait_all(w_widen + w_x1)
    if w_x1:
        second_norm(small, c)
    c.dn2[...] = mm_t(c.dh[...], c.widen[...])
    gain2 = small[gain2_row : gain2_row + 1]

    def norm_step(i, span):
        hat, scale = normed_parts(c.x1[span, :])
        grad = c.dn2[span, :]
        o_small[s_gain2 : s_gain2 + 1] += row_sum(grad * hat)
        o_small[s_shift2 : s_shift2 + 1] += row_sum(grad)
        c.gx1[span, :] = c.dy[span, :].astype(f32) + norm_back(grad, hat, scale, gain2)

    for at, value in sums.items():
        o_small[at : at + 1] += value
    by_rows(rows, 4, norm_step)
    yield
    wait_all(w_prev)

    def put(at, value):
        span = slice(at, at + feats)
        if prev is not None:
            value = value + prev[span, :].astype(f32)
        c.mats[span, :] = value.astype(bf16)

    for j in range(z.hidden // feats):
        put(j * feats, t_mm(c.n2[...], c.dh[:, j * feats : (j + 1) * feats]))
    half = c.mats.shape[0] // 2
    copies.write(c.mats.at[pl.ds(0, half)], o_mats.at[pl.ds(0, half)])
    wait_all(w_act)
    for j in range(z.hidden // feats):
        put(z.hidden + j * feats, t_mm(c.act[:, j * feats : (j + 1) * feats], c.dy[...]))
    copies.write(c.mats.at[pl.ds(half, half)], o_mats.at[pl.ds(half, half)])


def attend_back_stages(z, copies, c, small, waits, prev, o_rest, smalls):
    w_gx1, w_attend, w_mix, w_qkv, w_x, w_triple, w_prev = waits
    wins, _, feats = c.xs.shape
    rows = wins * cells
    depth = z.depth
    masks = head_masks(depth)
    scale = depth**-0.5
    mats = 4 * feats
    qkv, probs, gmix, gqkv, pair = c.qkv, c.probs, c.gmix, c.gqkv, c.pair
    wait_all(w_gx1)
    c.da[...] = c.gx1[...].astype(bf16)
    attend_b = row_sum(c.gx1[...])
    wait_all(w_attend)
    gmix[:, cells:, :] = jnp.zeros((wins, tall - cells, feats), bf16)
    gmix[:, :cells, :] = mm_t(c.da[...], c.attend[...]).reshape(wins, cells, feats).astype(bf16)
    pair[...] = jnp.zeros_like(pair)
    wait_all(w_qkv)

    def step(w, carry):
        for g in range(feats // 128):
            at = g * 128
            q = qkv[w, :, at : at + 128]
            k = qkv[w, :, feats + at : feats + at + 128]
            v = qkv[w, :, 2 * feats + at : 2 * feats + at + 128]
            wide = spread_heads(gmix[w, :, at : at + 128], masks)
            low = probs[w, g]
            high = low.astype(f32)[:cells]
            pulled = mm_t(v, wide)[:cells] * high
            ds = pulled - high * jnp.sum(pulled, 0, keepdims=True)
            pair[g] += ds
            ds = pad_rows(ds, tall).astype(bf16)
            gqkv[w, :, 2 * feats + at : 2 * feats + at + 128] = mm(low, wide)[:cells]
            gqkv[w, :, feats + at : feats + at + 128] = (
                mm(ds, spread_heads(q, masks))[:cells] * scale
            )
            gqkv[w, :, at : at + 128] = collect_heads(t_mm(ds, k), masks)[:cells] * scale
        return carry

    lax.fori_loop(0, wins, step, 0, unroll=8)
    gain1 = small[gain1_row : gain1_row + 1]
    shift1 = small[shift1_row : shift1_row + 1]
    if w_x:
        wait_all(w_x)
        image_to_windows(c.x_rows, c.spread, c.xs)

    def hat_step(i, span):
        hat, _ = normed_parts(c.xs[pl.ds(i * 4, 4)].reshape(4 * cells, feats))
        c.n1[span, :] = hat.astype(bf16)

    by_rows(rows, wins // 4, hat_step)
    wait_all(w_triple + w_mix + w_prev)

    def put(at, size, value):
        if prev is not None:
            value = value + prev[at : at + size, :].astype(f32)
        c.rest[at : at + size, :] = value.astype(bf16)

    put(3 * feats, feats, t_mm(c.low_mix[...], c.da[...]))
    columns = jnp.concatenate([gain1, shift1, jnp.zeros((6, feats), f32)], 0).T
    gain_column, shift_column = columns[:, 0:1], columns[:, 1:2]
    sums = []
    gain_grad = jnp.zeros((feats, 1), f32)
    shift_grad = jnp.zeros((8, feats), f32)
    for j in range(3):
        lanes = slice(j * feats, (j + 1) * feats)
        part = gqkv[:, :, lanes].reshape(rows, feats)
        total = row_sum(part)
        sums.append(total)
        c.dq[:, lanes] = part.astype(bf16)
        both = t_mm(c.n1[...], c.dq[:, lanes])
        put(j * feats, feats, gain_column * both + shift_column * total)
        gain_grad += jnp.sum(both * c.triple[:, lanes].astype(f32), -1, keepdims=True)
        top = total.astype(bf16)
        rest = (total - top.astype(f32)).astype(bf16)
        shift_grad += mm_t(
            jnp.concatenate([top.astype(f32), rest.astype(f32), jnp.zeros((6, feats), f32)], 0)
            .astype(bf16),
            c.triple[:, lanes],
        )
    sums.append(jnp.broadcast_to(gain_grad, (feats, 8)).T[0:1])
    sums.append(shift_grad[0:1] + shift_grad[1:2])
    sums.append(attend_b)
    put(
        mats,
        small_rows,
        smalls[...] + jnp.concatenate(sums + [jnp.zeros((small_rows - 6, feats), f32)], 0),
    )
    flat = pair[...].reshape(z.groups * cells, z.lanes)
    cut = flat.shape[0] * z.lanes // feats
    more = flat[cut:]
    put(
        mats + small_rows,
        cut,
        jnp.concatenate([flat[:cut], jnp.concatenate([more[:, :128], more[:, 128:]], 0)], 1),
    )
    copies.write(c.rest, o_rest)


def input_stages(z, c, small):
    wins, _, feats = c.xs.shape
    gain1 = small[gain1_row : gain1_row + 1]
    c.dn2[...] = mm_t(c.dq[...], c.triple[...])

    def norm_step(i, span):
        wide = pl.ds(i * 4, 4)
        hat, scale = normed_parts(c.xs[wide].reshape(4 * cells, feats))
        out = c.gx1[span, :] + norm_back(c.dn2[span, :], hat, scale, gain1)
        c.xs[wide] = out.reshape(4, cells, feats)

    by_rows(wins * cells, wins // 4, norm_step)


class Refs:
    def __init__(self, refs, names):
        self.refs = list(refs)
        for name in names:
            setattr(self, name, self.refs.pop(0))

    def several(self, number):
        return [self.refs.pop(0) for _ in range(number)]

    def pairs(self, number):
        return [tuple(self.several(2)) for _ in range(number)]

    def name(self, names):
        for name in names:
            setattr(self, name, self.refs.pop(0))


def forward_kernel(z, n_x, x_plan, scratch, core_ref, *refs):
    c = Refs(refs, ())
    x_refs = c.several(n_x)
    c.name(("own", "other", "base"))
    big = c.pairs(4)
    c.name(("y", "rim", "o_qkv", "o_probs", "o_mix", "o_x1", "o_act", "o_slope"))
    c.name(scratch)
    copies = Copies(core_ref, 0, c.sems)
    x_waits = copies.rows(x_refs, x_plan, c.x_rows)
    picks = [copies.pick(p, to) for p, to in zip(big, (c.triple, c.attend, c.widen, c.narrow))]
    small = copies.small(c.own, c.other)
    c.spread = spread_matrix(z.cols, 0)
    stages = forward_stages(z, 0, copies, c, small, (c.base, None), picks, x_waits)
    next(stages)
    copies.write(c.qkv, c.o_qkv)
    next(stages)
    copies.write(c.probs, c.o_probs)
    copies.write(c.low_mix, c.o_mix)
    next(stages)
    copies.write(c.x1, c.o_x1)
    next(stages)
    copies.write(c.act, c.o_act)
    copies.write(c.slope, c.o_slope)
    for _ in stages:
        pass
    windows_to_image(c.total, c.spread, c.y, c.rim, 0)
    copies.finish()


def both_kernel(z, n_x, x_plan, n_dy, dy_plan, chained, scratch, core_ref, *refs):
    c = Refs(refs, ())
    x_refs = c.several(n_x)
    dy_refs = c.several(n_dy)
    c.name(("own", "other", "base", "mask"))
    big = c.pairs(4)
    prev = c.several(2) if chained else None
    c.name(("y", "y_rim", "dx", "dx_rim", "o_mats", "o_rest"))
    c.name(scratch)
    copies = Copies(core_ref, 1, c.sems)
    x_waits = copies.rows(x_refs, x_plan, c.x_rows)
    picks = [copies.pick(p, to) for p, to in zip(big, (c.triple, c.attend, c.widen, c.narrow))]
    dy_waits = copies.rows(dy_refs, dy_plan, c.dy_rows)
    prev_waits = [[], []]
    if chained:
        prev_waits = [[copies.start(a, b)] for a, b in zip(prev, (c.prev_mats, c.prev_rest))]
    prev_refs = (c.prev_mats, c.prev_rest) if chained else (None, None)
    small = copies.small(c.own, c.other)
    c.spread = spread_matrix(z.cols, 3)
    c.smalls[...] = jnp.zeros_like(c.smalls)
    for _ in forward_stages(z, 1, copies, c, small, (c.base, c.mask), picks, x_waits):
        pass
    windows_to_image(c.total, c.spread, c.y, c.y_rim, 4)
    waits = (dy_waits, [], [], [], [], [], prev_waits[0])
    for _ in feed_back_stages(z, copies, c, small, waits, prev_refs[0], c.o_mats, c.smalls):
        pass
    waits = ([], [], [], [], [], [], prev_waits[1])
    attend_back_stages(z, copies, c, small, waits, prev_refs[1], c.o_rest, c.smalls)
    input_stages(z, c, small)
    windows_to_image(c.xs, c.spread, c.dx, c.dx_rim, 4)
    copies.finish()


def feed_back_kernel(z, n_dy, dy_plan, chained, scratch, core_ref, *refs):
    c = Refs(refs, ())
    dy_refs = c.several(n_dy)
    c.name(("own", "other"))
    big = c.pairs(2)
    kept = c.several(3)
    prev = c.several(2) if chained else None
    c.name(("o_gx1", "o_mats", "o_small"))
    c.name(scratch)
    copies = Copies(core_ref, 0, c.sems)
    w_dy = copies.rows(dy_refs, dy_plan, c.dy_rows)
    w_narrow = copies.pick(big[1], c.narrow)
    w_slope = copies.start(kept[2], c.slope)
    w_widen = copies.pick(big[0], c.widen)
    w_x1 = copies.start(kept[0], c.x1)
    w_act = copies.start(kept[1], c.act)
    w_prev = [copies.start(prev[0], c.prev_mats)] if chained else []
    small = copies.small(c.own, c.other)
    c.spread = spread_matrix(z.cols, 0)
    c.o_small[...] = prev[1][...] if chained else jnp.zeros_like(c.o_small)
    waits = (w_dy, [w_narrow], [w_slope], [w_widen], [w_x1], [w_act], w_prev)
    stages = feed_back_stages(
        z, copies, c, small, waits, c.prev_mats if chained else None, c.o_mats, c.o_small
    )
    next(stages)
    copies.write(c.gx1, c.o_gx1)
    for _ in stages:
        pass
    copies.finish()


def attend_back_kernel(z, n_x, x_plan, chained, last, scratch, core_ref, *refs):
    c = Refs(refs, ())
    x_refs = c.several(n_x)
    c.name(("own", "other"))
    big = c.pairs(2)
    kept = c.several(4)
    c.name(("smalls",))
    prev = c.several(1) if chained else None
    c.name(("out", "o_rest"))
    c.name(scratch)
    copies = Copies(core_ref, 0, c.sems)
    w_gx1 = copies.start(kept[0], c.gx1)
    w_attend = copies.pick(big[1], c.attend)
    w_qkv = [copies.start(kept[1], c.qkv), copies.start(kept[2], c.probs)]
    w_x = copies.rows(x_refs, x_plan, c.x_rows)
    w_mix = copies.start(kept[3], c.low_mix)
    w_triple = copies.pick(big[0], c.triple)
    w_prev = [copies.start(prev[0], c.prev_rest)] if chained else []
    small = copies.small(c.own, c.other)
    c.spread = spread_matrix(z.cols, 0)
    waits = ([w_gx1], [w_attend], [w_mix], w_qkv, w_x, [w_triple], w_prev)
    attend_back_stages(
        z, copies, c, small, waits, c.prev_rest if chained else None, c.o_rest, c.smalls
    )
    if last:
        copies.write(c.dq, c.out)
    else:
        input_stages(z, c, small)
        windows_to_image(c.xs, c.spread, c.out)
    copies.finish()


def input_kernel(z, n_x, x_plan, scratch, core_ref, *refs):
    c = Refs(refs, ())
    x_refs = c.several(n_x)
    c.name(("own", "other"))
    big = c.pairs(1)
    kept = c.several(2)
    c.name(("out",))
    c.name(scratch)
    copies = Copies(core_ref, 0, c.sems)
    w_dq = copies.start(kept[1], c.dq)
    w_triple = copies.pick(big[0], c.triple)
    w_x = copies.rows(x_refs, x_plan, c.x_rows)
    w_gx1 = copies.start(kept[0], c.gx1)
    small = copies.small(c.own, c.other)
    c.spread = spread_matrix(z.cols, 0)
    wait_all(w_x)
    image_to_windows(c.x_rows, c.spread, c.xs)
    wait_all([w_dq, w_triple, w_gx1])
    input_stages(z, c, small)
    windows_to_image(c.xs, c.spread, c.out)
    copies.finish()


class Sizes:
    def __init__(self, own_rows, cols, feats, hidden, heads):
        self.steps = own_rows // 7
        self.cols = cols
        self.feats = feats
        self.hidden = hidden
        self.wins = cols // 7
        self.rows = self.wins * cells
        self.depth = feats // heads
        self.groups = feats // 128
        self.lanes = 128 // self.depth * tall
        self.parts = 2
        self.feed_rows = 2 * hidden
        self.attend_rows = 4 * feats + small_rows + self.groups * cells * self.lanes // feats


def in_vmem(item):
    return pl.BlockSpec(item.shape, lambda i, c: (0,) * item.ndim)


hbm = pl.BlockSpec(memory_space=pl.ANY)


def shaped(shape, kind):
    return jax.ShapeDtypeStruct(shape, kind)


def scratch_table(z):
    feats, hidden, rows, wins = z.feats, z.hidden, z.rows, z.wins
    image = ((7, z.cols, feats), bf16)
    wide = ((wins, cells, feats), f32)
    low = ((rows, feats), bf16)
    high = ((rows, feats), f32)
    deep = ((rows, hidden), bf16)
    return {
        "triple": ((feats, 3 * feats), bf16),
        "attend": ((feats, feats), bf16),
        "widen": ((feats, hidden), bf16),
        "narrow": ((hidden, feats), bf16),
        "x_rows": image,
        "dy_rows": image,
        "xs": wide,
        "n1": low,
        "qkv": ((wins, tall, 3 * feats), bf16),
        "bias": ((3, z.groups, cells, z.lanes), f32),
        "probs": ((wins, z.groups, tall, z.lanes), bf16),
        "mixed": wide,
        "low_mix": low,
        "x1": high,
        "n2": low,
        "act": deep,
        "slope": deep,
        "total": wide,
        "dy": low,
        "dh": deep,
        "dn2": high,
        "gx1": high,
        "mats": ((z.feed_rows, feats), bf16),
        "prev_mats": ((z.feed_rows, feats), bf16),
        "smalls": ((small_rows, feats), f32),
        "da": low,
        "gmix": ((wins, tall, feats), bf16),
        "gqkv": ((wins, cells, 3 * feats), f32),
        "dq": ((rows, 3 * feats), bf16),
        "pair": ((z.groups, cells, z.lanes), f32),
        "rest": ((z.attend_rows, feats), bf16),
        "prev_rest": ((z.attend_rows, feats), bf16),
    }


def call(kernel, z, core, inputs, outputs, scratch, passes):
    inputs = [item if isinstance(item, tuple) else (item, hbm) for item in inputs]
    out_specs = [
        hbm if manual else pl.BlockSpec(shape, lambda i, c, n=len(shape): (0,) * n)
        for shape, _, manual in outputs
    ]
    table = scratch_table(z)
    return pl.pallas_call(
        partial(kernel, scratch + ("sems",)),
        grid_spec=pltpu.PrefetchScalarGridSpec(
            num_scalar_prefetch=1,
            grid=(1,),
            in_specs=[spec for _, spec in inputs],
            out_specs=out_specs,
            scratch_shapes=[pltpu.VMEM(*table[name]) for name in scratch]
            + [pltpu.SemaphoreType.DMA((20,))],
        ),
        out_shape=[shaped(shape, kind) for shape, kind, _ in outputs],
        compiler_params=pltpu.CompilerParams(
            dimension_semantics=("arbitrary",), vmem_limit_bytes=vmem_bytes
        ),
        cost_estimate=pl.CostEstimate(
            flops=int(passes * 20 * z.rows * z.feats * (4 * z.feats + 2 * z.hidden)),
            bytes_accessed=int(passes * 300_000_000),
            transcendentals=0,
        ),
    )(core, *(item for item, _ in inputs))


def resident(items):
    return [(item, in_vmem(item)) for item in items]


def flat_pairs(pairs):
    return [item for pair in pairs for item in pair]


forward_scratch = (
    "triple", "attend", "widen", "narrow", "x_rows", "xs", "n1", "qkv", "bias", "probs", "mixed",
    "low_mix", "x1", "n2", "act", "slope", "total",
)
back_scratch = ("dy_rows", "dy", "dh", "dn2", "gx1", "mats")
attend_back_scratch = ("da", "gmix", "gqkv", "dq", "pair", "rest")


def run_forward(z, core, xs, x_plan, params, base):
    inputs = list(xs) + resident(params["small"] + [base]) + flat_pairs(params["big"])
    table = scratch_table(z)
    rim = ((3, z.cols, z.feats), bf16, False)
    outputs = [(*table["x_rows"], False), rim] + [
        (*table[name], True) for name in ("qkv", "probs", "low_mix", "x1", "act", "slope")
    ]
    kernel = partial(bind, forward_kernel, (z, len(xs), x_plan))
    return call(kernel, z, core, inputs, outputs, forward_scratch, 1.2)


def bind(kernel, arguments, scratch, *refs):
    kernel(*arguments, scratch, *refs)


def run_both(z, core, xs, x_plan, dys, dy_plan, params, base, mask, prev):
    inputs = list(xs) + list(dys) + resident(params["small"] + [base, mask])
    inputs += flat_pairs(params["big"]) + list(prev or [])
    table = scratch_table(z)
    image = (*table["x_rows"], False)
    rim = ((3, z.cols, z.feats), bf16, False)
    outputs = [image, rim, image, rim] + [(*table[name], True) for name in ("mats", "rest")]
    scratch = forward_scratch + back_scratch + attend_back_scratch + ("smalls",)
    if prev:
        scratch += ("prev_mats", "prev_rest")
    arguments = (z, len(xs), x_plan, len(dys), dy_plan, bool(prev))
    return call(partial(bind, both_kernel, arguments), z, core, inputs, outputs, scratch, 4.0)


def run_feed_back(z, core, dys, dy_plan, params, kept, prev):
    inputs = list(dys) + resident(params["small"]) + flat_pairs(params["big"][2:]) + list(kept)
    if prev:
        inputs += [prev[0]] + resident(prev[1:])
    table = scratch_table(z)
    outputs = [(*table["gx1"], True), (*table["mats"], True), (*table["smalls"], False)]
    scratch = back_scratch + ("widen", "narrow", "x1", "n2", "act", "slope", "total")
    if prev:
        scratch += ("prev_mats",)
    arguments = (z, len(dys), dy_plan, bool(prev))
    return call(
        partial(bind, feed_back_kernel, arguments), z, core, inputs, outputs, scratch, 1.2
    )


def run_attend_back(z, core, xs, x_plan, params, kept, smalls, prev, last):
    inputs = list(xs) + resident(params["small"]) + flat_pairs(params["big"][:2]) + list(kept)
    inputs += resident([smalls])
    if prev is not None:
        inputs.append(prev)
    table = scratch_table(z)
    outputs = [
        (*table["dq"], True) if last else (*table["x_rows"], False),
        (*table["rest"], True),
    ]
    scratch = attend_back_scratch + (
        "triple", "attend", "x_rows", "xs", "n1", "qkv", "probs", "low_mix", "gx1", "dn2",
    )
    if prev is not None:
        scratch += ("prev_rest",)
    arguments = (z, len(xs), x_plan, prev is not None, last)
    return call(
        partial(bind, attend_back_kernel, arguments), z, core, inputs, outputs, scratch, 1.5
    )


def run_input(z, core, xs, x_plan, params, kept):
    inputs = list(xs) + resident(params["small"]) + flat_pairs(params["big"][:1]) + list(kept)
    scratch = ("triple", "x_rows", "xs", "gx1", "dq", "dn2")
    arguments = (z, len(xs), x_plan)
    outputs = [(*scratch_table(z)["x_rows"], False)]
    return call(partial(bind, input_kernel, arguments), z, core, inputs, outputs, scratch, 0.4)[0]


def pair_index():
    place = np.arange(tall)
    u, w = place // 8, place % 8
    real = (u < 7) & (w < 7)
    index = (u[None, :] - u[:, None] + 6) * 13 + (w[None, :] - w[:, None] + 6)
    return np.where(real[:, None] & real[None, :], index, 169)[:cells]


def pair_onehot():
    return jnp.asarray(
        np.arange(169)[:, None] == pair_index().reshape(-1)[None, :], bf16
    )


def bias_base(table, z):
    spread = lax.dot_general(
        table, pair_onehot(), (((0,), (0,)), ((), ())), preferred_element_type=f32
    )
    spread = spread.reshape(z.groups, -1, cells, tall).transpose(0, 2, 1, 3)
    real = (np.arange(cells) % 8 < 7)[None, :, None, None]
    return (
        jnp.where(real, spread, masked_score).astype(bf16).reshape(z.groups, cells, z.lanes)
    )


def region_mask(z, step, first_row, total_rows):
    place = np.arange(tall)
    u, w = np.minimum(place // 8, 6), np.minimum(place % 8, 6)
    rows = jnp.mod(first_row + step * 7 + u + 3, total_rows)
    vertical = (rows >= total_rows - 7).astype(jnp.int32) + (rows >= total_rows - 3)
    kinds = []
    for column in (0, z.wins - 2, z.wins - 1):
        at = np.mod(column * 7 + w + 3, z.cols)
        horizontal = (at >= z.cols - 7).astype(np.int32) + (at >= z.cols - 3)
        code = vertical * 3 + horizontal
        alike = code[:cells, None] == code[None, :]
        kinds.append(jnp.where(alike, 0.0, masked_score).astype(f32))
    mask = jnp.stack(kinds)
    return jnp.tile(mask, (1, 1, z.lanes // tall))


def table_slope(pair, z, heads):
    pair = pair.reshape(z.groups, cells, -1, tall).transpose(1, 3, 0, 2).reshape(-1, heads)
    return mm(pair_onehot(), pair.astype(bf16))


def swap_cores(item):
    return lax.ppermute(item, "pipe", [(0, 1), (1, 0)])


def take(pair, index):
    return lax.dynamic_index_in_dim(pair, index, 0, keepdims=False)


def tie(item, *others):
    return lax.optimization_barrier((item,) + others)


class Reduction:
    near = 4

    def __init__(self, buf, owner):
        self.owner = owner
        self.count = lax.axis_size("rows")
        self.far = self.count // self.near
        self.place = lax.axis_index("rows")
        self.value = buf
        self.phase = 0

    def route(self, bit):
        base = self.owner * self.count
        return [(base + i, base + (i ^ bit)) for i in range(self.count)]

    def send(self, item, route):
        return lax.ppermute(item, ("pipe", "rows"), route)

    def scatter(self, value, size, unit, mine):
        value = value.reshape((size, -1) + value.shape[1:])
        arrived = [
            self.send(take(value, mine ^ d), self.route(d * unit)) for d in range(1, size)
        ]
        total = take(value, mine).astype(f32)
        for item in arrived:
            total = total + item.astype(f32)
        return total.astype(bf16)

    def gather(self, value, size, unit, mine):
        arrived = [self.send(value, self.route(d * unit)) for d in range(1, size)]
        out = jnp.zeros((size,) + value.shape, bf16)
        for d, item in enumerate([value] + arrived):
            out = lax.dynamic_update_index_in_dim(out, item, mine ^ d, 0)
        return out.reshape((-1,) + value.shape[1:])

    def advance(self):
        value = self.value
        if self.phase == 0:
            here, there = self.owner * self.count, (1 - self.owner) * self.count
            route = [(there + i, here + i) for i in range(self.count)]
            value = (value.astype(f32) + self.send(value, route).astype(f32)).astype(bf16)
        elif self.phase == 1:
            value = self.scatter(value, self.near, 1, self.place % self.near)
        elif self.phase == 2:
            value = self.scatter(value, self.far, self.near, self.place // self.near)
        elif self.phase == 3:
            value = self.gather(value, self.far, self.near, self.place // self.near)
        elif self.phase == 4:
            value = self.gather(value, self.near, 1, self.place % self.near)
        self.value = value
        self.phase += 1

    def join(self, other):
        joined = Reduction(jnp.concatenate([self.value, other.value], 0), self.owner)
        joined.phase = self.phase
        return joined

    def parted_whole(self, rows):
        return self.value[:rows], self.value[rows:]

    def parted(self, rows):
        pieces = self.value.reshape((self.near, -1) + self.value.shape[1:])
        return [
            part.reshape((-1,) + part.shape[2:]) for part in (pieces[:, :rows], pieces[:, rows:])
        ]


def on_device(
    image_tokens,
    out_grad,
    first_gain,
    first_shift,
    triple_weight,
    query_bias,
    value_bias,
    bias_table,
    attend_weight,
    attend_bias,
    second_gain,
    second_shift,
    widen_weight,
    widen_bias,
    narrow_weight,
    narrow_bias,
):
    core = lax.axis_index("pipe")
    core_id = core.astype(jnp.int32).reshape(1)
    count = lax.axis_size("rows")
    place = lax.axis_index("rows")
    batches, own_rows, cols, feats = image_tokens.shape
    heads = bias_table.shape[2]
    hidden = widen_weight.shape[2]
    z = Sizes(own_rows, cols, feats, hidden, heads)
    total_rows = own_rows * count
    first_row = place * own_rows

    small = jnp.concatenate(
        [
            first_gain,
            first_shift,
            query_bias,
            jnp.zeros_like(query_bias),
            value_bias,
            attend_bias,
            second_gain,
            second_shift,
            narrow_bias,
            widen_bias.reshape(-1, feats),
            jnp.zeros((small_rows - 9 - hidden // feats, feats), bf16),
        ],
        0,
    ).astype(f32)
    tables = [bias_table[0], swap_cores(bias_table[0])]
    first = core == 0
    big = (triple_weight, attend_weight, widen_weight, narrow_weight)
    params = {
        "small": [small, swap_cores(small)],
        "big": [(item, swap_cores(item)) for item in big],
    }
    to_previous = [((i + 1) % count, i) for i in range(count)]
    to_next = [(i, (i + 1) % count) for i in range(count)]
    base0 = bias_base(jnp.where(first, tables[0], tables[1]), z)

    upper = [(0, True, 0, 7)]
    lower = [(0, True, 7, 7)]

    y00, y0_rim, *kept0 = run_forward(z, core_id, [image_tokens], upper, params, base0)
    y0_halo = lax.ppermute(y0_rim, "rows", to_previous)
    late_grad, late_row, late_table, _ = tie(
        out_grad, first_row, jnp.where(first, tables[1], tables[0]), y00
    )
    grad_halo = lax.ppermute(take(late_grad, core)[:3], "rows", to_previous)
    masks = [region_mask(z, step, late_row, total_rows) for step in range(2)]
    base1 = bias_base(late_table, z)
    y01, _, *kept1 = run_forward(z, core_id, [image_tokens], lower, params, base0)
    (qkv0, probs0, mix0, x10, act0, slope0) = kept0
    (qkv1, probs1, mix1, x11, act1, slope1) = kept1

    y10, _, dx10, _, mats10, rest10 = run_both(
        z, core_id, [y00, y01], [(0, False, 3, 4), (1, False, 0, 3)], [out_grad],
        [(0, True, 3, 7)], params, base1, masks[0], None,
    )
    y11, y1_rim, dx11, dx1_rim, mats11, rest11 = run_both(
        z, core_id, [y01, y0_halo], [(0, False, 3, 4), (1, False, 0, 3)],
        [out_grad, grad_halo], [(0, True, 10, 4), (1, False, 0, 3)], params, base1, masks[1],
        (mats10, rest10),
    )
    dx1_halo = lax.ppermute(dx1_rim, "rows", to_next)
    feed1 = Reduction(mats11, 1)
    attend1 = Reduction(rest11, 1)
    y1_halo = lax.ppermute(y1_rim, "rows", to_next)

    feed1.advance()
    attend1.advance()
    joined1 = feed1.join(attend1)
    gx01, mats01, small01 = run_feed_back(
        z, core_id, [dx10, dx11], [(0, False, 4, 3), (1, False, 0, 4)], params,
        [x11, act1, slope1], None,
    )
    dx1_halo, joined1.value = tie(dx1_halo, joined1.value)
    joined1.advance()
    gx00, mats00, small00 = run_feed_back(
        z, core_id, [dx1_halo, dx10], [(0, False, 0, 3), (1, False, 0, 4)], params,
        [x10, act0, slope0], (mats01, small01),
    )
    feed0 = Reduction(mats00, 0)
    gx01, joined1.value = tie(gx01, joined1.value)
    joined1.advance()
    feed0.advance()
    dx01, rest01 = run_attend_back(
        z, core_id, [image_tokens], lower, params, [gx01, qkv1, probs1, mix1],
        jnp.zeros((small_rows, feats), f32), None, False,
    )
    gx00, feed0.value, joined1.value = tie(gx00, feed0.value, joined1.value)
    joined1.advance()
    feed0.advance()
    dq00, rest00 = run_attend_back(
        z, core_id, [image_tokens], upper, params, [gx00, qkv0, probs0, mix0], small00, rest01,
        True,
    )
    rest00, feed0.value, joined1.value = tie(rest00, feed0.value, joined1.value)
    joined1.advance()
    attend0 = Reduction(rest00, 0)
    dx00 = run_input(z, core_id, [image_tokens], upper, params, [gx00, dq00])
    attend0.advance()
    attend0.advance()
    joined = feed0.join(attend0)
    for _ in range(3):
        joined.advance()
    feed0, attend0 = joined.parted(feed0.value.shape[0])

    def exchanged(block0, block1):
        other = swap_cores(jnp.where(first, block1, block0))
        return jnp.where(first, jnp.stack([block0, other]), jnp.stack([other, block1]))[None]

    late_halo, _ = tie(y1_halo, rest00)
    final = jnp.concatenate([late_halo, y10, y11[:4]], 0)
    entry_grad = jnp.concatenate([dx1_halo, dx10, dx11[:4]], 0)
    block_outputs = exchanged(jnp.concatenate([y00, y01], 0), final)
    input_grads = exchanged(jnp.concatenate([dx00, dx01], 0), entry_grad)

    feed1, attend1 = joined1.parted_whole(hidden * 2)
    feed = jnp.where(first, feed0, feed1).astype(f32)
    rest = jnp.where(first, attend0, attend1).astype(f32)

    def blocks(item, at, number):
        return jnp.concatenate(
            [item[at + i * feats : at + (i + 1) * feats] for i in range(number)], 1
        )[None]

    sums = rest[4 * feats : 4 * feats + small_rows]
    flat = rest[4 * feats + small_rows :]
    cut = flat.shape[0]
    left = z.groups * cells - cut
    more = flat[:, z.lanes :]
    pair = jnp.concatenate(
        [flat[:, : z.lanes], jnp.concatenate([more[:left], more[left:]], 1)], 0
    )

    def line(at):
        return sums[at : at + 1]

    return (
        block_outputs,
        input_grads,
        line(s_gain1),
        line(s_shift1),
        blocks(rest, 0, 3),
        line(0),
        line(2),
        table_slope(pair, z, heads)[None],
        rest[3 * feats : 4 * feats][None],
        line(s_attend_b),
        line(s_gain2),
        line(s_shift2),
        blocks(feed, 0, hidden // feats),
        sums[s_widen_b : s_widen_b + hidden // feats].reshape(1, hidden),
        feed[hidden:][None],
        line(s_narrow_b),
    )


def solution(mesh):
    param_specs = [
        P("pipe", None),
        P("pipe", None),
        P("pipe", None, None),
        P("pipe", None),
        P("pipe", None),
        P("pipe", None, None),
        P("pipe", None, None),
        P("pipe", None),
        P("pipe", None),
        P("pipe", None),
        P("pipe", None, None),
        P("pipe", None),
        P("pipe", None, None),
        P("pipe", None),
    ]
    in_specs = (P(None, "rows", None, None),) * 2 + tuple(param_specs)
    out_specs = (P("pipe", None, "rows", None, None),) * 2 + tuple(param_specs)
    return jax.shard_map(
        on_device, mesh=mesh, in_specs=in_specs, out_specs=out_specs, check_vma=False
    )
```

```python
from functools import partial

import jax
import jax.numpy as jnp
import numpy as np
from jax import lax
from jax.experimental import pallas as pl
from jax.experimental.pallas import tpu as pltpu
from jax.sharding import PartitionSpec as P

f32 = jnp.float32
bf16 = jnp.bfloat16
epsilon = 1e-05
masked_score = -1e30
vmem_bytes = 60 * 1024 * 1024
cells = 56
tall = 64

gain1_row, shift1_row, query_bias_row, value_bias_row = 0, 1, 2, 4
attend_bias_row, gain2_row, shift2_row, narrow_bias_row, widen_bias_row = 5, 6, 7, 8, 9
s_gain1, s_shift1, s_attend_b, s_gain2, s_shift2, s_narrow_b, s_widen_b = 3, 4, 5, 6, 7, 8, 9
small_rows = 16


def mm(left, right):
    return lax.dot_general(left, right, (((1,), (0,)), ((), ())), preferred_element_type=f32)


def mm_t(left, right):
    return lax.dot_general(left, right, (((1,), (1,)), ((), ())), preferred_element_type=f32)


def t_mm(left, right):
    return lax.dot_general(left, right, (((0,), (0,)), ((), ())), preferred_element_type=f32)


def normed_parts(values):
    center = values - jnp.mean(values, -1, keepdims=True)
    spread = jnp.mean(center * center, -1, keepdims=True)
    scale = lax.rsqrt(spread + epsilon)
    return center * scale, scale


def norm_back(grad, hat, scale, gain):
    pulled = grad * gain
    return scale * (
        pulled
        - jnp.mean(pulled, -1, keepdims=True)
        - hat * jnp.mean(pulled * hat, -1, keepdims=True)
    )


def gelu_parts(value):
    below = 0.5 + 0.5 * lax.erf(value * 0.5**0.5)
    bell = jnp.exp(value * value * -0.5)
    return value * below, below + value * bell * (2.0 * np.pi) ** -0.5


def row_sum(values):
    return jnp.sum(values, 0, keepdims=True)


def head_masks(depth):
    place = lax.broadcasted_iota(jnp.int32, (1, 128), 1) // depth
    return [(place == h) for h in range(128 // depth)]


def spread_heads(part, masks):
    return jnp.concatenate([part * m.astype(bf16) for m in masks], 0)


def collect_heads(high, masks):
    rows = high.shape[0] // len(masks)
    out = high[:rows]
    for h in range(1, len(masks)):
        out = jnp.where(masks[h], high[h * rows : (h + 1) * rows], out)
    return out


def pad_rows(values, rows):
    return jnp.concatenate(
        [values, jnp.zeros((rows - values.shape[0], values.shape[1]), values.dtype)], 0
    )


def spread_matrix(cols, roll_by):
    place = lax.broadcasted_iota(jnp.int32, (cols // 7 * 8, cols), 0)
    column = lax.broadcasted_iota(jnp.int32, (cols // 7 * 8, cols), 1)
    w = place & 7
    target = (place >> 3) * 7 + w + roll_by
    target = jnp.where(target >= cols, target - cols, target)
    return jnp.where((target == column) & (w < 7), 1.0, 0.0).astype(bf16)


def image_to_windows(image, spread, out):
    for u in range(7):
        part = mm(spread, image[u])
        out[:, u * 8 : (u + 1) * 8, :] = part.reshape(-1, 8, part.shape[-1])


def windows_to_image(windows, spread, image, rim=None, first=0):
    wins, _, feats = windows.shape
    for u in range(7):
        part = windows[:, u * 8 : (u + 1) * 8, :].reshape(wins * 8, feats).astype(bf16)
        row = t_mm(spread, part).astype(bf16)
        image[u] = row
        if rim is not None and first <= u < first + 3:
            rim[u - first] = row


def by_rows(rows, parts, step):
    size = rows // parts

    def body(i, carry):
        step(i, pl.ds(pl.multiple_of(i * size, size), size))
        return carry

    lax.fori_loop(0, parts, body, 0)


class Copies:
    def __init__(self, core_ref, block, sems):
        self.core = core_ref[0]
        self.mine = self.core == block
        self.sems = sems
        self.count = 0
        self.writes = []

    def next(self):
        self.count += 1
        return self.sems.at[self.count - 1]

    def start(self, source, target):
        copy = pltpu.make_async_copy(source, target, self.next())
        copy.start()
        return copy

    def pick(self, pair, target):
        own, other = pair
        sem = self.next()

        @pl.when(self.mine)
        def _():
            pltpu.make_async_copy(own.at[0], target, sem).start()

        @pl.when(jnp.logical_not(self.mine))
        def _():
            pltpu.make_async_copy(other.at[0], target, sem).start()

        return pltpu.make_async_copy(own.at[0], target, sem)

    def rows(self, refs, plan, target):
        at = 0
        copies = []
        for which, batched, first, size in plan:
            source = refs[which].at[self.core] if batched else refs[which]
            copies.append(
                self.start(source.at[pl.ds(first, size)], target.at[pl.ds(at, size)])
            )
            at += size
        return copies

    def write(self, source, target):
        self.writes.append(self.start(source, target))

    def finish(self):
        for copy in self.writes:
            copy.wait()

    def small(self, own, other):
        return jnp.where(self.mine, own[...], other[...])


def wait_all(copies):
    for copy in copies:
        copy.wait()


def stage_norm(xs, gain, shift, n1):
    wins, _, feats = xs.shape

    def step(i, span):
        hat, _ = normed_parts(xs[pl.ds(i * 4, 4)].reshape(4 * cells, feats))
        n1[span, :] = (hat * gain + shift).astype(bf16)

    by_rows(wins * cells, wins // 4, step)


def stage_triple(n1, triple, small, qkv):
    wins, _, width = qkv.shape
    feats = width // 3
    qkv[:, cells:, :] = jnp.zeros((wins, tall - cells, width), bf16)
    offsets = (query_bias_row, None, value_bias_row)
    for j in range(3):
        lanes = slice(j * feats, (j + 1) * feats)
        part = mm(n1[...], triple[:, lanes])
        if offsets[j] is not None:
            part = part + small[offsets[j] : offsets[j] + 1]
        qkv[:, :cells, lanes] = part.reshape(wins, cells, feats).astype(bf16)


def stage_attend(qkv, bias, probs, mixed, depth, shifted):
    wins, _, width = qkv.shape
    feats = width // 3
    masks = head_masks(depth)
    scale = depth**-0.5

    def step(w, carry):
        kind = jnp.maximum(w - (wins - 3), 0) if shifted else 0
        for g in range(feats // 128):
            at = g * 128
            q = qkv[w, :, at : at + 128]
            k = qkv[w, :, feats + at : feats + at + 128]
            v = qkv[w, :, 2 * feats + at : 2 * feats + at + 128]
            scores = mm_t(k, spread_heads(q, masks))[:cells] * scale + bias[kind, g]
            powers = jnp.exp(scores - jnp.max(scores, 0, keepdims=True))
            weights = powers * (1.0 / jnp.sum(powers, 0, keepdims=True))
            low = pad_rows(weights, tall).astype(bf16)
            probs[w, g] = low
            mixed[w, :, at : at + 128] = collect_heads(t_mm(low, v), masks)[:cells]
        return carry

    lax.fori_loop(0, wins, step, 0, unroll=8)


def forward_stages(z, block, copies, c, small, bias_parts, picks, x_waits):
    rows, feats = c.x1.shape
    base, mask = bias_parts
    base = base[...].astype(f32)
    if block == 1:
        for kind in range(3):
            for g in range(z.groups):
                c.bias[kind, g] = base[g] + mask[kind]
    else:
        c.bias[0] = base
    wait_all(x_waits)
    image_to_windows(c.x_rows, c.spread, c.xs)
    stage_norm(c.xs, small[gain1_row : gain1_row + 1], small[shift1_row : shift1_row + 1], c.n1)
    picks[0].wait()
    stage_triple(c.n1, c.triple, small, c.qkv)
    yield
    stage_attend(c.qkv, c.bias, c.probs, c.mixed, z.depth, block == 1)
    c.low_mix[...] = c.mixed[...].reshape(rows, feats).astype(bf16)
    yield
    picks[1].wait()
    c.x1[...] = (
        c.xs[...].reshape(rows, feats)
        + mm(c.low_mix[...], c.attend[...])
        + small[attend_bias_row : attend_bias_row + 1]
    )
    yield
    second_norm(small, c)
    picks[2].wait()
    part = z.hidden // z.parts
    for j in range(z.parts):
        lanes = slice(j * part, (j + 1) * part)
        offset = jnp.concatenate(
            [
                small[widen_bias_row + i : widen_bias_row + i + 1]
                for i in range(j * part // feats, (j + 1) * part // feats)
            ],
            1,
        )
        value, pull = gelu_parts(mm(c.n2[...], c.widen[:, lanes]) + offset)
        c.act[:, lanes] = value.astype(bf16)
        c.slope[:, lanes] = pull.astype(bf16)
    yield
    picks[3].wait()
    c.total[...] = (
        c.x1[...]
        + mm(c.act[...], c.narrow[...])
        + small[narrow_bias_row : narrow_bias_row + 1]
    ).reshape(c.total.shape)


def second_norm(small, c):
    gain2 = small[gain2_row : gain2_row + 1]
    shift2 = small[shift2_row : shift2_row + 1]

    def norm_step(i, span):
        hat, _ = normed_parts(c.x1[span, :])
        c.n2[span, :] = (hat * gain2 + shift2).astype(bf16)

    by_rows(c.x1.shape[0], 4, norm_step)


def feed_back_stages(z, copies, c, small, waits, prev, o_mats, o_small):
    rows, feats = c.x1.shape
    w_dy, w_narrow, w_slope, w_widen, w_x1, w_act, w_prev = waits
    wait_all(w_dy)
    image_to_windows(c.dy_rows, c.spread, c.total)
    c.dy[...] = c.total[...].reshape(rows, feats).astype(bf16)
    sums = {s_narrow_b: row_sum(c.total[...].reshape(rows, feats))}
    part = z.hidden // z.parts
    wait_all(w_narrow + w_slope)
    for j in range(z.parts):
        lanes = slice(j * part, (j + 1) * part)
        grad = mm_t(c.dy[...], c.narrow[lanes, :]) * c.slope[:, lanes].astype(f32)
        total = row_sum(grad)
        for i in range(part // feats):
            sums[s_widen_b + j * part // feats + i] = total[:, i * feats : (i + 1) * feats]
        c.dh[:, lanes] = grad.astype(bf16)
    wait_all(w_widen + w_x1)
    if w_x1:
        second_norm(small, c)
    c.dn2[...] = mm_t(c.dh[...], c.widen[...])
    gain2 = small[gain2_row : gain2_row + 1]

    def norm_step(i, span):
        hat, scale = normed_parts(c.x1[span, :])
        grad = c.dn2[span, :]
        o_small[s_gain2 : s_gain2 + 1] += row_sum(grad * hat)
        o_small[s_shift2 : s_shift2 + 1] += row_sum(grad)
        c.gx1[span, :] = c.dy[span, :].astype(f32) + norm_back(grad, hat, scale, gain2)

    for at, value in sums.items():
        o_small[at : at + 1] += value
    by_rows(rows, 4, norm_step)
    yield
    wait_all(w_prev)

    def put(at, value):
        span = slice(at, at + feats)
        if prev is not None:
            value = value + prev[span, :].astype(f32)
        c.mats[span, :] = value.astype(bf16)

    for j in range(z.hidden // feats):
        put(j * feats, t_mm(c.n2[...], c.dh[:, j * feats : (j + 1) * feats]))
    half = c.mats.shape[0] // 2
    copies.write(c.mats.at[pl.ds(0, half)], o_mats.at[pl.ds(0, half)])
    wait_all(w_act)
    for j in range(z.hidden // feats):
        put(z.hidden + j * feats, t_mm(c.act[:, j * feats : (j + 1) * feats], c.dy[...]))
    copies.write(c.mats.at[pl.ds(half, half)], o_mats.at[pl.ds(half, half)])


def attend_back_stages(z, copies, c, small, waits, prev, o_rest, smalls):
    w_gx1, w_attend, w_mix, w_qkv, w_x, w_triple, w_prev = waits
    wins, _, feats = c.xs.shape
    rows = wins * cells
    depth = z.depth
    masks = head_masks(depth)
    scale = depth**-0.5
    mats = 4 * feats
    qkv, probs, gmix, gqkv, pair = c.qkv, c.probs, c.gmix, c.gqkv, c.pair
    wait_all(w_gx1)
    c.da[...] = c.gx1[...].astype(bf16)
    attend_b = row_sum(c.gx1[...])
    wait_all(w_attend)
    gmix[:, cells:, :] = jnp.zeros((wins, tall - cells, feats), bf16)
    gmix[:, :cells, :] = mm_t(c.da[...], c.attend[...]).reshape(wins, cells, feats).astype(bf16)
    pair[...] = jnp.zeros_like(pair)
    wait_all(w_qkv)

    def step(w, carry):
        for g in range(feats // 128):
            at = g * 128
            q = qkv[w, :, at : at + 128]
            k = qkv[w, :, feats + at : feats + at + 128]
            v = qkv[w, :, 2 * feats + at : 2 * feats + at + 128]
            wide = spread_heads(gmix[w, :, at : at + 128], masks)
            low = probs[w, g]
            high = low.astype(f32)[:cells]
            pulled = mm_t(v, wide)[:cells] * high
            ds = pulled - high * jnp.sum(pulled, 0, keepdims=True)
            pair[g] += ds
            ds = pad_rows(ds, tall).astype(bf16)
            gqkv[w, :, 2 * feats + at : 2 * feats + at + 128] = mm(low, wide)[:cells]
            gqkv[w, :, feats + at : feats + at + 128] = (
                mm(ds, spread_heads(q, masks))[:cells] * scale
            )
            gqkv[w, :, at : at + 128] = collect_heads(t_mm(ds, k), masks)[:cells] * scale
        return carry

    lax.fori_loop(0, wins, step, 0, unroll=8)
    gain1 = small[gain1_row : gain1_row + 1]
    shift1 = small[shift1_row : shift1_row + 1]
    if w_x:
        wait_all(w_x)
        image_to_windows(c.x_rows, c.spread, c.xs)

    def hat_step(i, span):
        hat, _ = normed_parts(c.xs[pl.ds(i * 4, 4)].reshape(4 * cells, feats))
        c.n1[span, :] = hat.astype(bf16)

    by_rows(rows, wins // 4, hat_step)
    wait_all(w_triple + w_mix + w_prev)

    def put(at, size, value):
        if prev is not None:
            value = value + prev[at : at + size, :].astype(f32)
        c.rest[at : at + size, :] = value.astype(bf16)

    put(3 * feats, feats, t_mm(c.low_mix[...], c.da[...]))
    columns = jnp.concatenate([gain1, shift1, jnp.zeros((6, feats), f32)], 0).T
    gain_column, shift_column = columns[:, 0:1], columns[:, 1:2]
    sums = []
    gain_grad = jnp.zeros((feats, 1), f32)
    shift_grad = jnp.zeros((8, feats), f32)
    for j in range(3):
        lanes = slice(j * feats, (j + 1) * feats)
        part = gqkv[:, :, lanes].reshape(rows, feats)
        total = row_sum(part)
        sums.append(total)
        c.dq[:, lanes] = part.astype(bf16)
        both = t_mm(c.n1[...], c.dq[:, lanes])
        put(j * feats, feats, gain_column * both + shift_column * total)
        gain_grad += jnp.sum(both * c.triple[:, lanes].astype(f32), -1, keepdims=True)
        top = total.astype(bf16)
        rest = (total - top.astype(f32)).astype(bf16)
        shift_grad += mm_t(
            jnp.concatenate([top.astype(f32), rest.astype(f32), jnp.zeros((6, feats), f32)], 0)
            .astype(bf16),
            c.triple[:, lanes],
        )
    sums.append(jnp.broadcast_to(gain_grad, (feats, 8)).T[0:1])
    sums.append(shift_grad[0:1] + shift_grad[1:2])
    sums.append(attend_b)
    put(
        mats,
        small_rows,
        smalls[...] + jnp.concatenate(sums + [jnp.zeros((small_rows - 6, feats), f32)], 0),
    )
    flat = pair[...].reshape(z.groups * cells, z.lanes)
    cut = flat.shape[0] * z.lanes // feats
    more = flat[cut:]
    put(
        mats + small_rows,
        cut,
        jnp.concatenate([flat[:cut], jnp.concatenate([more[:, :128], more[:, 128:]], 0)], 1),
    )
    end = mats + small_rows + cut
    c.rest[end:, :] = jnp.zeros((c.rest.shape[0] - end, feats), bf16)
    copies.write(c.rest, o_rest)


def input_stages(z, c, small):
    wins, _, feats = c.xs.shape
    gain1 = small[gain1_row : gain1_row + 1]
    c.dn2[...] = mm_t(c.dq[...], c.triple[...])

    def norm_step(i, span):
        wide = pl.ds(i * 4, 4)
        hat, scale = normed_parts(c.xs[wide].reshape(4 * cells, feats))
        out = c.gx1[span, :] + norm_back(c.dn2[span, :], hat, scale, gain1)
        c.xs[wide] = out.reshape(4, cells, feats)

    by_rows(wins * cells, wins // 4, norm_step)


class Refs:
    def __init__(self, refs, names):
        self.refs = list(refs)
        for name in names:
            setattr(self, name, self.refs.pop(0))

    def several(self, number):
        return [self.refs.pop(0) for _ in range(number)]

    def pairs(self, number):
        return [tuple(self.several(2)) for _ in range(number)]

    def name(self, names):
        for name in names:
            setattr(self, name, self.refs.pop(0))


def forward_kernel(z, n_x, x_plan, scratch, core_ref, *refs):
    c = Refs(refs, ())
    x_refs = c.several(n_x)
    c.name(("own", "other", "base"))
    big = c.pairs(4)
    c.name(("y", "rim", "o_qkv", "o_probs", "o_mix", "o_x1", "o_act", "o_slope"))
    c.name(scratch)
    copies = Copies(core_ref, 0, c.sems)
    x_waits = copies.rows(x_refs, x_plan, c.x_rows)
    picks = [copies.pick(p, to) for p, to in zip(big, (c.triple, c.attend, c.widen, c.narrow))]
    small = copies.small(c.own, c.other)
    c.spread = spread_matrix(z.cols, 0)
    stages = forward_stages(z, 0, copies, c, small, (c.base, None), picks, x_waits)
    next(stages)
    copies.write(c.qkv, c.o_qkv)
    next(stages)
    copies.write(c.probs, c.o_probs)
    copies.write(c.low_mix, c.o_mix)
    next(stages)
    copies.write(c.x1, c.o_x1)
    next(stages)
    copies.write(c.act, c.o_act)
    copies.write(c.slope, c.o_slope)
    for _ in stages:
        pass
    windows_to_image(c.total, c.spread, c.y, c.rim, 0)
    copies.finish()


def both_kernel(z, n_x, x_plan, n_dy, dy_plan, chained, scratch, core_ref, *refs):
    c = Refs(refs, ())
    x_refs = c.several(n_x)
    dy_refs = c.several(n_dy)
    c.name(("own", "other", "base", "mask"))
    big = c.pairs(4)
    prev = c.several(1) if chained else None
    c.name(("y", "y_rim", "dx", "dx_rim", "o_all"))
    c.o_mats = c.o_all.at[pl.ds(0, z.feed_rows)]
    c.o_rest = c.o_all.at[pl.ds(z.feed_rows, z.attend_rows)]
    c.name(scratch)
    copies = Copies(core_ref, 1, c.sems)
    x_waits = copies.rows(x_refs, x_plan, c.x_rows)
    picks = [copies.pick(p, to) for p, to in zip(big, (c.triple, c.attend, c.widen, c.narrow))]
    dy_waits = copies.rows(dy_refs, dy_plan, c.dy_rows)
    prev_waits = [[], []]
    if chained:
        parts = ((0, c.prev_mats), (z.feed_rows, c.prev_rest))
        prev_waits = [
            [copies.start(prev[0].at[pl.ds(at, to.shape[0])], to)] for at, to in parts
        ]
    prev_refs = (c.prev_mats, c.prev_rest) if chained else (None, None)
    small = copies.small(c.own, c.other)
    c.spread = spread_matrix(z.cols, 3)
    c.smalls[...] = jnp.zeros_like(c.smalls)
    for _ in forward_stages(z, 1, copies, c, small, (c.base, c.mask), picks, x_waits):
        pass
    windows_to_image(c.total, c.spread, c.y, c.y_rim, 4)
    waits = (dy_waits, [], [], [], [], [], prev_waits[0])
    for _ in feed_back_stages(z, copies, c, small, waits, prev_refs[0], c.o_mats, c.smalls):
        pass
    waits = ([], [], [], [], [], [], prev_waits[1])
    attend_back_stages(z, copies, c, small, waits, prev_refs[1], c.o_rest, c.smalls)
    input_stages(z, c, small)
    windows_to_image(c.xs, c.spread, c.dx, c.dx_rim, 4)
    copies.finish()


def feed_back_kernel(z, n_dy, dy_plan, chained, scratch, core_ref, *refs):
    c = Refs(refs, ())
    dy_refs = c.several(n_dy)
    c.name(("own", "other"))
    big = c.pairs(2)
    kept = c.several(3)
    prev = c.several(2) if chained else None
    c.name(("o_gx1", "o_mats", "o_small"))
    c.name(scratch)
    copies = Copies(core_ref, 0, c.sems)
    w_dy = copies.rows(dy_refs, dy_plan, c.dy_rows)
    w_narrow = copies.pick(big[1], c.narrow)
    w_slope = copies.start(kept[2], c.slope)
    w_widen = copies.pick(big[0], c.widen)
    w_x1 = copies.start(kept[0], c.x1)
    w_act = copies.start(kept[1], c.act)
    w_prev = [copies.start(prev[0], c.prev_mats)] if chained else []
    small = copies.small(c.own, c.other)
    c.spread = spread_matrix(z.cols, 0)
    c.o_small[...] = prev[1][...] if chained else jnp.zeros_like(c.o_small)
    waits = (w_dy, [w_narrow], [w_slope], [w_widen], [w_x1], [w_act], w_prev)
    stages = feed_back_stages(
        z, copies, c, small, waits, c.prev_mats if chained else None, c.o_mats, c.o_small
    )
    next(stages)
    copies.write(c.gx1, c.o_gx1)
    for _ in stages:
        pass
    copies.finish()


def attend_back_kernel(z, n_x, x_plan, chained, last, scratch, core_ref, *refs):
    c = Refs(refs, ())
    x_refs = c.several(n_x)
    c.name(("own", "other"))
    big = c.pairs(2)
    kept = c.several(4)
    c.name(("smalls",))
    prev = c.several(1) if chained else None
    c.name(("out", "o_rest"))
    c.name(scratch)
    copies = Copies(core_ref, 0, c.sems)
    w_gx1 = copies.start(kept[0], c.gx1)
    w_attend = copies.pick(big[1], c.attend)
    w_qkv = [copies.start(kept[1], c.qkv), copies.start(kept[2], c.probs)]
    w_x = copies.rows(x_refs, x_plan, c.x_rows)
    w_mix = copies.start(kept[3], c.low_mix)
    w_triple = copies.pick(big[0], c.triple)
    w_prev = [copies.start(prev[0], c.prev_rest)] if chained else []
    small = copies.small(c.own, c.other)
    c.spread = spread_matrix(z.cols, 0)
    waits = ([w_gx1], [w_attend], [w_mix], w_qkv, w_x, [w_triple], w_prev)
    attend_back_stages(
        z, copies, c, small, waits, c.prev_rest if chained else None, c.o_rest, c.smalls
    )
    if last:
        copies.write(c.dq, c.out)
    else:
        input_stages(z, c, small)
        windows_to_image(c.xs, c.spread, c.out)
    copies.finish()


def input_kernel(z, n_x, x_plan, scratch, core_ref, *refs):
    c = Refs(refs, ())
    x_refs = c.several(n_x)
    c.name(("own", "other"))
    big = c.pairs(1)
    kept = c.several(2)
    c.name(("out",))
    c.name(scratch)
    copies = Copies(core_ref, 0, c.sems)
    w_dq = copies.start(kept[1], c.dq)
    w_triple = copies.pick(big[0], c.triple)
    w_x = copies.rows(x_refs, x_plan, c.x_rows)
    w_gx1 = copies.start(kept[0], c.gx1)
    small = copies.small(c.own, c.other)
    c.spread = spread_matrix(z.cols, 0)
    wait_all(w_x)
    image_to_windows(c.x_rows, c.spread, c.xs)
    wait_all([w_dq, w_triple, w_gx1])
    input_stages(z, c, small)
    windows_to_image(c.xs, c.spread, c.out)
    copies.finish()


def unpack_kernel(z, scratch, core_ref, *refs):
    c = Refs(refs, ("value0", "value1", "arrived"))
    c.name(("triple", "attend", "widen", "narrow", "gain1", "shift1", "query_b", "value_b",
            "attend_b", "gain2", "shift2", "widen_b", "narrow_b", "pair"))
    c.name(scratch)
    copies = Copies(core_ref, 0, c.sems)
    feats, hidden = z.feats, z.hidden
    waits = [[], [], []]

    def fetch(stage, at, size, from0, from1):
        target = c.all_rows.at[pl.ds(at, size)]
        sem = copies.next()
        copy0, copy1 = (
            pltpu.make_async_copy(ref.at[pl.ds(row, size)], target, sem)
            for ref, row in (from0, from1)
        )
        pl.when(copies.mine)(copy0.start)
        pl.when(jnp.logical_not(copies.mine))(copy1.start)
        waits[stage].append(copy1)

    total = z.feed_rows + z.attend_rows
    quarters = (z.feed_rows // 8, z.attend_rows // 8)
    piece = sum(quarters)
    for half, source0 in enumerate((c.value0, c.arrived)):
        for which, quarter in enumerate(quarters):
            for i in range(4):
                at = which * z.feed_rows + (half * 4 + i) * quarter
                row0 = i * piece + which * quarters[0]
                cuts = [at, at + quarter]
                if at < total // 2 < at + quarter:
                    cuts.insert(1, total // 2)
                for low, high in zip(cuts, cuts[1:]):
                    if low < total // 2:
                        from1 = (c.arrived, low)
                    else:
                        from1 = (c.value1, low - total // 2)
                    stage = 2 if which else half
                    fetch(stage, low, high - low, (source0, row0 + low - at), from1)

    def rows(first, size):
        return c.all_rows[first : first + size, :].astype(f32)

    wait_all(waits[0])
    for j in range(hidden // feats):
        c.v_widen[:, j * feats : (j + 1) * feats] = rows(j * feats, feats)
    copies.write(c.v_widen, c.widen.at[0])
    wait_all(waits[1])
    c.v_narrow[...] = rows(hidden, hidden)
    copies.write(c.v_narrow, c.narrow.at[0])
    wait_all(waits[2])
    at = z.feed_rows
    for j in range(3):
        c.v_triple[:, j * feats : (j + 1) * feats] = rows(at + j * feats, feats)
    copies.write(c.v_triple, c.triple.at[0])
    c.v_attend[...] = rows(at + 3 * feats, feats)
    copies.write(c.v_attend, c.attend.at[0])
    at += 4 * feats
    smalls = rows(at, small_rows)
    for ref, row in ((c.query_b, 0), (c.value_b, 2), (c.gain1, s_gain1), (c.shift1, s_shift1),
                     (c.attend_b, s_attend_b), (c.gain2, s_gain2), (c.shift2, s_shift2),
                     (c.narrow_b, s_narrow_b)):
        ref[...] = smalls[row : row + 1]
    for j in range(hidden // feats):
        row = s_widen_b + j
        c.widen_b[:, j * feats : (j + 1) * feats] = smalls[row : row + 1]
    at += small_rows
    cut = z.groups * cells * z.lanes // feats
    flat = rows(at, cut)
    left = z.groups * cells - cut
    more = flat[:, z.lanes :]
    c.pair[...] = jnp.concatenate(
        [flat[:, : z.lanes], jnp.concatenate([more[:left], more[left:]], 1)], 0
    ).reshape(c.pair.shape)
    copies.finish()


class Sizes:
    def __init__(self, own_rows, cols, feats, hidden, heads):
        self.steps = own_rows // 7
        self.cols = cols
        self.feats = feats
        self.hidden = hidden
        self.wins = cols // 7
        self.rows = self.wins * cells
        self.depth = feats // heads
        self.groups = feats // 128
        self.lanes = 128 // self.depth * tall
        self.parts = 2
        self.feed_rows = 2 * hidden
        rows = self.feed_rows + 4 * feats + small_rows + self.groups * cells * self.lanes // feats
        self.attend_rows = -(-rows // 256) * 256 - self.feed_rows


def in_vmem(item):
    return pl.BlockSpec(item.shape, lambda i, c: (0,) * item.ndim)


hbm = pl.BlockSpec(memory_space=pl.ANY)


def shaped(shape, kind):
    return jax.ShapeDtypeStruct(shape, kind)


def scratch_table(z):
    feats, hidden, rows, wins = z.feats, z.hidden, z.rows, z.wins
    image = ((7, z.cols, feats), bf16)
    wide = ((wins, cells, feats), f32)
    low = ((rows, feats), bf16)
    high = ((rows, feats), f32)
    deep = ((rows, hidden), bf16)
    return {
        "triple": ((feats, 3 * feats), bf16),
        "attend": ((feats, feats), bf16),
        "widen": ((feats, hidden), bf16),
        "narrow": ((hidden, feats), bf16),
        "x_rows": image,
        "dy_rows": image,
        "xs": wide,
        "n1": low,
        "qkv": ((wins, tall, 3 * feats), bf16),
        "bias": ((3, z.groups, cells, z.lanes), f32),
        "probs": ((wins, z.groups, tall, z.lanes), bf16),
        "mixed": wide,
        "low_mix": low,
        "x1": high,
        "n2": low,
        "act": deep,
        "slope": deep,
        "total": wide,
        "dy": low,
        "dh": deep,
        "dn2": high,
        "gx1": high,
        "mats": ((z.feed_rows, feats), bf16),
        "prev_mats": ((z.feed_rows, feats), bf16),
        "smalls": ((small_rows, feats), f32),
        "da": low,
        "gmix": ((wins, tall, feats), bf16),
        "gqkv": ((wins, cells, 3 * feats), f32),
        "dq": ((rows, 3 * feats), bf16),
        "pair": ((z.groups, cells, z.lanes), f32),
        "rest": ((z.attend_rows, feats), bf16),
        "prev_rest": ((z.attend_rows, feats), bf16),
        "all_rows": ((z.feed_rows + z.attend_rows, feats), bf16),
        "v_triple": ((feats, 3 * feats), f32),
        "v_attend": ((feats, feats), f32),
        "v_widen": ((feats, hidden), f32),
        "v_narrow": ((hidden, feats), f32),
    }


def call(kernel, z, core, inputs, outputs, scratch, passes):
    inputs = [item if isinstance(item, tuple) else (item, hbm) for item in inputs]
    out_specs = [
        hbm if manual else pl.BlockSpec(shape, lambda i, c, n=len(shape): (0,) * n)
        for shape, _, manual in outputs
    ]
    table = scratch_table(z)
    return pl.pallas_call(
        partial(kernel, scratch + ("sems",)),
        grid_spec=pltpu.PrefetchScalarGridSpec(
            num_scalar_prefetch=1,
            grid=(1,),
            in_specs=[spec for _, spec in inputs],
            out_specs=out_specs,
            scratch_shapes=[pltpu.VMEM(*table[name]) for name in scratch]
            + [pltpu.SemaphoreType.DMA((24,))],
        ),
        out_shape=[shaped(shape, kind) for shape, kind, _ in outputs],
        compiler_params=pltpu.CompilerParams(
            dimension_semantics=("arbitrary",), vmem_limit_bytes=vmem_bytes
        ),
        cost_estimate=pl.CostEstimate(
            flops=int(passes * 20 * z.rows * z.feats * (4 * z.feats + 2 * z.hidden)),
            bytes_accessed=int(passes * 300_000_000),
            transcendentals=0,
        ),
    )(core, *(item for item, _ in inputs))


def resident(items):
    return [(item, in_vmem(item)) for item in items]


def flat_pairs(pairs):
    return [item for pair in pairs for item in pair]


forward_scratch = (
    "triple", "attend", "widen", "narrow", "x_rows", "xs", "n1", "qkv", "bias", "probs", "mixed",
    "low_mix", "x1", "n2", "act", "slope", "total",
)
back_scratch = ("dy_rows", "dy", "dh", "dn2", "gx1", "mats")
attend_back_scratch = ("da", "gmix", "gqkv", "dq", "pair", "rest")


def run_forward(z, core, xs, x_plan, params, base):
    inputs = list(xs) + resident(params["small"] + [base]) + flat_pairs(params["big"])
    table = scratch_table(z)
    rim = ((3, z.cols, z.feats), bf16, False)
    outputs = [(*table["x_rows"], False), rim] + [
        (*table[name], True) for name in ("qkv", "probs", "low_mix", "x1", "act", "slope")
    ]
    kernel = partial(bind, forward_kernel, (z, len(xs), x_plan))
    return call(kernel, z, core, inputs, outputs, forward_scratch, 1.2)


def bind(kernel, arguments, scratch, *refs):
    kernel(*arguments, scratch, *refs)


def run_both(z, core, xs, x_plan, dys, dy_plan, params, base, mask, prev):
    inputs = list(xs) + list(dys) + resident(params["small"] + [base, mask])
    inputs += flat_pairs(params["big"]) + ([] if prev is None else [prev])
    table = scratch_table(z)
    image = (*table["x_rows"], False)
    rim = ((3, z.cols, z.feats), bf16, False)
    outputs = [image, rim, image, rim]
    outputs.append(((z.feed_rows + z.attend_rows, z.feats), bf16, True))
    scratch = forward_scratch + back_scratch + attend_back_scratch + ("smalls",)
    if prev is not None:
        scratch += ("prev_mats", "prev_rest")
    arguments = (z, len(xs), x_plan, len(dys), dy_plan, prev is not None)
    return call(partial(bind, both_kernel, arguments), z, core, inputs, outputs, scratch, 4.0)


def run_feed_back(z, core, dys, dy_plan, params, kept, prev):
    inputs = list(dys) + resident(params["small"]) + flat_pairs(params["big"][2:]) + list(kept)
    if prev:
        inputs += [prev[0]] + resident(prev[1:])
    table = scratch_table(z)
    outputs = [(*table["gx1"], True), (*table["mats"], True), (*table["smalls"], False)]
    scratch = back_scratch + ("widen", "narrow", "x1", "n2", "act", "slope", "total")
    if prev:
        scratch += ("prev_mats",)
    arguments = (z, len(dys), dy_plan, bool(prev))
    return call(
        partial(bind, feed_back_kernel, arguments), z, core, inputs, outputs, scratch, 1.2
    )


def run_attend_back(z, core, xs, x_plan, params, kept, smalls, prev, last):
    inputs = list(xs) + resident(params["small"]) + flat_pairs(params["big"][:2]) + list(kept)
    inputs += resident([smalls])
    if prev is not None:
        inputs.append(prev)
    table = scratch_table(z)
    outputs = [
        (*table["dq"], True) if last else (*table["x_rows"], False),
        (*table["rest"], True),
    ]
    scratch = attend_back_scratch + (
        "triple", "attend", "x_rows", "xs", "n1", "qkv", "probs", "low_mix", "gx1", "dn2",
    )
    if prev is not None:
        scratch += ("prev_rest",)
    arguments = (z, len(xs), x_plan, prev is not None, last)
    return call(
        partial(bind, attend_back_kernel, arguments), z, core, inputs, outputs, scratch, 1.5
    )


def run_input(z, core, xs, x_plan, params, kept):
    inputs = list(xs) + resident(params["small"]) + flat_pairs(params["big"][:1]) + list(kept)
    scratch = ("triple", "x_rows", "xs", "gx1", "dq", "dn2")
    arguments = (z, len(xs), x_plan)
    outputs = [(*scratch_table(z)["x_rows"], False)]
    return call(partial(bind, input_kernel, arguments), z, core, inputs, outputs, scratch, 0.4)[0]


def run_unpack(z, core, value0, value1, arrived):
    feats, hidden = z.feats, z.hidden
    outputs = [
        ((1, feats, 3 * feats), f32, True),
        ((1, feats, feats), f32, True),
        ((1, feats, hidden), f32, True),
        ((1, hidden, feats), f32, True),
    ]
    outputs += [((1, feats), f32, False)] * 7
    outputs += [((1, hidden), f32, False), ((1, feats), f32, False)]
    outputs.append((*scratch_table(z)["pair"], False))
    scratch = ("all_rows", "v_triple", "v_attend", "v_widen", "v_narrow")
    kernel = partial(bind, unpack_kernel, (z,))
    return call(kernel, z, core, [value0, value1, arrived], outputs, scratch, 0.2)


def pair_index():
    place = np.arange(tall)
    u, w = place // 8, place % 8
    real = (u < 7) & (w < 7)
    index = (u[None, :] - u[:, None] + 6) * 13 + (w[None, :] - w[:, None] + 6)
    return np.where(real[:, None] & real[None, :], index, 169)[:cells]


def pair_onehot():
    return jnp.asarray(
        np.arange(169)[:, None] == pair_index().reshape(-1)[None, :], bf16
    )


def bias_base(table, z):
    spread = lax.dot_general(
        table, pair_onehot(), (((0,), (0,)), ((), ())), preferred_element_type=f32
    )
    spread = spread.reshape(z.groups, -1, cells, tall).transpose(0, 2, 1, 3)
    real = (np.arange(cells) % 8 < 7)[None, :, None, None]
    return (
        jnp.where(real, spread, masked_score).astype(bf16).reshape(z.groups, cells, z.lanes)
    )


def region_mask(z, step, first_row, total_rows):
    place = np.arange(tall)
    u, w = np.minimum(place // 8, 6), np.minimum(place % 8, 6)
    rows = jnp.mod(first_row + step * 7 + u + 3, total_rows)
    vertical = (rows >= total_rows - 7).astype(jnp.int32) + (rows >= total_rows - 3)
    kinds = []
    for column in (0, z.wins - 2, z.wins - 1):
        at = np.mod(column * 7 + w + 3, z.cols)
        horizontal = (at >= z.cols - 7).astype(np.int32) + (at >= z.cols - 3)
        code = vertical * 3 + horizontal
        alike = code[:cells, None] == code[None, :]
        kinds.append(jnp.where(alike, 0.0, masked_score).astype(f32))
    mask = jnp.stack(kinds)
    return jnp.tile(mask, (1, 1, z.lanes // tall))


def table_slope(pair, z, heads):
    pair = pair.reshape(z.groups, cells, -1, tall).transpose(1, 3, 0, 2).reshape(-1, heads)
    return mm(pair_onehot(), pair.astype(bf16))


def swap_cores(item):
    return lax.ppermute(item, "pipe", [(0, 1), (1, 0)])


def take(pair, index):
    return lax.dynamic_index_in_dim(pair, index, 0, keepdims=False)


def tie(item, *others):
    return lax.optimization_barrier((item,) + others)


class Reduction:
    near = 4

    def __init__(self, item=None, value=None):
        if value is None:
            core = lax.axis_index("pipe")
            pair = item.reshape((2, -1) + item.shape[1:])
            arrived = swap_cores(take(pair, 1 - core))
            value = (take(pair, core).astype(f32) + arrived.astype(f32)).astype(bf16)
        self.value = value

    def partners(self, near):
        count, place = lax.axis_size("rows"), lax.axis_index("rows")
        size, unit = (self.near, 1) if near else (count // self.near, self.near)
        mine = (place // unit) % size
        return size, mine, [[(i, i ^ (d * unit)) for i in range(count)] for d in range(1, size)]

    def scatter(self, near):
        size, mine, routes = self.partners(near)
        parts = self.value.reshape((size, -1) + self.value.shape[1:])
        arrived = [
            lax.ppermute(take(parts, mine ^ d), "rows", route)
            for d, route in enumerate(routes, 1)
        ]
        total = take(parts, mine).astype(f32)
        for item in arrived:
            total = total + item.astype(f32)
        self.value = total.astype(bf16)

    def gather(self, near):
        size, mine, routes = self.partners(near)
        arrived = [lax.ppermute(self.value, "rows", route) for route in routes]
        parts = jnp.zeros((size,) + self.value.shape, bf16)
        for d, item in enumerate([self.value] + arrived):
            parts = lax.dynamic_update_index_in_dim(parts, item, mine ^ d, 0)
        self.value = parts.reshape((-1,) + self.value.shape[1:])

    def join(self, other):
        return Reduction(value=jnp.concatenate([self.value, other.value], 0))


def on_device(
    image_tokens,
    out_grad,
    first_gain,
    first_shift,
    triple_weight,
    query_bias,
    value_bias,
    bias_table,
    attend_weight,
    attend_bias,
    second_gain,
    second_shift,
    widen_weight,
    widen_bias,
    narrow_weight,
    narrow_bias,
):
    core = lax.axis_index("pipe")
    core_id = core.astype(jnp.int32).reshape(1)
    count = lax.axis_size("rows")
    place = lax.axis_index("rows")
    batches, own_rows, cols, feats = image_tokens.shape
    heads = bias_table.shape[2]
    hidden = widen_weight.shape[2]
    z = Sizes(own_rows, cols, feats, hidden, heads)
    total_rows = own_rows * count
    first_row = place * own_rows

    small = jnp.concatenate(
        [
            first_gain,
            first_shift,
            query_bias,
            jnp.zeros_like(query_bias),
            value_bias,
            attend_bias,
            second_gain,
            second_shift,
            narrow_bias,
            widen_bias.reshape(-1, feats),
            jnp.zeros((small_rows - 9 - hidden // feats, feats), bf16),
        ],
        0,
    ).astype(f32)
    tables = [bias_table[0], swap_cores(bias_table[0])]
    first = core == 0
    big = (triple_weight, attend_weight, widen_weight, narrow_weight)
    params = {
        "small": [small, swap_cores(small)],
        "big": [(item, swap_cores(item)) for item in big],
    }
    to_previous = [((i + 1) % count, i) for i in range(count)]
    to_next = [(i, (i + 1) % count) for i in range(count)]
    base0 = bias_base(jnp.where(first, tables[0], tables[1]), z)

    upper = [(0, True, 0, 7)]
    lower = [(0, True, 7, 7)]

    y00, y0_rim, *kept0 = run_forward(z, core_id, [image_tokens], upper, params, base0)
    y0_halo = lax.ppermute(y0_rim, "rows", to_previous)
    late_grad, late_row, late_table, _ = tie(
        out_grad, first_row, jnp.where(first, tables[1], tables[0]), y00
    )
    grad_halo = lax.ppermute(take(late_grad, core)[:3], "rows", to_previous)
    masks = [region_mask(z, step, late_row, total_rows) for step in range(2)]
    base1 = bias_base(late_table, z)
    y01, _, *kept1 = run_forward(z, core_id, [image_tokens], lower, params, base0)
    (qkv0, probs0, mix0, x10, act0, slope0) = kept0
    (qkv1, probs1, mix1, x11, act1, slope1) = kept1

    y10, _, dx10, _, all10 = run_both(
        z, core_id, [y00, y01], [(0, False, 3, 4), (1, False, 0, 3)], [out_grad],
        [(0, True, 3, 7)], params, base1, masks[0], None,
    )
    y11, y1_rim, dx11, dx1_rim, all11 = run_both(
        z, core_id, [y01, y0_halo], [(0, False, 3, 4), (1, False, 0, 3)],
        [out_grad, grad_halo], [(0, True, 10, 4), (1, False, 0, 3)], params, base1, masks[1],
        all10,
    )
    dx1_halo, y1_halo = jnp.split(
        lax.ppermute(jnp.concatenate([dx1_rim, y1_rim], 0), "rows", to_next), 2
    )

    def sent(block0, block1):
        return swap_cores(jnp.where(first, block1, block0))

    def arranged(block0, block1, other):
        return jnp.where(first, jnp.stack([block0, other]), jnp.stack([other, block1]))[None]

    reduction1 = Reduction(all11)

    gx01, mats01, small01 = run_feed_back(
        z, core_id, [dx10, dx11], [(0, False, 4, 3), (1, False, 0, 4)], params,
        [x11, act1, slope1], None,
    )
    dx1_halo, reduction1.value = tie(dx1_halo, reduction1.value)
    reduction1.scatter(True)
    gx00, mats00, small00 = run_feed_back(
        z, core_id, [dx1_halo, dx10], [(0, False, 0, 3), (1, False, 0, 4)], params,
        [x10, act0, slope0], (mats01, small01),
    )
    gx01, reduction1.value = tie(gx01, reduction1.value)
    reduction1.scatter(False)
    feed0 = Reduction(mats00)
    dx01, rest01 = run_attend_back(
        z, core_id, [image_tokens], lower, params, [gx01, qkv1, probs1, mix1],
        jnp.zeros((small_rows, feats), f32), None, False,
    )
    gx00, reduction1.value, feed0.value = tie(gx00, reduction1.value, feed0.value)
    reduction1.gather(False)
    feed0.scatter(True)
    dq00, rest00 = run_attend_back(
        z, core_id, [image_tokens], upper, params, [gx00, qkv0, probs0, mix0], small00, rest01,
        True,
    )
    rest00, reduction1.value, feed0.value = tie(rest00, reduction1.value, feed0.value)
    reduction1.gather(True)
    rest0 = Reduction(rest00)
    dx00 = run_input(z, core_id, [image_tokens], upper, params, [gx00, dq00])
    entry_grad = jnp.concatenate([dx1_halo, dx10, dx11[:4]], 0)
    hidden_out = jnp.concatenate([y00, y01], 0)
    final = jnp.concatenate([y1_halo, y10, y11[:4]], 0)
    rest0.value, hidden_out, final = tie(rest0.value, hidden_out, final)
    other_out = sent(hidden_out, final)
    image_grad = jnp.concatenate([dx00, dx01], 0)
    block_outputs = arranged(hidden_out, final, other_out)
    input_grads = arranged(image_grad, entry_grad, sent(image_grad, entry_grad))

    rest0.scatter(True)
    rest0.value, block_outputs, input_grads = tie(rest0.value, block_outputs, input_grads)
    reduction = feed0.join(rest0)
    reduction.scatter(False)
    reduction.gather(False)
    reduction.gather(True)

    arrived = swap_cores(jnp.where(first, reduction1.value, reduction.value))
    (t_triple, t_attend, t_widen, t_narrow, t_gain1, t_shift1, t_query_b, t_value_b,
     t_attend_b, t_gain2, t_shift2, t_widen_b, t_narrow_b, pair) = run_unpack(
        z, core_id, reduction.value, reduction1.value, arrived
    )

    return (
        block_outputs,
        input_grads,
        t_gain1,
        t_shift1,
        t_triple,
        t_query_b,
        t_value_b,
        table_slope(pair, z, heads)[None],
        t_attend,
        t_attend_b,
        t_gain2,
        t_shift2,
        t_widen,
        t_widen_b,
        t_narrow,
        t_narrow_b,
    )


def solution(mesh):
    param_specs = [
        P("pipe", None),
        P("pipe", None),
        P("pipe", None, None),
        P("pipe", None),
        P("pipe", None),
        P("pipe", None, None),
        P("pipe", None, None),
        P("pipe", None),
        P("pipe", None),
        P("pipe", None),
        P("pipe", None, None),
        P("pipe", None),
        P("pipe", None, None),
        P("pipe", None),
    ]
    in_specs = (P(None, "rows", None, None),) * 2 + tuple(param_specs)
    out_specs = (P("pipe", None, "rows", None, None),) * 2 + tuple(param_specs)
    return jax.shard_map(
        on_device, mesh=mesh, in_specs=in_specs, out_specs=out_specs, check_vma=False
    )
```

```python
from functools import partial

import jax
import jax.numpy as jnp
import numpy as np
from jax import lax
from jax.experimental import pallas as pl
from jax.experimental.pallas import tpu as pltpu
from jax.sharding import PartitionSpec as P

f32 = jnp.float32
bf16 = jnp.bfloat16
epsilon = 1e-05
masked_score = -1e30
vmem_bytes = 60 * 1024 * 1024
cells = 56
tall = 64

gain1_row, shift1_row, query_bias_row, value_bias_row = 0, 1, 2, 4
attend_bias_row, gain2_row, shift2_row, narrow_bias_row, widen_bias_row = 5, 6, 7, 8, 9
s_gain1, s_shift1, s_attend_b, s_gain2, s_shift2, s_narrow_b, s_widen_b = 3, 4, 5, 6, 7, 8, 9
small_rows = 16


def mm(left, right):
    return lax.dot_general(left, right, (((1,), (0,)), ((), ())), preferred_element_type=f32)


def mm_t(left, right):
    return lax.dot_general(left, right, (((1,), (1,)), ((), ())), preferred_element_type=f32)


def t_mm(left, right):
    return lax.dot_general(left, right, (((0,), (0,)), ((), ())), preferred_element_type=f32)


def normed_parts(values):
    center = values - jnp.mean(values, -1, keepdims=True)
    spread = jnp.mean(center * center, -1, keepdims=True)
    scale = lax.rsqrt(spread + epsilon)
    return center * scale, scale


def norm_back(grad, hat, scale, gain):
    pulled = grad * gain
    return scale * (
        pulled
        - jnp.mean(pulled, -1, keepdims=True)
        - hat * jnp.mean(pulled * hat, -1, keepdims=True)
    )


def gelu_parts(value):
    below = 0.5 + 0.5 * lax.erf(value * 0.5**0.5)
    bell = jnp.exp(value * value * -0.5)
    return value * below, below + value * bell * (2.0 * np.pi) ** -0.5


def row_sum(values):
    return jnp.sum(values, 0, keepdims=True)


def head_masks(depth):
    place = lax.broadcasted_iota(jnp.int32, (1, 128), 1) // depth
    return [(place == h) for h in range(128 // depth)]


def spread_heads(part, masks):
    return jnp.concatenate([part * m.astype(bf16) for m in masks], 0)


def collect_heads(high, masks):
    rows = high.shape[0] // len(masks)
    out = high[:rows]
    for h in range(1, len(masks)):
        out = jnp.where(masks[h], high[h * rows : (h + 1) * rows], out)
    return out


def pad_rows(values, rows):
    return jnp.concatenate(
        [values, jnp.zeros((rows - values.shape[0], values.shape[1]), values.dtype)], 0
    )


def spread_matrix(cols, roll_by):
    place = lax.broadcasted_iota(jnp.int32, (cols // 7 * 8, cols), 0)
    column = lax.broadcasted_iota(jnp.int32, (cols // 7 * 8, cols), 1)
    w = place & 7
    target = (place >> 3) * 7 + w + roll_by
    target = jnp.where(target >= cols, target - cols, target)
    return jnp.where((target == column) & (w < 7), 1.0, 0.0).astype(bf16)


def image_to_windows(image, spread, out):
    for u in range(7):
        part = mm(spread, image[u])
        out[:, u * 8 : (u + 1) * 8, :] = part.reshape(-1, 8, part.shape[-1])


def windows_to_image(windows, spread, image, rim=None, first=0):
    wins, _, feats = windows.shape
    for u in range(7):
        part = windows[:, u * 8 : (u + 1) * 8, :].reshape(wins * 8, feats).astype(bf16)
        row = t_mm(spread, part).astype(bf16)
        image[u] = row
        if rim is not None and first <= u < first + 3:
            rim[u - first] = row


def by_rows(rows, parts, step):
    size = rows // parts

    def body(i, carry):
        step(i, pl.ds(pl.multiple_of(i * size, size), size))
        return carry

    lax.fori_loop(0, parts, body, 0)


class Copies:
    def __init__(self, core_ref, block, sems):
        self.core = core_ref[0]
        self.mine = self.core == block
        self.sems = sems
        self.count = 0
        self.writes = []

    def next(self):
        self.count += 1
        return self.sems.at[self.count - 1]

    def start(self, source, target):
        copy = pltpu.make_async_copy(source, target, self.next())
        copy.start()
        return copy

    def pick(self, pair, target):
        own, other = pair
        sem = self.next()

        @pl.when(self.mine)
        def _():
            pltpu.make_async_copy(own.at[0], target, sem).start()

        @pl.when(jnp.logical_not(self.mine))
        def _():
            pltpu.make_async_copy(other.at[0], target, sem).start()

        return pltpu.make_async_copy(own.at[0], target, sem)

    def rows(self, refs, plan, target):
        at = 0
        copies = []
        for which, batched, first, size in plan:
            source = refs[which].at[self.core] if batched else refs[which]
            copies.append(
                self.start(source.at[pl.ds(first, size)], target.at[pl.ds(at, size)])
            )
            at += size
        return copies

    def write(self, source, target):
        self.writes.append(self.start(source, target))

    def write_rows(self, source, at, outs):
        size = source.shape[0]
        if len(outs) == 1:
            self.write(source, outs[0].at[pl.ds(at, size)])
            return
        half = outs[0].shape[0]
        low = at
        while low < at + size:
            which = low // half
            high = min(at + size, (which + 1) * half)
            part = source.at[pl.ds(low - at, high - low)]
            keep, send = (out.at[pl.ds(low - which * half, high - low)] for out in outs)
            sem = self.next()
            pl.when(self.core == which)(pltpu.make_async_copy(part, keep, sem).start)
            pl.when(self.core != which)(pltpu.make_async_copy(part, send, sem).start)
            self.writes.append(pltpu.make_async_copy(part, keep, sem))
            low = high

    def finish(self):
        for copy in self.writes:
            copy.wait()

    def small(self, own, other):
        return jnp.where(self.mine, own[...], other[...])


def wait_all(copies):
    for copy in copies:
        copy.wait()


def stage_norm(xs, gain, shift, n1):
    wins, _, feats = xs.shape

    def step(i, span):
        hat, _ = normed_parts(xs[pl.ds(i * 4, 4)].reshape(4 * cells, feats))
        n1[span, :] = (hat * gain + shift).astype(bf16)

    by_rows(wins * cells, wins // 4, step)


def stage_triple(n1, triple, small, qkv):
    wins, _, width = qkv.shape
    feats = width // 3
    qkv[:, cells:, :] = jnp.zeros((wins, tall - cells, width), bf16)
    offsets = (query_bias_row, None, value_bias_row)
    for j in range(3):
        lanes = slice(j * feats, (j + 1) * feats)
        part = mm(n1[...], triple[:, lanes])
        if offsets[j] is not None:
            part = part + small[offsets[j] : offsets[j] + 1]
        qkv[:, :cells, lanes] = part.reshape(wins, cells, feats).astype(bf16)


def stage_attend(qkv, bias, probs, mixed, depth, shifted):
    wins, _, width = qkv.shape
    feats = width // 3
    masks = head_masks(depth)
    scale = depth**-0.5

    def step(w, carry):
        kind = jnp.maximum(w - (wins - 3), 0) if shifted else 0
        for g in range(feats // 128):
            at = g * 128
            q = qkv[w, :, at : at + 128]
            k = qkv[w, :, feats + at : feats + at + 128]
            v = qkv[w, :, 2 * feats + at : 2 * feats + at + 128]
            scores = mm_t(k, spread_heads(q, masks))[:cells] * scale + bias[kind, g]
            powers = jnp.exp(scores - jnp.max(scores, 0, keepdims=True))
            weights = powers * (1.0 / jnp.sum(powers, 0, keepdims=True))
            low = pad_rows(weights, tall).astype(bf16)
            probs[w, g] = low
            mixed[w, :, at : at + 128] = collect_heads(t_mm(low, v), masks)[:cells]
        return carry

    lax.fori_loop(0, wins, step, 0, unroll=16)


def forward_stages(z, block, copies, c, small, bias_parts, picks, x_waits):
    rows, feats = c.x1.shape
    base, mask = bias_parts
    base = base[...].astype(f32)
    if block == 1:
        for kind in range(3):
            for g in range(z.groups):
                c.bias[kind, g] = base[g] + mask[kind]
    else:
        c.bias[0] = base
    wait_all(x_waits)
    image_to_windows(c.x_rows, c.spread, c.xs)
    stage_norm(c.xs, small[gain1_row : gain1_row + 1], small[shift1_row : shift1_row + 1], c.n1)
    picks[0].wait()
    stage_triple(c.n1, c.triple, small, c.qkv)
    yield
    stage_attend(c.qkv, c.bias, c.probs, c.mixed, z.depth, block == 1)
    c.low_mix[...] = c.mixed[...].reshape(rows, feats).astype(bf16)
    yield
    picks[1].wait()
    c.x1[...] = (
        c.xs[...].reshape(rows, feats)
        + mm(c.low_mix[...], c.attend[...])
        + small[attend_bias_row : attend_bias_row + 1]
    )
    yield
    second_norm(small, c)
    picks[2].wait()
    part = z.hidden // z.parts
    for j in range(z.parts):
        lanes = slice(j * part, (j + 1) * part)
        offset = jnp.concatenate(
            [
                small[widen_bias_row + i : widen_bias_row + i + 1]
                for i in range(j * part // feats, (j + 1) * part // feats)
            ],
            1,
        )
        value, pull = gelu_parts(mm(c.n2[...], c.widen[:, lanes]) + offset)
        c.act[:, lanes] = value.astype(bf16)
        c.slope[:, lanes] = pull.astype(bf16)
    yield
    picks[3].wait()
    c.total[...] = (
        c.x1[...]
        + mm(c.act[...], c.narrow[...])
        + small[narrow_bias_row : narrow_bias_row + 1]
    ).reshape(c.total.shape)


def second_norm(small, c):
    gain2 = small[gain2_row : gain2_row + 1]
    shift2 = small[shift2_row : shift2_row + 1]

    def norm_step(i, span):
        hat, _ = normed_parts(c.x1[span, :])
        c.n2[span, :] = (hat * gain2 + shift2).astype(bf16)

    by_rows(c.x1.shape[0], 4, norm_step)


def feed_back_stages(z, copies, c, small, waits, prev, outs, o_small):
    rows, feats = c.x1.shape
    w_dy, w_narrow, w_slope, w_widen, w_x1, w_act, w_prev = waits
    wait_all(w_dy)
    image_to_windows(c.dy_rows, c.spread, c.total)
    c.dy[...] = c.total[...].reshape(rows, feats).astype(bf16)
    sums = {s_narrow_b: row_sum(c.total[...].reshape(rows, feats))}
    part = z.hidden // z.parts
    wait_all(w_narrow + w_slope)
    for j in range(z.parts):
        lanes = slice(j * part, (j + 1) * part)
        grad = mm_t(c.dy[...], c.narrow[lanes, :]) * c.slope[:, lanes].astype(f32)
        total = row_sum(grad)
        for i in range(part // feats):
            sums[s_widen_b + j * part // feats + i] = total[:, i * feats : (i + 1) * feats]
        c.dh[:, lanes] = grad.astype(bf16)
    wait_all(w_widen + w_x1)
    if w_x1:
        second_norm(small, c)
    c.dn2[...] = mm_t(c.dh[...], c.widen[...])
    gain2 = small[gain2_row : gain2_row + 1]

    def norm_step(i, span):
        hat, scale = normed_parts(c.x1[span, :])
        grad = c.dn2[span, :]
        o_small[s_gain2 : s_gain2 + 1] += row_sum(grad * hat)
        o_small[s_shift2 : s_shift2 + 1] += row_sum(grad)
        c.gx1[span, :] = c.dy[span, :].astype(f32) + norm_back(grad, hat, scale, gain2)

    for at, value in sums.items():
        o_small[at : at + 1] += value
    by_rows(rows, 4, norm_step)
    yield
    wait_all(w_prev)

    def put(at, value):
        span = slice(at, at + feats)
        if prev is not None:
            value = value + prev[span, :].astype(f32)
        c.mats[span, :] = value.astype(bf16)

    for j in range(z.hidden // feats):
        put(j * feats, t_mm(c.n2[...], c.dh[:, j * feats : (j + 1) * feats]))
    half = c.mats.shape[0] // 2
    copies.write_rows(c.mats.at[pl.ds(0, half)], 0, outs)
    wait_all(w_act)
    for j in range(z.hidden // feats):
        put(z.hidden + j * feats, t_mm(c.act[:, j * feats : (j + 1) * feats], c.dy[...]))
    copies.write_rows(c.mats.at[pl.ds(half, half)], half, outs)


def attend_back_stages(z, copies, c, small, waits, prev, outs, first_row, smalls):
    w_gx1, w_attend, w_mix, w_qkv, w_x, w_triple, w_prev = waits
    wins, _, feats = c.xs.shape
    rows = wins * cells
    depth = z.depth
    masks = head_masks(depth)
    scale = depth**-0.5
    mats = 4 * feats
    qkv, probs, gmix, gqkv, pair = c.qkv, c.probs, c.gmix, c.gqkv, c.pair
    wait_all(w_gx1)
    c.da[...] = c.gx1[...].astype(bf16)
    attend_b = row_sum(c.gx1[...])
    wait_all(w_attend)
    gmix[:, cells:, :] = jnp.zeros((wins, tall - cells, feats), bf16)
    gmix[:, :cells, :] = mm_t(c.da[...], c.attend[...]).reshape(wins, cells, feats).astype(bf16)
    pair[...] = jnp.zeros_like(pair)
    wait_all(w_qkv)

    def step(w, carry):
        for g in range(feats // 128):
            at = g * 128
            q = qkv[w, :, at : at + 128]
            k = qkv[w, :, feats + at : feats + at + 128]
            v = qkv[w, :, 2 * feats + at : 2 * feats + at + 128]
            wide = spread_heads(gmix[w, :, at : at + 128], masks)
            low = probs[w, g]
            high = low.astype(f32)[:cells]
            pulled = mm_t(v, wide)[:cells] * high
            ds = pulled - high * jnp.sum(pulled, 0, keepdims=True)
            pair[g] += ds
            ds = pad_rows(ds, tall).astype(bf16)
            gqkv[w, :, 2 * feats + at : 2 * feats + at + 128] = mm(low, wide)[:cells]
            gqkv[w, :, feats + at : feats + at + 128] = (
                mm(ds, spread_heads(q, masks))[:cells] * scale
            )
            gqkv[w, :, at : at + 128] = collect_heads(t_mm(ds, k), masks)[:cells] * scale
        return carry

    lax.fori_loop(0, wins, step, 0, unroll=16)
    gain1 = small[gain1_row : gain1_row + 1]
    shift1 = small[shift1_row : shift1_row + 1]
    if w_x:
        wait_all(w_x)
        image_to_windows(c.x_rows, c.spread, c.xs)

    def hat_step(i, span):
        hat, _ = normed_parts(c.xs[pl.ds(i * 4, 4)].reshape(4 * cells, feats))
        c.n1[span, :] = hat.astype(bf16)

    by_rows(rows, wins // 4, hat_step)
    wait_all(w_triple + w_mix + w_prev)

    def put(at, size, value):
        if prev is not None:
            value = value + prev[at : at + size, :].astype(f32)
        c.rest[at : at + size, :] = value.astype(bf16)

    put(3 * feats, feats, t_mm(c.low_mix[...], c.da[...]))
    columns = jnp.concatenate([gain1, shift1, jnp.zeros((6, feats), f32)], 0).T
    gain_column, shift_column = columns[:, 0:1], columns[:, 1:2]
    sums = []
    gain_grad = jnp.zeros((feats, 1), f32)
    shift_grad = jnp.zeros((8, feats), f32)
    for j in range(3):
        lanes = slice(j * feats, (j + 1) * feats)
        part = gqkv[:, :, lanes].reshape(rows, feats)
        total = row_sum(part)
        sums.append(total)
        c.dq[:, lanes] = part.astype(bf16)
        both = t_mm(c.n1[...], c.dq[:, lanes])
        put(j * feats, feats, gain_column * both + shift_column * total)
        gain_grad += jnp.sum(both * c.triple[:, lanes].astype(f32), -1, keepdims=True)
        top = total.astype(bf16)
        rest = (total - top.astype(f32)).astype(bf16)
        shift_grad += mm_t(
            jnp.concatenate([top.astype(f32), rest.astype(f32), jnp.zeros((6, feats), f32)], 0)
            .astype(bf16),
            c.triple[:, lanes],
        )
    sums.append(jnp.broadcast_to(gain_grad, (feats, 8)).T[0:1])
    sums.append(shift_grad[0:1] + shift_grad[1:2])
    sums.append(attend_b)
    put(
        mats,
        small_rows,
        smalls[...] + jnp.concatenate(sums + [jnp.zeros((small_rows - 6, feats), f32)], 0),
    )
    flat = pair[...].reshape(z.groups * cells, z.lanes)
    cut = flat.shape[0] * z.lanes // feats
    more = flat[cut:]
    put(
        mats + small_rows,
        cut,
        jnp.concatenate([flat[:cut], jnp.concatenate([more[:, :128], more[:, 128:]], 0)], 1),
    )
    end = mats + small_rows + cut
    c.rest[end:, :] = jnp.zeros((c.rest.shape[0] - end, feats), bf16)
    copies.write_rows(c.rest, first_row, outs)


def input_stages(z, c, small):
    wins, _, feats = c.xs.shape
    gain1 = small[gain1_row : gain1_row + 1]
    c.dn2[...] = mm_t(c.dq[...], c.triple[...])

    def norm_step(i, span):
        wide = pl.ds(i * 4, 4)
        hat, scale = normed_parts(c.xs[wide].reshape(4 * cells, feats))
        out = c.gx1[span, :] + norm_back(c.dn2[span, :], hat, scale, gain1)
        c.xs[wide] = out.reshape(4, cells, feats)

    by_rows(wins * cells, wins // 4, norm_step)


class Refs:
    def __init__(self, refs, names):
        self.refs = list(refs)
        for name in names:
            setattr(self, name, self.refs.pop(0))

    def several(self, number):
        return [self.refs.pop(0) for _ in range(number)]

    def pairs(self, number):
        return [tuple(self.several(2)) for _ in range(number)]

    def name(self, names):
        for name in names:
            setattr(self, name, self.refs.pop(0))


def forward_kernel(z, n_x, x_plan, scratch, core_ref, *refs):
    c = Refs(refs, ())
    x_refs = c.several(n_x)
    c.name(("own", "other", "base"))
    big = c.pairs(4)
    c.name(("y", "rim", "o_qkv", "o_probs", "o_mix", "o_x1", "o_act", "o_slope"))
    c.name(scratch)
    copies = Copies(core_ref, 0, c.sems)
    x_waits = copies.rows(x_refs, x_plan, c.x_rows)
    picks = [copies.pick(p, to) for p, to in zip(big, (c.triple, c.attend, c.widen, c.narrow))]
    small = copies.small(c.own, c.other)
    c.spread = spread_matrix(z.cols, 0)
    stages = forward_stages(z, 0, copies, c, small, (c.base, None), picks, x_waits)
    next(stages)
    copies.write(c.qkv, c.o_qkv)
    next(stages)
    copies.write(c.probs, c.o_probs)
    copies.write(c.low_mix, c.o_mix)
    next(stages)
    copies.write(c.x1, c.o_x1)
    next(stages)
    copies.write(c.act, c.o_act)
    copies.write(c.slope, c.o_slope)
    for _ in stages:
        pass
    windows_to_image(c.total, c.spread, c.y, c.rim, 0)
    copies.finish()


def both_kernel(z, n_x, x_plan, n_dy, dy_plan, chained, scratch, core_ref, *refs):
    c = Refs(refs, ())
    x_refs = c.several(n_x)
    dy_refs = c.several(n_dy)
    c.name(("own", "other", "base", "mask"))
    big = c.pairs(4)
    prev = c.several(1) if chained else None
    c.name(("y", "dx", "rim"))
    outs = c.several(2 if chained else 1)
    c.name(scratch)
    copies = Copies(core_ref, 1, c.sems)
    x_waits = copies.rows(x_refs, x_plan, c.x_rows)
    picks = [copies.pick(p, to) for p, to in zip(big, (c.triple, c.attend, c.widen, c.narrow))]
    dy_waits = copies.rows(dy_refs, dy_plan, c.dy_rows)
    prev_waits = [[], []]
    if chained:
        parts = ((0, c.prev_mats), (z.feed_rows, c.prev_rest))
        prev_waits = [
            [copies.start(prev[0].at[pl.ds(at, to.shape[0])], to)] for at, to in parts
        ]
    prev_refs = (c.prev_mats, c.prev_rest) if chained else (None, None)
    small = copies.small(c.own, c.other)
    c.spread = spread_matrix(z.cols, 3)
    c.smalls[...] = jnp.zeros_like(c.smalls)
    for _ in forward_stages(z, 1, copies, c, small, (c.base, c.mask), picks, x_waits):
        pass
    windows_to_image(c.total, c.spread, c.y, c.rim.at[pl.ds(3, 3)], 4)
    waits = (dy_waits, [], [], [], [], [], prev_waits[0])
    for _ in feed_back_stages(z, copies, c, small, waits, prev_refs[0], outs, c.smalls):
        pass
    waits = ([], [], [], [], [], [], prev_waits[1])
    attend_back_stages(z, copies, c, small, waits, prev_refs[1], outs, z.feed_rows, c.smalls)
    input_stages(z, c, small)
    windows_to_image(c.xs, c.spread, c.dx, c.rim.at[pl.ds(0, 3)], 4)
    copies.finish()


def feed_back_kernel(z, n_dy, dy_plan, chained, scratch, core_ref, *refs):
    c = Refs(refs, ())
    dy_refs = c.several(n_dy)
    c.name(("own", "other"))
    big = c.pairs(2)
    kept = c.several(3)
    prev = c.several(2) if chained else None
    c.name(("o_gx1", "o_small"))
    outs = c.several(2 if chained else 1)
    c.name(scratch)
    copies = Copies(core_ref, 0, c.sems)
    w_dy = copies.rows(dy_refs, dy_plan, c.dy_rows)
    w_narrow = copies.pick(big[1], c.narrow)
    w_slope = copies.start(kept[2], c.slope)
    w_widen = copies.pick(big[0], c.widen)
    w_x1 = copies.start(kept[0], c.x1)
    w_act = copies.start(kept[1], c.act)
    w_prev = [copies.start(prev[0], c.prev_mats)] if chained else []
    small = copies.small(c.own, c.other)
    c.spread = spread_matrix(z.cols, 0)
    c.o_small[...] = prev[1][...] if chained else jnp.zeros_like(c.o_small)
    waits = (w_dy, [w_narrow], [w_slope], [w_widen], [w_x1], [w_act], w_prev)
    stages = feed_back_stages(
        z, copies, c, small, waits, c.prev_mats if chained else None, outs, c.o_small
    )
    next(stages)
    copies.write(c.gx1, c.o_gx1)
    for _ in stages:
        pass
    copies.finish()


def attend_back_kernel(z, n_x, x_plan, chained, last, scratch, core_ref, *refs):
    c = Refs(refs, ())
    x_refs = c.several(n_x)
    c.name(("own", "other"))
    big = c.pairs(2)
    kept = c.several(4)
    c.name(("smalls",))
    prev = c.several(1) if chained else None
    c.name(("out",))
    outs = c.several(2 if chained else 1)
    c.name(scratch)
    copies = Copies(core_ref, 0, c.sems)
    w_gx1 = copies.start(kept[0], c.gx1)
    w_attend = copies.pick(big[1], c.attend)
    w_qkv = [copies.start(kept[1], c.qkv), copies.start(kept[2], c.probs)]
    w_x = copies.rows(x_refs, x_plan, c.x_rows)
    w_mix = copies.start(kept[3], c.low_mix)
    w_triple = copies.pick(big[0], c.triple)
    w_prev = [copies.start(prev[0], c.prev_rest)] if chained else []
    small = copies.small(c.own, c.other)
    c.spread = spread_matrix(z.cols, 0)
    waits = ([w_gx1], [w_attend], [w_mix], w_qkv, w_x, [w_triple], w_prev)
    attend_back_stages(
        z, copies, c, small, waits, c.prev_rest if chained else None, outs, 0, c.smalls
    )
    if last:
        copies.write(c.dq, c.out)
    else:
        input_stages(z, c, small)
        windows_to_image(c.xs, c.spread, c.out)
    copies.finish()


def input_kernel(z, n_x, x_plan, scratch, core_ref, *refs):
    c = Refs(refs, ())
    x_refs = c.several(n_x)
    c.name(("own", "other"))
    big = c.pairs(1)
    kept = c.several(2)
    c.name(("out",))
    c.name(scratch)
    copies = Copies(core_ref, 0, c.sems)
    w_dq = copies.start(kept[1], c.dq)
    w_triple = copies.pick(big[0], c.triple)
    w_x = copies.rows(x_refs, x_plan, c.x_rows)
    w_gx1 = copies.start(kept[0], c.gx1)
    small = copies.small(c.own, c.other)
    c.spread = spread_matrix(z.cols, 0)
    wait_all(w_x)
    image_to_windows(c.x_rows, c.spread, c.xs)
    wait_all([w_dq, w_triple, w_gx1])
    input_stages(z, c, small)
    windows_to_image(c.xs, c.spread, c.out)
    copies.finish()


def unpack_kernel(z, scratch, core_ref, *refs):
    c = Refs(refs, ("value0", "value1", "arrived"))
    c.name(("triple", "attend", "widen", "narrow", "gain1", "shift1", "query_b", "value_b",
            "attend_b", "gain2", "shift2", "widen_b", "narrow_b", "pair"))
    c.name(scratch)
    copies = Copies(core_ref, 0, c.sems)
    feats, hidden = z.feats, z.hidden
    waits = [[], [], []]

    def fetch(stage, at, size, from0, from1):
        target = c.all_rows.at[pl.ds(at, size)]
        sem = copies.next()
        copy0, copy1 = (
            pltpu.make_async_copy(ref.at[pl.ds(row, size)], target, sem)
            for ref, row in (from0, from1)
        )
        pl.when(copies.mine)(copy0.start)
        pl.when(jnp.logical_not(copies.mine))(copy1.start)
        waits[stage].append(copy1)

    total = z.feed_rows + z.attend_rows
    quarters = (z.feed_rows // 8, z.attend_rows // 8)
    piece = sum(quarters)
    for half, source0 in enumerate((c.value0, c.arrived)):
        for which, quarter in enumerate(quarters):
            for i in range(4):
                at = which * z.feed_rows + (half * 4 + i) * quarter
                row0 = i * piece + which * quarters[0]
                cuts = [at, at + quarter]
                if at < total // 2 < at + quarter:
                    cuts.insert(1, total // 2)
                for low, high in zip(cuts, cuts[1:]):
                    if low < total // 2:
                        from1 = (c.arrived, low)
                    else:
                        from1 = (c.value1, low - total // 2)
                    stage = 2 if which else half
                    fetch(stage, low, high - low, (source0, row0 + low - at), from1)

    def rows(first, size):
        return c.all_rows[first : first + size, :].astype(f32)

    wait_all(waits[0])
    for j in range(hidden // feats):
        c.v_widen[:, j * feats : (j + 1) * feats] = rows(j * feats, feats)
    copies.write(c.v_widen, c.widen.at[0])
    wait_all(waits[1])
    c.v_narrow[...] = rows(hidden, hidden)
    copies.write(c.v_narrow, c.narrow.at[0])
    wait_all(waits[2])
    at = z.feed_rows
    for j in range(3):
        c.v_triple[:, j * feats : (j + 1) * feats] = rows(at + j * feats, feats)
    copies.write(c.v_triple, c.triple.at[0])
    c.v_attend[...] = rows(at + 3 * feats, feats)
    copies.write(c.v_attend, c.attend.at[0])
    at += 4 * feats
    smalls = rows(at, small_rows)
    for ref, row in ((c.query_b, 0), (c.value_b, 2), (c.gain1, s_gain1), (c.shift1, s_shift1),
                     (c.attend_b, s_attend_b), (c.gain2, s_gain2), (c.shift2, s_shift2),
                     (c.narrow_b, s_narrow_b)):
        ref[...] = smalls[row : row + 1]
    for j in range(hidden // feats):
        row = s_widen_b + j
        c.widen_b[:, j * feats : (j + 1) * feats] = smalls[row : row + 1]
    at += small_rows
    cut = z.groups * cells * z.lanes // feats
    flat = rows(at, cut)
    left = z.groups * cells - cut
    more = flat[:, z.lanes :]
    c.pair[...] = jnp.concatenate(
        [flat[:, : z.lanes], jnp.concatenate([more[:left], more[left:]], 1)], 0
    ).reshape(c.pair.shape)
    copies.finish()


class Sizes:
    def __init__(self, own_rows, cols, feats, hidden, heads):
        self.steps = own_rows // 7
        self.cols = cols
        self.feats = feats
        self.hidden = hidden
        self.wins = cols // 7
        self.rows = self.wins * cells
        self.depth = feats // heads
        self.groups = feats // 128
        self.lanes = 128 // self.depth * tall
        self.parts = 2
        self.feed_rows = 2 * hidden
        rows = self.feed_rows + 4 * feats + small_rows + self.groups * cells * self.lanes // feats
        self.attend_rows = -(-rows // 256) * 256 - self.feed_rows


def in_vmem(item):
    return pl.BlockSpec(item.shape, lambda i, c: (0,) * item.ndim)


hbm = pl.BlockSpec(memory_space=pl.ANY)


def shaped(shape, kind):
    return jax.ShapeDtypeStruct(shape, kind)


def scratch_table(z):
    feats, hidden, rows, wins = z.feats, z.hidden, z.rows, z.wins
    image = ((7, z.cols, feats), bf16)
    wide = ((wins, cells, feats), f32)
    low = ((rows, feats), bf16)
    high = ((rows, feats), f32)
    deep = ((rows, hidden), bf16)
    return {
        "triple": ((feats, 3 * feats), bf16),
        "attend": ((feats, feats), bf16),
        "widen": ((feats, hidden), bf16),
        "narrow": ((hidden, feats), bf16),
        "x_rows": image,
        "dy_rows": image,
        "xs": wide,
        "n1": low,
        "qkv": ((wins, tall, 3 * feats), bf16),
        "bias": ((3, z.groups, cells, z.lanes), f32),
        "probs": ((wins, z.groups, tall, z.lanes), bf16),
        "mixed": wide,
        "low_mix": low,
        "x1": high,
        "n2": low,
        "act": deep,
        "slope": deep,
        "total": wide,
        "dy": low,
        "dh": deep,
        "dn2": high,
        "gx1": high,
        "mats": ((z.feed_rows, feats), bf16),
        "prev_mats": ((z.feed_rows, feats), bf16),
        "smalls": ((small_rows, feats), f32),
        "da": low,
        "gmix": ((wins, tall, feats), bf16),
        "gqkv": ((wins, cells, 3 * feats), f32),
        "dq": ((rows, 3 * feats), bf16),
        "pair": ((z.groups, cells, z.lanes), f32),
        "rest": ((z.attend_rows, feats), bf16),
        "prev_rest": ((z.attend_rows, feats), bf16),
        "all_rows": ((z.feed_rows + z.attend_rows, feats), bf16),
        "v_triple": ((feats, 3 * feats), f32),
        "v_attend": ((feats, feats), f32),
        "v_widen": ((feats, hidden), f32),
        "v_narrow": ((hidden, feats), f32),
    }


def call(kernel, z, core, inputs, outputs, scratch, passes):
    inputs = [item if isinstance(item, tuple) else (item, hbm) for item in inputs]
    out_specs = [
        hbm if manual else pl.BlockSpec(shape, lambda i, c, n=len(shape): (0,) * n)
        for shape, _, manual in outputs
    ]
    table = scratch_table(z)
    return pl.pallas_call(
        partial(kernel, scratch + ("sems",)),
        grid_spec=pltpu.PrefetchScalarGridSpec(
            num_scalar_prefetch=1,
            grid=(1,),
            in_specs=[spec for _, spec in inputs],
            out_specs=out_specs,
            scratch_shapes=[pltpu.VMEM(*table[name]) for name in scratch]
            + [pltpu.SemaphoreType.DMA((24,))],
        ),
        out_shape=[shaped(shape, kind) for shape, kind, _ in outputs],
        compiler_params=pltpu.CompilerParams(
            dimension_semantics=("arbitrary",), vmem_limit_bytes=vmem_bytes
        ),
        cost_estimate=pl.CostEstimate(
            flops=int(passes * 20 * z.rows * z.feats * (4 * z.feats + 2 * z.hidden)),
            bytes_accessed=int(passes * 300_000_000),
            transcendentals=0,
        ),
    )(core, *(item for item, _ in inputs))


def gradient_outputs(z, rows, chained):
    return [((rows // 2, z.feats), bf16, True)] * 2 if chained else [((rows, z.feats), bf16, True)]


def resident(items):
    return [(item, in_vmem(item)) for item in items]


def flat_pairs(pairs):
    return [item for pair in pairs for item in pair]


forward_scratch = (
    "triple", "attend", "widen", "narrow", "x_rows", "xs", "n1", "qkv", "bias", "probs", "mixed",
    "low_mix", "x1", "n2", "act", "slope", "total",
)
back_scratch = ("dy_rows", "dy", "dh", "dn2", "gx1", "mats")
attend_back_scratch = ("da", "gmix", "gqkv", "dq", "pair", "rest")


def run_forward(z, core, xs, x_plan, params, base):
    inputs = list(xs) + resident(params["small"] + [base]) + flat_pairs(params["big"])
    table = scratch_table(z)
    rim = ((3, z.cols, z.feats), bf16, False)
    outputs = [(*table["x_rows"], False), rim] + [
        (*table[name], True) for name in ("qkv", "probs", "low_mix", "x1", "act", "slope")
    ]
    kernel = partial(bind, forward_kernel, (z, len(xs), x_plan))
    return call(kernel, z, core, inputs, outputs, forward_scratch, 1.2)


def bind(kernel, arguments, scratch, *refs):
    kernel(*arguments, scratch, *refs)


def run_both(z, core, xs, x_plan, dys, dy_plan, params, base, mask, prev):
    inputs = list(xs) + list(dys) + resident(params["small"] + [base, mask])
    inputs += flat_pairs(params["big"]) + ([] if prev is None else [prev])
    table = scratch_table(z)
    image = (*table["x_rows"], False)
    outputs = [image, image, ((6, z.cols, z.feats), bf16, False)]
    outputs += gradient_outputs(z, z.feed_rows + z.attend_rows, prev is not None)
    scratch = forward_scratch + back_scratch + attend_back_scratch + ("smalls",)
    if prev is not None:
        scratch += ("prev_mats", "prev_rest")
    arguments = (z, len(xs), x_plan, len(dys), dy_plan, prev is not None)
    return call(partial(bind, both_kernel, arguments), z, core, inputs, outputs, scratch, 4.0)


def run_feed_back(z, core, dys, dy_plan, params, kept, prev):
    inputs = list(dys) + resident(params["small"]) + flat_pairs(params["big"][2:]) + list(kept)
    if prev:
        inputs += [prev[0]] + resident(prev[1:])
    table = scratch_table(z)
    outputs = [(*table["gx1"], True), (*table["smalls"], False)]
    outputs += gradient_outputs(z, z.feed_rows, bool(prev))
    scratch = back_scratch + ("widen", "narrow", "x1", "n2", "act", "slope", "total")
    if prev:
        scratch += ("prev_mats",)
    arguments = (z, len(dys), dy_plan, bool(prev))
    return call(
        partial(bind, feed_back_kernel, arguments), z, core, inputs, outputs, scratch, 1.2
    )


def run_attend_back(z, core, xs, x_plan, params, kept, smalls, prev, last):
    inputs = list(xs) + resident(params["small"]) + flat_pairs(params["big"][:2]) + list(kept)
    inputs += resident([smalls])
    if prev is not None:
        inputs.append(prev)
    table = scratch_table(z)
    outputs = [(*table["dq"], True) if last else (*table["x_rows"], False)]
    outputs += gradient_outputs(z, z.attend_rows, prev is not None)
    scratch = attend_back_scratch + (
        "triple", "attend", "x_rows", "xs", "n1", "qkv", "probs", "low_mix", "gx1", "dn2",
    )
    if prev is not None:
        scratch += ("prev_rest",)
    arguments = (z, len(xs), x_plan, prev is not None, last)
    return call(
        partial(bind, attend_back_kernel, arguments), z, core, inputs, outputs, scratch, 1.5
    )


def run_input(z, core, xs, x_plan, params, kept):
    inputs = list(xs) + resident(params["small"]) + flat_pairs(params["big"][:1]) + list(kept)
    scratch = ("triple", "x_rows", "xs", "gx1", "dq", "dn2")
    arguments = (z, len(xs), x_plan)
    outputs = [(*scratch_table(z)["x_rows"], False)]
    return call(partial(bind, input_kernel, arguments), z, core, inputs, outputs, scratch, 0.4)[0]


def run_unpack(z, core, value0, value1, arrived):
    feats, hidden = z.feats, z.hidden
    outputs = [
        ((1, feats, 3 * feats), f32, True),
        ((1, feats, feats), f32, True),
        ((1, feats, hidden), f32, True),
        ((1, hidden, feats), f32, True),
    ]
    outputs += [((1, feats), f32, False)] * 7
    outputs += [((1, hidden), f32, False), ((1, feats), f32, False)]
    outputs.append((*scratch_table(z)["pair"], False))
    scratch = ("all_rows", "v_triple", "v_attend", "v_widen", "v_narrow")
    kernel = partial(bind, unpack_kernel, (z,))
    return call(kernel, z, core, [value0, value1, arrived], outputs, scratch, 0.2)


def pair_index():
    place = np.arange(tall)
    u, w = place // 8, place % 8
    real = (u < 7) & (w < 7)
    index = (u[None, :] - u[:, None] + 6) * 13 + (w[None, :] - w[:, None] + 6)
    return np.where(real[:, None] & real[None, :], index, 169)[:cells]


def pair_onehot():
    return jnp.asarray(
        np.arange(169)[:, None] == pair_index().reshape(-1)[None, :], bf16
    )


def bias_base(table, z):
    spread = lax.dot_general(
        table, pair_onehot(), (((0,), (0,)), ((), ())), preferred_element_type=f32
    )
    spread = spread.reshape(z.groups, -1, cells, tall).transpose(0, 2, 1, 3)
    real = (np.arange(cells) % 8 < 7)[None, :, None, None]
    return (
        jnp.where(real, spread, masked_score).astype(bf16).reshape(z.groups, cells, z.lanes)
    )


def region_mask(z, step, first_row, total_rows):
    place = np.arange(tall)
    u, w = np.minimum(place // 8, 6), np.minimum(place % 8, 6)
    rows = jnp.mod(first_row + step * 7 + u + 3, total_rows)
    vertical = (rows >= total_rows - 7).astype(jnp.int32) + (rows >= total_rows - 3)
    kinds = []
    for column in (0, z.wins - 2, z.wins - 1):
        at = np.mod(column * 7 + w + 3, z.cols)
        horizontal = (at >= z.cols - 7).astype(np.int32) + (at >= z.cols - 3)
        code = vertical * 3 + horizontal
        alike = code[:cells, None] == code[None, :]
        kinds.append(jnp.where(alike, 0.0, masked_score).astype(f32))
    mask = jnp.stack(kinds)
    return jnp.tile(mask, (1, 1, z.lanes // tall))


def table_slope(pair, z, heads):
    pair = pair.reshape(z.groups, cells, -1, tall).transpose(1, 3, 0, 2).reshape(-1, heads)
    return mm(pair_onehot(), pair.astype(bf16))


def swap_cores(item):
    return lax.ppermute(item, "pipe", [(0, 1), (1, 0)])


def take(pair, index):
    return lax.dynamic_index_in_dim(pair, index, 0, keepdims=False)


def tie(item, *others):
    return lax.optimization_barrier((item,) + others)


class Reduction:
    near = 4

    def __init__(self, kept, sent=None):
        if sent is not None:
            kept = (kept.astype(f32) + swap_cores(sent).astype(f32)).astype(bf16)
        self.value = kept

    def partners(self, near):
        count, place = lax.axis_size("rows"), lax.axis_index("rows")
        size, unit = (self.near, 1) if near else (count // self.near, self.near)
        mine = (place // unit) % size
        return size, mine, [[(i, i ^ (d * unit)) for i in range(count)] for d in range(1, size)]

    def scatter(self, near):
        size, mine, routes = self.partners(near)
        parts = self.value.reshape((size, -1) + self.value.shape[1:])
        arrived = [
            lax.ppermute(take(parts, mine ^ d), "rows", route)
            for d, route in enumerate(routes, 1)
        ]
        total = take(parts, mine).astype(f32)
        for item in arrived:
            total = total + item.astype(f32)
        self.value = total.astype(bf16)

    def gather(self, near):
        size, mine, routes = self.partners(near)
        arrived = [lax.ppermute(self.value, "rows", route) for route in routes]
        parts = jnp.zeros((size,) + self.value.shape, bf16)
        for d, item in enumerate([self.value] + arrived):
            parts = lax.dynamic_update_index_in_dim(parts, item, mine ^ d, 0)
        self.value = parts.reshape((-1,) + self.value.shape[1:])

    def join(self, other):
        return Reduction(jnp.concatenate([self.value, other.value], 0))


def on_device(
    image_tokens,
    out_grad,
    first_gain,
    first_shift,
    triple_weight,
    query_bias,
    value_bias,
    bias_table,
    attend_weight,
    attend_bias,
    second_gain,
    second_shift,
    widen_weight,
    widen_bias,
    narrow_weight,
    narrow_bias,
):
    core = lax.axis_index("pipe")
    core_id = core.astype(jnp.int32).reshape(1)
    count = lax.axis_size("rows")
    place = lax.axis_index("rows")
    batches, own_rows, cols, feats = image_tokens.shape
    heads = bias_table.shape[2]
    hidden = widen_weight.shape[2]
    z = Sizes(own_rows, cols, feats, hidden, heads)
    total_rows = own_rows * count
    first_row = place * own_rows

    small = jnp.concatenate(
        [
            first_gain,
            first_shift,
            query_bias,
            jnp.zeros_like(query_bias),
            value_bias,
            attend_bias,
            second_gain,
            second_shift,
            narrow_bias,
            widen_bias.reshape(-1, feats),
            jnp.zeros((small_rows - 9 - hidden // feats, feats), bf16),
        ],
        0,
    ).astype(f32)
    tables = [bias_table[0], swap_cores(bias_table[0])]
    first = core == 0
    big = (triple_weight, attend_weight, widen_weight, narrow_weight)
    params = {
        "small": [small, swap_cores(small)],
        "big": [(item, swap_cores(item)) for item in big],
    }
    to_previous = [((i + 1) % count, i) for i in range(count)]
    to_next = [(i, (i + 1) % count) for i in range(count)]
    base0 = bias_base(jnp.where(first, tables[0], tables[1]), z)

    upper = [(0, True, 0, 7)]
    lower = [(0, True, 7, 7)]

    y00, y0_rim, *kept0 = run_forward(z, core_id, [image_tokens], upper, params, base0)
    y0_halo = lax.ppermute(y0_rim, "rows", to_previous)
    late_grad, late_row, late_table, _ = tie(
        out_grad, first_row, jnp.where(first, tables[1], tables[0]), y00
    )
    grad_halo = lax.ppermute(take(late_grad, core)[:3], "rows", to_previous)
    masks = [region_mask(z, step, late_row, total_rows) for step in range(2)]
    base1 = bias_base(late_table, z)
    y01, _, *kept1 = run_forward(z, core_id, [image_tokens], lower, params, base0)
    (qkv0, probs0, mix0, x10, act0, slope0) = kept0
    (qkv1, probs1, mix1, x11, act1, slope1) = kept1

    y10, dx10, _, all10 = run_both(
        z, core_id, [y00, y01], [(0, False, 3, 4), (1, False, 0, 3)], [out_grad],
        [(0, True, 3, 7)], params, base1, masks[0], None,
    )
    y11, dx11, rim1, *all11 = run_both(
        z, core_id, [y01, y0_halo], [(0, False, 3, 4), (1, False, 0, 3)],
        [out_grad, grad_halo], [(0, True, 10, 4), (1, False, 0, 3)], params, base1, masks[1],
        all10,
    )
    halo1 = lax.ppermute(rim1, "rows", to_next)

    def sent(block0, block1):
        return swap_cores(jnp.where(first, block1, block0))

    def arranged(block0, block1, other):
        return jnp.where(first, jnp.stack([block0, other]), jnp.stack([other, block1]))[None]

    reduction1 = Reduction(*all11)

    gx01, small01, mats01 = run_feed_back(
        z, core_id, [dx10, dx11], [(0, False, 4, 3), (1, False, 0, 4)], params,
        [x11, act1, slope1], None,
    )
    halo1, reduction1.value = tie(halo1, reduction1.value)
    reduction1.scatter(True)
    gx00, small00, *mats00 = run_feed_back(
        z, core_id, [halo1, dx10], [(0, False, 0, 3), (1, False, 0, 4)], params,
        [x10, act0, slope0], (mats01, small01),
    )
    gx01, reduction1.value = tie(gx01, reduction1.value)
    reduction1.scatter(False)
    feed0 = Reduction(*mats00)
    dx01, rest01 = run_attend_back(
        z, core_id, [image_tokens], lower, params, [gx01, qkv1, probs1, mix1],
        jnp.zeros((small_rows, feats), f32), None, False,
    )
    gx00, reduction1.value, feed0.value = tie(gx00, reduction1.value, feed0.value)
    reduction1.gather(False)
    feed0.scatter(True)
    dq00, *rest00 = run_attend_back(
        z, core_id, [image_tokens], upper, params, [gx00, qkv0, probs0, mix0], small00, rest01,
        True,
    )
    rest00[0], reduction1.value, feed0.value = tie(
        rest00[0], reduction1.value, feed0.value
    )
    reduction1.gather(True)
    rest0 = Reduction(*rest00)
    dx00 = run_input(z, core_id, [image_tokens], upper, params, [gx00, dq00])
    rest0.value, y00, y01, y10, y11, dx10, dx11, halo1 = tie(
        rest0.value, y00, y01, y10, y11, dx10, dx11, halo1
    )
    hidden_out = jnp.concatenate([y00, y01], 0)
    final = jnp.concatenate([halo1[3:], y10, y11[:4]], 0)
    entry_grad = jnp.concatenate([halo1[:3], dx10, dx11[:4]], 0)
    image_grad = jnp.concatenate([dx00, dx01], 0)
    block_outputs = arranged(hidden_out, final, sent(hidden_out, final))
    input_grads = arranged(image_grad, entry_grad, sent(image_grad, entry_grad))

    rest0.scatter(True)
    rest0.value, block_outputs, input_grads = tie(rest0.value, block_outputs, input_grads)
    reduction = feed0.join(rest0)
    reduction.scatter(False)
    reduction.gather(False)
    reduction.gather(True)

    arrived = swap_cores(jnp.where(first, reduction1.value, reduction.value))
    (t_triple, t_attend, t_widen, t_narrow, t_gain1, t_shift1, t_query_b, t_value_b,
     t_attend_b, t_gain2, t_shift2, t_widen_b, t_narrow_b, pair) = run_unpack(
        z, core_id, reduction.value, reduction1.value, arrived
    )

    return (
        block_outputs,
        input_grads,
        t_gain1,
        t_shift1,
        t_triple,
        t_query_b,
        t_value_b,
        table_slope(pair, z, heads)[None],
        t_attend,
        t_attend_b,
        t_gain2,
        t_shift2,
        t_widen,
        t_widen_b,
        t_narrow,
        t_narrow_b,
    )


def solution(mesh):
    param_specs = [
        P("pipe", None),
        P("pipe", None),
        P("pipe", None, None),
        P("pipe", None),
        P("pipe", None),
        P("pipe", None, None),
        P("pipe", None, None),
        P("pipe", None),
        P("pipe", None),
        P("pipe", None),
        P("pipe", None, None),
        P("pipe", None),
        P("pipe", None, None),
        P("pipe", None),
    ]
    in_specs = (P(None, "rows", None, None),) * 2 + tuple(param_specs)
    out_specs = (P("pipe", None, "rows", None, None),) * 2 + tuple(param_specs)
    return jax.shard_map(
        on_device, mesh=mesh, in_specs=in_specs, out_specs=out_specs, check_vma=False
    )
```

```python
from functools import partial

import jax
import jax.numpy as jnp
import numpy as np
from jax import lax
from jax.experimental import pallas as pl
from jax.experimental.pallas import tpu as pltpu
from jax.sharding import PartitionSpec as P

f32 = jnp.float32
bf16 = jnp.bfloat16
epsilon = 1e-05
masked_score = -1e30
vmem_bytes = 60 * 1024 * 1024
cells = 56
tall = 64

gain1_row, shift1_row, query_bias_row, value_bias_row = 0, 1, 2, 4
attend_bias_row, gain2_row, shift2_row, narrow_bias_row, widen_bias_row = 5, 6, 7, 8, 9
s_gain1, s_shift1, s_attend_b, s_gain2, s_shift2, s_narrow_b, s_widen_b = 3, 4, 5, 6, 7, 8, 9
small_rows = 16


def mm(left, right):
    return lax.dot_general(left, right, (((1,), (0,)), ((), ())), preferred_element_type=f32)


def mm_t(left, right):
    return lax.dot_general(left, right, (((1,), (1,)), ((), ())), preferred_element_type=f32)


def t_mm(left, right):
    return lax.dot_general(left, right, (((0,), (0,)), ((), ())), preferred_element_type=f32)


def normed_parts(values):
    center = values - jnp.mean(values, -1, keepdims=True)
    spread = jnp.mean(center * center, -1, keepdims=True)
    scale = lax.rsqrt(spread + epsilon)
    return center * scale, scale


def norm_back(grad, hat, scale, gain):
    pulled = grad * gain
    return scale * (
        pulled
        - jnp.mean(pulled, -1, keepdims=True)
        - hat * jnp.mean(pulled * hat, -1, keepdims=True)
    )


def gelu_parts(value):
    below = 0.5 + 0.5 * lax.erf(value * 0.5**0.5)
    bell = jnp.exp(value * value * -0.5)
    return value * below, below + value * bell * (2.0 * np.pi) ** -0.5


def row_sum(values):
    return jnp.sum(values, 0, keepdims=True)


def head_masks(depth):
    place = lax.broadcasted_iota(jnp.int32, (1, 128), 1) // depth
    return [(place == h) for h in range(128 // depth)]


def spread_heads(part, masks):
    return jnp.concatenate([part * m.astype(bf16) for m in masks], 0)


def collect_heads(high, masks):
    rows = high.shape[0] // len(masks)
    out = high[:rows]
    for h in range(1, len(masks)):
        out = jnp.where(masks[h], high[h * rows : (h + 1) * rows], out)
    return out


def pad_rows(values, rows):
    return jnp.concatenate(
        [values, jnp.zeros((rows - values.shape[0], values.shape[1]), values.dtype)], 0
    )


def spread_matrix(cols, roll_by):
    place = lax.broadcasted_iota(jnp.int32, (cols // 7 * 8, cols), 0)
    column = lax.broadcasted_iota(jnp.int32, (cols // 7 * 8, cols), 1)
    w = place & 7
    target = (place >> 3) * 7 + w + roll_by
    target = jnp.where(target >= cols, target - cols, target)
    return jnp.where((target == column) & (w < 7), 1.0, 0.0).astype(bf16)


def image_to_windows(image, spread, out):
    for u in range(7):
        part = mm(spread, image[u])
        out[:, u * 8 : (u + 1) * 8, :] = part.reshape(-1, 8, part.shape[-1])


def windows_to_image(windows, spread, image, rim=None, first=0):
    wins, _, feats = windows.shape
    for u in range(7):
        part = windows[:, u * 8 : (u + 1) * 8, :].reshape(wins * 8, feats).astype(bf16)
        row = t_mm(spread, part).astype(bf16)
        image[u] = row
        if rim is not None and first <= u < first + 3:
            rim[u - first] = row


def by_rows(rows, parts, step):
    size = rows // parts

    def body(i, carry):
        step(i, pl.ds(pl.multiple_of(i * size, size), size))
        return carry

    lax.fori_loop(0, parts, body, 0)


class Copies:
    def __init__(self, core_ref, block, sems):
        self.core = core_ref[0]
        self.mine = self.core == block
        self.sems = sems
        self.count = 0
        self.writes = []

    def next(self):
        self.count += 1
        return self.sems.at[self.count - 1]

    def start(self, source, target):
        copy = pltpu.make_async_copy(source, target, self.next())
        copy.start()
        return copy

    def pick(self, pair, target):
        own, other = pair
        sem = self.next()

        @pl.when(self.mine)
        def _():
            pltpu.make_async_copy(own.at[0], target, sem).start()

        @pl.when(jnp.logical_not(self.mine))
        def _():
            pltpu.make_async_copy(other.at[0], target, sem).start()

        return pltpu.make_async_copy(own.at[0], target, sem)

    def rows(self, refs, plan, target):
        at = 0
        copies = []
        for which, batched, first, size in plan:
            source = refs[which].at[self.core] if batched else refs[which]
            copies.append(
                self.start(source.at[pl.ds(first, size)], target.at[pl.ds(at, size)])
            )
            at += size
        return copies

    def write(self, source, target):
        self.writes.append(self.start(source, target))

    def write_rows(self, source, at, outs):
        size = source.shape[0]
        if len(outs) == 1:
            self.write(source, outs[0].at[pl.ds(at, size)])
            return
        half = outs[0].shape[0]
        low = at
        while low < at + size:
            which = low // half
            high = min(at + size, (which + 1) * half)
            part = source.at[pl.ds(low - at, high - low)]
            keep, send = (out.at[pl.ds(low - which * half, high - low)] for out in outs)
            sem = self.next()
            pl.when(self.core == which)(pltpu.make_async_copy(part, keep, sem).start)
            pl.when(self.core != which)(pltpu.make_async_copy(part, send, sem).start)
            self.writes.append(pltpu.make_async_copy(part, keep, sem))
            low = high

    def finish(self):
        for copy in self.writes:
            copy.wait()

    def small(self, own, other):
        return jnp.where(self.mine, own[...], other[...])


def wait_all(copies):
    for copy in copies:
        copy.wait()


def stage_norm(xs, gain, shift, n1):
    wins, _, feats = xs.shape

    def step(i, span):
        hat, _ = normed_parts(xs[pl.ds(i * 4, 4)].reshape(4 * cells, feats))
        n1[span, :] = (hat * gain + shift).astype(bf16)

    by_rows(wins * cells, wins // 4, step)


def stage_triple(n1, triple, small, qkv):
    wins, _, width = qkv.shape
    feats = width // 3
    qkv[:, cells:, :] = jnp.zeros((wins, tall - cells, width), bf16)
    offsets = (query_bias_row, None, value_bias_row)
    for j in range(3):
        lanes = slice(j * feats, (j + 1) * feats)
        part = mm(n1[...], triple[:, lanes])
        if offsets[j] is not None:
            part = part + small[offsets[j] : offsets[j] + 1]
        qkv[:, :cells, lanes] = part.reshape(wins, cells, feats).astype(bf16)


def stage_attend(qkv, bias, probs, mixed, depth, shifted):
    wins, _, width = qkv.shape
    feats = width // 3
    masks = head_masks(depth)
    scale = depth**-0.5

    def step(w, carry):
        kind = jnp.maximum(w - (wins - 3), 0) if shifted else 0
        for g in range(feats // 128):
            at = g * 128
            q = qkv[w, :, at : at + 128]
            k = qkv[w, :, feats + at : feats + at + 128]
            v = qkv[w, :, 2 * feats + at : 2 * feats + at + 128]
            scores = mm_t(k, spread_heads(q, masks))[:cells] * scale + bias[kind, g]
            powers = jnp.exp(scores - jnp.max(scores, 0, keepdims=True))
            weights = powers * (1.0 / jnp.sum(powers, 0, keepdims=True))
            low = pad_rows(weights, tall).astype(bf16)
            probs[w, g] = low
            mixed[w, :, at : at + 128] = collect_heads(t_mm(low, v), masks)[:cells]
        return carry

    lax.fori_loop(0, wins, step, 0, unroll=16)


def forward_stages(z, block, copies, c, small, bias_parts, picks, x_waits):
    rows, feats = c.x1.shape
    base, mask = bias_parts
    base = base[...].astype(f32)
    if block == 1:
        for kind in range(3):
            for g in range(z.groups):
                c.bias[kind, g] = base[g] + jnp.concatenate(
                    [mask[kind]] * (z.lanes // tall), 1
                )
    else:
        c.bias[0] = base
    wait_all(x_waits)
    image_to_windows(c.x_rows, c.spread, c.xs)
    stage_norm(c.xs, small[gain1_row : gain1_row + 1], small[shift1_row : shift1_row + 1], c.n1)
    picks[0].wait()
    stage_triple(c.n1, c.triple, small, c.qkv)
    yield
    stage_attend(c.qkv, c.bias, c.probs, c.mixed, z.depth, block == 1)
    c.low_mix[...] = c.mixed[...].reshape(rows, feats).astype(bf16)
    yield
    picks[1].wait()
    c.x1[...] = (
        c.xs[...].reshape(rows, feats)
        + mm(c.low_mix[...], c.attend[...])
        + small[attend_bias_row : attend_bias_row + 1]
    )
    yield
    second_norm(small, c)
    picks[2].wait()
    part = z.hidden // z.parts
    for j in range(z.parts):
        lanes = slice(j * part, (j + 1) * part)
        offset = jnp.concatenate(
            [
                small[widen_bias_row + i : widen_bias_row + i + 1]
                for i in range(j * part // feats, (j + 1) * part // feats)
            ],
            1,
        )
        value, pull = gelu_parts(mm(c.n2[...], c.widen[:, lanes]) + offset)
        c.act[:, lanes] = value.astype(bf16)
        c.slope[:, lanes] = pull.astype(bf16)
    yield
    picks[3].wait()
    c.total[...] = (
        c.x1[...]
        + mm(c.act[...], c.narrow[...])
        + small[narrow_bias_row : narrow_bias_row + 1]
    ).reshape(c.total.shape)


def second_norm(small, c):
    gain2 = small[gain2_row : gain2_row + 1]
    shift2 = small[shift2_row : shift2_row + 1]

    def norm_step(i, span):
        hat, _ = normed_parts(c.x1[span, :])
        c.n2[span, :] = (hat * gain2 + shift2).astype(bf16)

    by_rows(c.x1.shape[0], 4, norm_step)


def feed_back_stages(z, copies, c, small, waits, prev, outs, o_small):
    rows, feats = c.x1.shape
    w_dy, w_narrow, w_slope, w_widen, w_x1, w_act, w_prev = waits
    wait_all(w_dy)
    image_to_windows(c.dy_rows, c.spread, c.total)
    c.dy[...] = c.total[...].reshape(rows, feats).astype(bf16)
    sums = {s_narrow_b: row_sum(c.total[...].reshape(rows, feats))}
    part = z.hidden // z.parts
    wait_all(w_narrow + w_slope)
    for j in range(z.parts):
        lanes = slice(j * part, (j + 1) * part)
        grad = mm_t(c.dy[...], c.narrow[lanes, :]) * c.slope[:, lanes].astype(f32)
        total = row_sum(grad)
        for i in range(part // feats):
            sums[s_widen_b + j * part // feats + i] = total[:, i * feats : (i + 1) * feats]
        c.dh[:, lanes] = grad.astype(bf16)
    wait_all(w_widen + w_x1)
    if w_x1:
        second_norm(small, c)
    c.dn2[...] = mm_t(c.dh[...], c.widen[...])
    gain2 = small[gain2_row : gain2_row + 1]

    def norm_step(i, span):
        hat, scale = normed_parts(c.x1[span, :])
        grad = c.dn2[span, :]
        o_small[s_gain2 : s_gain2 + 1] += row_sum(grad * hat)
        o_small[s_shift2 : s_shift2 + 1] += row_sum(grad)
        c.gx1[span, :] = c.dy[span, :].astype(f32) + norm_back(grad, hat, scale, gain2)

    for at, value in sums.items():
        o_small[at : at + 1] += value
    by_rows(rows, 4, norm_step)
    yield
    wait_all(w_prev)

    def put(at, value):
        span = slice(at, at + feats)
        if prev is not None:
            value = value + prev[span, :].astype(f32)
        c.mats[span, :] = value.astype(bf16)

    for j in range(z.hidden // feats):
        put(j * feats, t_mm(c.n2[...], c.dh[:, j * feats : (j + 1) * feats]))
    half = c.mats.shape[0] // 2
    copies.write_rows(c.mats.at[pl.ds(0, half)], 0, outs)
    wait_all(w_act)
    for j in range(z.hidden // feats):
        put(z.hidden + j * feats, t_mm(c.act[:, j * feats : (j + 1) * feats], c.dy[...]))
    copies.write_rows(c.mats.at[pl.ds(half, half)], half, outs)


def attend_back_stages(z, copies, c, small, waits, prev, outs, first_row, smalls):
    w_gx1, w_attend, w_mix, w_qkv, w_x, w_triple, w_prev = waits
    wins, _, feats = c.xs.shape
    rows = wins * cells
    depth = z.depth
    masks = head_masks(depth)
    scale = depth**-0.5
    mats = 4 * feats
    qkv, probs, gmix, gqkv, pair = c.qkv, c.probs, c.gmix, c.gqkv, c.pair
    wait_all(w_gx1)
    c.da[...] = c.gx1[...].astype(bf16)
    attend_b = row_sum(c.gx1[...])
    wait_all(w_attend)
    gmix[:, cells:, :] = jnp.zeros((wins, tall - cells, feats), bf16)
    gmix[:, :cells, :] = mm_t(c.da[...], c.attend[...]).reshape(wins, cells, feats).astype(bf16)
    pair[...] = jnp.zeros_like(pair)
    wait_all(w_qkv)

    def step(w, carry):
        for g in range(feats // 128):
            at = g * 128
            q = qkv[w, :, at : at + 128]
            k = qkv[w, :, feats + at : feats + at + 128]
            v = qkv[w, :, 2 * feats + at : 2 * feats + at + 128]
            wide = spread_heads(gmix[w, :, at : at + 128], masks)
            low = probs[w, g]
            high = low.astype(f32)[:cells]
            pulled = mm_t(v, wide)[:cells] * high
            ds = pulled - high * jnp.sum(pulled, 0, keepdims=True)
            pair[g] += ds
            ds = pad_rows(ds, tall).astype(bf16)
            gqkv[w, :, 2 * feats + at : 2 * feats + at + 128] = mm(low, wide)[:cells]
            gqkv[w, :, feats + at : feats + at + 128] = (
                mm(ds, spread_heads(q, masks))[:cells] * scale
            )
            gqkv[w, :, at : at + 128] = collect_heads(t_mm(ds, k), masks)[:cells] * scale
        return carry

    lax.fori_loop(0, wins, step, 0, unroll=16)
    gain1 = small[gain1_row : gain1_row + 1]
    shift1 = small[shift1_row : shift1_row + 1]
    if w_x:
        wait_all(w_x)
        image_to_windows(c.x_rows, c.spread, c.xs)

    def hat_step(i, span):
        hat, _ = normed_parts(c.xs[pl.ds(i * 4, 4)].reshape(4 * cells, feats))
        c.n1[span, :] = hat.astype(bf16)

    by_rows(rows, wins // 4, hat_step)
    wait_all(w_triple + w_mix + w_prev)

    def put(at, size, value):
        if prev is not None:
            value = value + prev[at : at + size, :].astype(f32)
        c.rest[at : at + size, :] = value.astype(bf16)

    put(3 * feats, feats, t_mm(c.low_mix[...], c.da[...]))
    columns = jnp.concatenate([gain1, shift1, jnp.zeros((6, feats), f32)], 0).T
    gain_column, shift_column = columns[:, 0:1], columns[:, 1:2]
    sums = []
    gain_grad = jnp.zeros((feats, 1), f32)
    shift_grad = jnp.zeros((8, feats), f32)
    for j in range(3):
        lanes = slice(j * feats, (j + 1) * feats)
        part = gqkv[:, :, lanes].reshape(rows, feats)
        total = row_sum(part)
        sums.append(total)
        c.dq[:, lanes] = part.astype(bf16)
        both = t_mm(c.n1[...], c.dq[:, lanes])
        put(j * feats, feats, gain_column * both + shift_column * total)
        gain_grad += jnp.sum(both * c.triple[:, lanes].astype(f32), -1, keepdims=True)
        top = total.astype(bf16)
        rest = (total - top.astype(f32)).astype(bf16)
        shift_grad += mm_t(
            jnp.concatenate([top.astype(f32), rest.astype(f32), jnp.zeros((6, feats), f32)], 0)
            .astype(bf16),
            c.triple[:, lanes],
        )
    sums.append(jnp.broadcast_to(gain_grad, (feats, 8)).T[0:1])
    sums.append(shift_grad[0:1] + shift_grad[1:2])
    sums.append(attend_b)
    put(
        mats,
        small_rows,
        smalls[...] + jnp.concatenate(sums + [jnp.zeros((small_rows - 6, feats), f32)], 0),
    )
    flat = pair[...].reshape(z.groups * cells, z.lanes)
    cut = flat.shape[0] * z.lanes // feats
    more = flat[cut:]
    put(
        mats + small_rows,
        cut,
        jnp.concatenate([flat[:cut], jnp.concatenate([more[:, :128], more[:, 128:]], 0)], 1),
    )
    end = mats + small_rows + cut
    c.rest[end:, :] = jnp.zeros((c.rest.shape[0] - end, feats), bf16)
    copies.write_rows(c.rest, first_row, outs)


def input_stages(z, c, small):
    wins, _, feats = c.xs.shape
    gain1 = small[gain1_row : gain1_row + 1]
    c.dn2[...] = mm_t(c.dq[...], c.triple[...])

    def norm_step(i, span):
        wide = pl.ds(i * 4, 4)
        hat, scale = normed_parts(c.xs[wide].reshape(4 * cells, feats))
        out = c.gx1[span, :] + norm_back(c.dn2[span, :], hat, scale, gain1)
        c.xs[wide] = out.reshape(4, cells, feats)

    by_rows(wins * cells, wins // 4, norm_step)


class Refs:
    def __init__(self, refs, names):
        self.refs = list(refs)
        for name in names:
            setattr(self, name, self.refs.pop(0))

    def several(self, number):
        return [self.refs.pop(0) for _ in range(number)]

    def pairs(self, number):
        return [tuple(self.several(2)) for _ in range(number)]

    def name(self, names):
        for name in names:
            setattr(self, name, self.refs.pop(0))


def forward_kernel(z, n_x, x_plan, scratch, core_ref, *refs):
    c = Refs(refs, ())
    x_refs = c.several(n_x)
    c.name(("own", "other", "base"))
    big = c.pairs(4)
    c.name(("y", "rim", "o_qkv", "o_probs", "o_mix", "o_x1", "o_act", "o_slope"))
    c.name(scratch)
    copies = Copies(core_ref, 0, c.sems)
    x_waits = copies.rows(x_refs, x_plan, c.x_rows)
    picks = [copies.pick(p, to) for p, to in zip(big, (c.triple, c.attend, c.widen, c.narrow))]
    small = copies.small(c.own, c.other)
    c.spread = spread_matrix(z.cols, 0)
    stages = forward_stages(z, 0, copies, c, small, (c.base, None), picks, x_waits)
    next(stages)
    copies.write(c.qkv, c.o_qkv)
    next(stages)
    copies.write(c.probs, c.o_probs)
    copies.write(c.low_mix, c.o_mix)
    next(stages)
    copies.write(c.x1, c.o_x1)
    next(stages)
    copies.write(c.act, c.o_act)
    copies.write(c.slope, c.o_slope)
    for _ in stages:
        pass
    windows_to_image(c.total, c.spread, c.y, c.rim, 0)
    copies.finish()


def both_kernel(z, n_x, x_plan, n_dy, dy_plan, chained, scratch, core_ref, *refs):
    c = Refs(refs, ())
    x_refs = c.several(n_x)
    dy_refs = c.several(n_dy)
    c.name(("own", "other", "base", "mask"))
    big = c.pairs(4)
    prev = c.several(1) if chained else None
    c.name(("y", "dx", "rim"))
    outs = c.several(2 if chained else 1)
    c.name(scratch)
    copies = Copies(core_ref, 1, c.sems)
    x_waits = copies.rows(x_refs, x_plan, c.x_rows)
    picks = [copies.pick(p, to) for p, to in zip(big, (c.triple, c.attend, c.widen, c.narrow))]
    dy_waits = copies.rows(dy_refs, dy_plan, c.dy_rows)
    prev_waits = [[], []]
    if chained:
        parts = ((0, c.prev_mats), (z.feed_rows, c.prev_rest))
        prev_waits = [
            [copies.start(prev[0].at[pl.ds(at, to.shape[0])], to)] for at, to in parts
        ]
    prev_refs = (c.prev_mats, c.prev_rest) if chained else (None, None)
    small = copies.small(c.own, c.other)
    c.spread = spread_matrix(z.cols, 3)
    c.smalls[...] = jnp.zeros_like(c.smalls)
    for _ in forward_stages(z, 1, copies, c, small, (c.base, c.mask), picks, x_waits):
        pass
    windows_to_image(c.total, c.spread, c.y, c.rim.at[pl.ds(3, 3)], 4)
    waits = (dy_waits, [], [], [], [], [], prev_waits[0])
    for _ in feed_back_stages(z, copies, c, small, waits, prev_refs[0], outs, c.smalls):
        pass
    waits = ([], [], [], [], [], [], prev_waits[1])
    attend_back_stages(z, copies, c, small, waits, prev_refs[1], outs, z.feed_rows, c.smalls)
    input_stages(z, c, small)
    windows_to_image(c.xs, c.spread, c.dx, c.rim.at[pl.ds(0, 3)], 4)
    copies.finish()


def feed_back_kernel(z, n_dy, dy_plan, chained, scratch, core_ref, *refs):
    c = Refs(refs, ())
    dy_refs = c.several(n_dy)
    c.name(("own", "other"))
    big = c.pairs(2)
    kept = c.several(3)
    prev = c.several(2) if chained else None
    c.name(("o_gx1", "o_small"))
    outs = c.several(2 if chained else 1)
    c.name(scratch)
    copies = Copies(core_ref, 0, c.sems)
    w_dy = copies.rows(dy_refs, dy_plan, c.dy_rows)
    w_narrow = copies.pick(big[1], c.narrow)
    w_slope = copies.start(kept[2], c.slope)
    w_widen = copies.pick(big[0], c.widen)
    w_x1 = copies.start(kept[0], c.x1)
    w_act = copies.start(kept[1], c.act)
    w_prev = [copies.start(prev[0], c.prev_mats)] if chained else []
    small = copies.small(c.own, c.other)
    c.spread = spread_matrix(z.cols, 0)
    c.o_small[...] = prev[1][...] if chained else jnp.zeros_like(c.o_small)
    waits = (w_dy, [w_narrow], [w_slope], [w_widen], [w_x1], [w_act], w_prev)
    stages = feed_back_stages(
        z, copies, c, small, waits, c.prev_mats if chained else None, outs, c.o_small
    )
    next(stages)
    copies.write(c.gx1, c.o_gx1)
    for _ in stages:
        pass
    copies.finish()


def attend_back_kernel(z, n_x, x_plan, chained, last, scratch, core_ref, *refs):
    c = Refs(refs, ())
    x_refs = c.several(n_x)
    c.name(("own", "other"))
    big = c.pairs(2)
    kept = c.several(4)
    c.name(("smalls",))
    prev = c.several(1) if chained else None
    c.name(("out",))
    outs = c.several(2 if chained else 1)
    c.name(scratch)
    copies = Copies(core_ref, 0, c.sems)
    w_gx1 = copies.start(kept[0], c.gx1)
    w_attend = copies.pick(big[1], c.attend)
    w_qkv = [copies.start(kept[1], c.qkv), copies.start(kept[2], c.probs)]
    w_x = copies.rows(x_refs, x_plan, c.x_rows)
    w_mix = copies.start(kept[3], c.low_mix)
    w_triple = copies.pick(big[0], c.triple)
    w_prev = [copies.start(prev[0], c.prev_rest)] if chained else []
    small = copies.small(c.own, c.other)
    c.spread = spread_matrix(z.cols, 0)
    waits = ([w_gx1], [w_attend], [w_mix], w_qkv, w_x, [w_triple], w_prev)
    attend_back_stages(
        z, copies, c, small, waits, c.prev_rest if chained else None, outs, 0, c.smalls
    )
    if last:
        copies.write(c.dq, c.out)
    else:
        input_stages(z, c, small)
        windows_to_image(c.xs, c.spread, c.out)
    copies.finish()


def input_kernel(z, n_x, x_plan, scratch, core_ref, *refs):
    c = Refs(refs, ())
    x_refs = c.several(n_x)
    c.name(("own", "other"))
    big = c.pairs(1)
    kept = c.several(2)
    c.name(("out",))
    c.name(scratch)
    copies = Copies(core_ref, 0, c.sems)
    w_dq = copies.start(kept[1], c.dq)
    w_triple = copies.pick(big[0], c.triple)
    w_x = copies.rows(x_refs, x_plan, c.x_rows)
    w_gx1 = copies.start(kept[0], c.gx1)
    small = copies.small(c.own, c.other)
    c.spread = spread_matrix(z.cols, 0)
    wait_all(w_x)
    image_to_windows(c.x_rows, c.spread, c.xs)
    wait_all([w_dq, w_triple, w_gx1])
    input_stages(z, c, small)
    windows_to_image(c.xs, c.spread, c.out)
    copies.finish()


def unpack_kernel(z, scratch, core_ref, *refs):
    c = Refs(refs, ("value0", "arrived0", "value1", "arrived1"))
    c.name(("triple", "attend", "widen", "narrow", "gain1", "shift1", "query_b", "value_b",
            "attend_b", "gain2", "shift2", "widen_b", "narrow_b", "pair"))
    c.name(scratch)
    copies = Copies(core_ref, 0, c.sems)
    feats, hidden = z.feats, z.hidden
    waits = [[], [], []]

    def fetch(stage, at, size, from0, from1):
        target = c.all_rows.at[pl.ds(at, size)]
        sem = copies.next()
        copy0, copy1 = (
            pltpu.make_async_copy(ref.at[pl.ds(row, size)], target, sem)
            for ref, row in (from0, from1)
        )
        pl.when(copies.mine)(copy0.start)
        pl.when(jnp.logical_not(copies.mine))(copy1.start)
        waits[stage].append(copy1)

    total = z.feed_rows + z.attend_rows
    quarters = (z.feed_rows // 8, z.attend_rows // 8)
    piece = sum(quarters)
    for half, source0 in enumerate((c.value0, c.arrived0)):
        for which, quarter in enumerate(quarters):
            for i in range(4):
                at = which * z.feed_rows + (half * 4 + i) * quarter
                row0 = i * piece + which * quarters[0]
                cuts = [at, at + quarter]
                if at < total // 2 < at + quarter:
                    cuts.insert(1, total // 2)
                for low, high in zip(cuts, cuts[1:]):
                    if low < total // 2:
                        from1 = (c.arrived1, low)
                    else:
                        from1 = (c.value1, low - total // 2)
                    stage = 2 if which else half
                    fetch(stage, low, high - low, (source0, row0 + low - at), from1)

    def rows(first, size):
        return c.all_rows[first : first + size, :].astype(f32)

    wait_all(waits[0])
    for j in range(hidden // feats):
        c.v_widen[:, j * feats : (j + 1) * feats] = rows(j * feats, feats)
    copies.write(c.v_widen, c.widen.at[0])
    wait_all(waits[1])
    c.v_narrow[...] = rows(hidden, hidden)
    copies.write(c.v_narrow, c.narrow.at[0])
    wait_all(waits[2])
    at = z.feed_rows
    for j in range(3):
        c.v_triple[:, j * feats : (j + 1) * feats] = rows(at + j * feats, feats)
    copies.write(c.v_triple, c.triple.at[0])
    c.v_attend[...] = rows(at + 3 * feats, feats)
    copies.write(c.v_attend, c.attend.at[0])
    at += 4 * feats
    smalls = rows(at, small_rows)
    for ref, row in ((c.query_b, 0), (c.value_b, 2), (c.gain1, s_gain1), (c.shift1, s_shift1),
                     (c.attend_b, s_attend_b), (c.gain2, s_gain2), (c.shift2, s_shift2),
                     (c.narrow_b, s_narrow_b)):
        ref[...] = smalls[row : row + 1]
    for j in range(hidden // feats):
        row = s_widen_b + j
        c.widen_b[:, j * feats : (j + 1) * feats] = smalls[row : row + 1]
    at += small_rows
    cut = z.groups * cells * z.lanes // feats
    flat = rows(at, cut)
    left = z.groups * cells - cut
    more = flat[:, z.lanes :]
    c.pair[...] = jnp.concatenate(
        [flat[:, : z.lanes], jnp.concatenate([more[:left], more[left:]], 1)], 0
    ).reshape(c.pair.shape)
    copies.finish()


class Sizes:
    def __init__(self, own_rows, cols, feats, hidden, heads):
        self.steps = own_rows // 7
        self.cols = cols
        self.feats = feats
        self.hidden = hidden
        self.wins = cols // 7
        self.rows = self.wins * cells
        self.depth = feats // heads
        self.groups = feats // 128
        self.lanes = 128 // self.depth * tall
        self.parts = 2
        self.feed_rows = 2 * hidden
        rows = self.feed_rows + 4 * feats + small_rows + self.groups * cells * self.lanes // feats
        self.attend_rows = -(-rows // 256) * 256 - self.feed_rows


def in_vmem(item):
    return pl.BlockSpec(item.shape, lambda i, c: (0,) * item.ndim)


hbm = pl.BlockSpec(memory_space=pl.ANY)


def shaped(shape, kind):
    return jax.ShapeDtypeStruct(shape, kind)


def scratch_table(z):
    feats, hidden, rows, wins = z.feats, z.hidden, z.rows, z.wins
    image = ((7, z.cols, feats), bf16)
    wide = ((wins, cells, feats), f32)
    low = ((rows, feats), bf16)
    high = ((rows, feats), f32)
    deep = ((rows, hidden), bf16)
    return {
        "triple": ((feats, 3 * feats), bf16),
        "attend": ((feats, feats), bf16),
        "widen": ((feats, hidden), bf16),
        "narrow": ((hidden, feats), bf16),
        "x_rows": image,
        "dy_rows": image,
        "xs": wide,
        "n1": low,
        "qkv": ((wins, tall, 3 * feats), bf16),
        "bias": ((3, z.groups, cells, z.lanes), f32),
        "probs": ((wins, z.groups, tall, z.lanes), bf16),
        "mixed": wide,
        "low_mix": low,
        "x1": high,
        "n2": low,
        "act": deep,
        "slope": deep,
        "total": wide,
        "dy": low,
        "dh": deep,
        "dn2": high,
        "gx1": high,
        "mats": ((z.feed_rows, feats), bf16),
        "prev_mats": ((z.feed_rows, feats), bf16),
        "smalls": ((small_rows, feats), f32),
        "da": low,
        "gmix": ((wins, tall, feats), bf16),
        "gqkv": ((wins, cells, 3 * feats), f32),
        "dq": ((rows, 3 * feats), bf16),
        "pair": ((z.groups, cells, z.lanes), f32),
        "rest": ((z.attend_rows, feats), bf16),
        "prev_rest": ((z.attend_rows, feats), bf16),
        "all_rows": ((z.feed_rows + z.attend_rows, feats), bf16),
        "v_triple": ((feats, 3 * feats), f32),
        "v_attend": ((feats, feats), f32),
        "v_widen": ((feats, hidden), f32),
        "v_narrow": ((hidden, feats), f32),
    }


def call(kernel, z, core, inputs, outputs, scratch, passes):
    inputs = [item if isinstance(item, tuple) else (item, hbm) for item in inputs]
    out_specs = [
        hbm if manual else pl.BlockSpec(shape, lambda i, c, n=len(shape): (0,) * n)
        for shape, _, manual in outputs
    ]
    table = scratch_table(z)
    return pl.pallas_call(
        partial(kernel, scratch + ("sems",)),
        grid_spec=pltpu.PrefetchScalarGridSpec(
            num_scalar_prefetch=1,
            grid=(1,),
            in_specs=[spec for _, spec in inputs],
            out_specs=out_specs,
            scratch_shapes=[pltpu.VMEM(*table[name]) for name in scratch]
            + [pltpu.SemaphoreType.DMA((24,))],
        ),
        out_shape=[shaped(shape, kind) for shape, kind, _ in outputs],
        compiler_params=pltpu.CompilerParams(
            dimension_semantics=("arbitrary",), vmem_limit_bytes=vmem_bytes
        ),
        cost_estimate=pl.CostEstimate(
            flops=int(passes * 20 * z.rows * z.feats * (4 * z.feats + 2 * z.hidden)),
            bytes_accessed=int(passes * 300_000_000),
            transcendentals=0,
        ),
    )(core, *(item for item, _ in inputs))


def gradient_outputs(z, rows, chained):
    return [((rows // 2, z.feats), bf16, True)] * 2 if chained else [((rows, z.feats), bf16, True)]


def resident(items):
    return [(item, in_vmem(item)) for item in items]


def flat_pairs(pairs):
    return [item for pair in pairs for item in pair]


forward_scratch = (
    "triple", "attend", "widen", "narrow", "x_rows", "xs", "n1", "qkv", "bias", "probs", "mixed",
    "low_mix", "x1", "n2", "act", "slope", "total",
)
back_scratch = ("dy_rows", "dy", "dh", "dn2", "gx1", "mats")
attend_back_scratch = ("da", "gmix", "gqkv", "dq", "pair", "rest")


def run_forward(z, core, xs, x_plan, params, base):
    inputs = list(xs) + resident(params["small"] + [base]) + flat_pairs(params["big"])
    table = scratch_table(z)
    rim = ((3, z.cols, z.feats), bf16, False)
    outputs = [(*table["x_rows"], False), rim] + [
        (*table[name], True) for name in ("qkv", "probs", "low_mix", "x1", "act", "slope")
    ]
    kernel = partial(bind, forward_kernel, (z, len(xs), x_plan))
    return call(kernel, z, core, inputs, outputs, forward_scratch, 1.2)


def bind(kernel, arguments, scratch, *refs):
    kernel(*arguments, scratch, *refs)


def run_both(z, core, xs, x_plan, dys, dy_plan, params, base, mask, prev):
    inputs = list(xs) + list(dys) + resident(params["small"] + [base, mask])
    inputs += flat_pairs(params["big"]) + ([] if prev is None else [prev])
    table = scratch_table(z)
    image = (*table["x_rows"], False)
    outputs = [image, image, ((6, z.cols, z.feats), bf16, False)]
    outputs += gradient_outputs(z, z.feed_rows + z.attend_rows, prev is not None)
    scratch = forward_scratch + back_scratch + attend_back_scratch + ("smalls",)
    if prev is not None:
        scratch += ("prev_mats", "prev_rest")
    arguments = (z, len(xs), x_plan, len(dys), dy_plan, prev is not None)
    return call(partial(bind, both_kernel, arguments), z, core, inputs, outputs, scratch, 4.0)


def run_feed_back(z, core, dys, dy_plan, params, kept, prev):
    inputs = list(dys) + resident(params["small"]) + flat_pairs(params["big"][2:]) + list(kept)
    if prev:
        inputs += [prev[0]] + resident(prev[1:])
    table = scratch_table(z)
    outputs = [(*table["gx1"], True), (*table["smalls"], False)]
    outputs += gradient_outputs(z, z.feed_rows, bool(prev))
    scratch = back_scratch + ("widen", "narrow", "x1", "n2", "act", "slope", "total")
    if prev:
        scratch += ("prev_mats",)
    arguments = (z, len(dys), dy_plan, bool(prev))
    return call(
        partial(bind, feed_back_kernel, arguments), z, core, inputs, outputs, scratch, 1.2
    )


def run_attend_back(z, core, xs, x_plan, params, kept, smalls, prev, last):
    inputs = list(xs) + resident(params["small"]) + flat_pairs(params["big"][:2]) + list(kept)
    inputs += resident([smalls])
    if prev is not None:
        inputs.append(prev)
    table = scratch_table(z)
    outputs = [(*table["dq"], True) if last else (*table["x_rows"], False)]
    outputs += gradient_outputs(z, z.attend_rows, prev is not None)
    scratch = attend_back_scratch + (
        "triple", "attend", "x_rows", "xs", "n1", "qkv", "probs", "low_mix", "gx1", "dn2",
    )
    if prev is not None:
        scratch += ("prev_rest",)
    arguments = (z, len(xs), x_plan, prev is not None, last)
    return call(
        partial(bind, attend_back_kernel, arguments), z, core, inputs, outputs, scratch, 1.5
    )


def run_input(z, core, xs, x_plan, params, kept):
    inputs = list(xs) + resident(params["small"]) + flat_pairs(params["big"][:1]) + list(kept)
    scratch = ("triple", "x_rows", "xs", "gx1", "dq", "dn2")
    arguments = (z, len(xs), x_plan)
    outputs = [(*scratch_table(z)["x_rows"], False)]
    return call(partial(bind, input_kernel, arguments), z, core, inputs, outputs, scratch, 0.4)[0]


def run_unpack(z, core, value0, arrived0, value1, arrived1):
    feats, hidden = z.feats, z.hidden
    outputs = [
        ((1, feats, 3 * feats), f32, True),
        ((1, feats, feats), f32, True),
        ((1, feats, hidden), f32, True),
        ((1, hidden, feats), f32, True),
    ]
    outputs += [((1, feats), f32, False)] * 7
    outputs += [((1, hidden), f32, False), ((1, feats), f32, False)]
    outputs.append((*scratch_table(z)["pair"], False))
    scratch = ("all_rows", "v_triple", "v_attend", "v_widen", "v_narrow")
    kernel = partial(bind, unpack_kernel, (z,))
    return call(kernel, z, core, [value0, arrived0, value1, arrived1], outputs, scratch, 0.2)


def pair_index():
    place = np.arange(tall)
    u, w = place // 8, place % 8
    real = (u < 7) & (w < 7)
    index = (u[None, :] - u[:, None] + 6) * 13 + (w[None, :] - w[:, None] + 6)
    return np.where(real[:, None] & real[None, :], index, 169)[:cells]


def pair_onehot():
    return jnp.asarray(
        np.arange(169)[:, None] == pair_index().reshape(-1)[None, :], bf16
    )


def bias_base(table, z):
    spread = lax.dot_general(
        table, pair_onehot(), (((0,), (0,)), ((), ())), preferred_element_type=f32
    )
    spread = spread.reshape(z.groups, -1, cells, tall).transpose(0, 2, 1, 3)
    real = (np.arange(cells) % 8 < 7)[None, :, None, None]
    return (
        jnp.where(real, spread, masked_score).astype(bf16).reshape(z.groups, cells, z.lanes)
    )


def region_mask(z, step, first_row, total_rows):
    place = np.arange(tall)
    u, w = np.minimum(place // 8, 6), np.minimum(place % 8, 6)
    rows = jnp.mod(first_row + step * 7 + u + 3, total_rows)
    vertical = (rows >= total_rows - 7).astype(jnp.int32) + (rows >= total_rows - 3)
    kinds = []
    for column in (0, z.wins - 2, z.wins - 1):
        at = np.mod(column * 7 + w + 3, z.cols)
        horizontal = (at >= z.cols - 7).astype(np.int32) + (at >= z.cols - 3)
        code = vertical * 3 + horizontal
        alike = code[:cells, None] == code[None, :]
        kinds.append(jnp.where(alike, 0.0, masked_score).astype(f32))
    return jnp.stack(kinds)


def table_slope(pair, z, heads):
    pair = pair.reshape(z.groups, cells, -1, tall).transpose(1, 3, 0, 2).reshape(-1, heads)
    return mm(pair_onehot(), pair.astype(bf16))


def swap_cores(item):
    return lax.ppermute(item, "pipe", [(0, 1), (1, 0)])


def take(pair, index):
    return lax.dynamic_index_in_dim(pair, index, 0, keepdims=False)


def tie(item, *others):
    return lax.optimization_barrier((item,) + others)


class Reduction:
    near = 4

    def __init__(self, kept, sent=None):
        if sent is not None:
            kept = (kept.astype(f32) + swap_cores(sent).astype(f32)).astype(bf16)
        self.value = kept

    def partners(self, near):
        count, place = lax.axis_size("rows"), lax.axis_index("rows")
        size, unit = (self.near, 1) if near else (count // self.near, self.near)
        mine = (place // unit) % size
        return size, mine, [[(i, i ^ (d * unit)) for i in range(count)] for d in range(1, size)]

    def scatter(self, near):
        size, mine, routes = self.partners(near)
        parts = self.value.reshape((size, -1) + self.value.shape[1:])
        arrived = [
            lax.ppermute(take(parts, mine ^ d), "rows", route)
            for d, route in enumerate(routes, 1)
        ]
        total = take(parts, mine).astype(f32)
        for item in arrived:
            total = total + item.astype(f32)
        self.value = total.astype(bf16)

    def gather(self, near):
        size, mine, routes = self.partners(near)
        arrived = [lax.ppermute(self.value, "rows", route) for route in routes]
        parts = jnp.zeros((size,) + self.value.shape, bf16)
        for d, item in enumerate([self.value] + arrived):
            parts = lax.dynamic_update_index_in_dim(parts, item, mine ^ d, 0)
        self.value = parts.reshape((-1,) + self.value.shape[1:])

    def join(self, other):
        return Reduction(jnp.concatenate([self.value, other.value], 0))


def on_device(
    image_tokens,
    out_grad,
    first_gain,
    first_shift,
    triple_weight,
    query_bias,
    value_bias,
    bias_table,
    attend_weight,
    attend_bias,
    second_gain,
    second_shift,
    widen_weight,
    widen_bias,
    narrow_weight,
    narrow_bias,
):
    core = lax.axis_index("pipe")
    core_id = core.astype(jnp.int32).reshape(1)
    count = lax.axis_size("rows")
    place = lax.axis_index("rows")
    batches, own_rows, cols, feats = image_tokens.shape
    heads = bias_table.shape[2]
    hidden = widen_weight.shape[2]
    z = Sizes(own_rows, cols, feats, hidden, heads)
    total_rows = own_rows * count
    first_row = place * own_rows

    small = jnp.concatenate(
        [
            first_gain,
            first_shift,
            query_bias,
            jnp.zeros_like(query_bias),
            value_bias,
            attend_bias,
            second_gain,
            second_shift,
            narrow_bias,
            widen_bias.reshape(-1, feats),
            jnp.zeros((small_rows - 9 - hidden // feats, feats), bf16),
        ],
        0,
    ).astype(f32)
    tables = [bias_table[0], swap_cores(bias_table[0])]
    first = core == 0
    big = (triple_weight, attend_weight, widen_weight, narrow_weight)
    params = {
        "small": [small, swap_cores(small)],
        "big": [(item, swap_cores(item)) for item in big],
    }
    to_previous = [((i + 1) % count, i) for i in range(count)]
    to_next = [(i, (i + 1) % count) for i in range(count)]
    base0 = bias_base(jnp.where(first, tables[0], tables[1]), z)

    upper = [(0, True, 0, 7)]
    lower = [(0, True, 7, 7)]

    y00, y0_rim, *kept0 = run_forward(z, core_id, [image_tokens], upper, params, base0)
    y0_halo = lax.ppermute(y0_rim, "rows", to_previous)
    late_grad, late_row, late_table, _ = tie(
        out_grad, first_row, jnp.where(first, tables[1], tables[0]), y00
    )
    grad_top = lax.dynamic_slice(late_grad, (core, 0, 0, 0), (1, 3) + late_grad.shape[2:])
    grad_halo = lax.ppermute(grad_top[0], "rows", to_previous)
    masks = [region_mask(z, step, late_row, total_rows) for step in range(2)]
    base1 = bias_base(late_table, z)
    y01, _, *kept1 = run_forward(z, core_id, [image_tokens], lower, params, base0)
    (qkv0, probs0, mix0, x10, act0, slope0) = kept0
    (qkv1, probs1, mix1, x11, act1, slope1) = kept1

    y10, dx10, _, all10 = run_both(
        z, core_id, [y00, y01], [(0, False, 3, 4), (1, False, 0, 3)], [out_grad],
        [(0, True, 3, 7)], params, base1, masks[0], None,
    )
    y11, dx11, rim1, *all11 = run_both(
        z, core_id, [y01, y0_halo], [(0, False, 3, 4), (1, False, 0, 3)],
        [out_grad, grad_halo], [(0, True, 10, 4), (1, False, 0, 3)], params, base1, masks[1],
        all10,
    )
    halo1 = lax.ppermute(rim1, "rows", to_next)

    def sent(block0, block1):
        return swap_cores(jnp.where(first, block1, block0))

    def arranged(block0, block1, other):
        return jnp.where(first, jnp.stack([block0, other]), jnp.stack([other, block1]))[None]

    reduction1 = Reduction(*all11)

    gx01, small01, mats01 = run_feed_back(
        z, core_id, [dx10, dx11], [(0, False, 4, 3), (1, False, 0, 4)], params,
        [x11, act1, slope1], None,
    )
    halo1, reduction1.value = tie(halo1, reduction1.value)
    reduction1.scatter(True)
    gx00, small00, *mats00 = run_feed_back(
        z, core_id, [halo1, dx10], [(0, False, 0, 3), (1, False, 0, 4)], params,
        [x10, act0, slope0], (mats01, small01),
    )
    gx01, reduction1.value = tie(gx01, reduction1.value)
    reduction1.scatter(False)
    feed0 = Reduction(*mats00)
    dx01, rest01 = run_attend_back(
        z, core_id, [image_tokens], lower, params, [gx01, qkv1, probs1, mix1],
        jnp.zeros((small_rows, feats), f32), None, False,
    )
    gx00, reduction1.value, feed0.value = tie(gx00, reduction1.value, feed0.value)
    feed0.scatter(True)
    dq00, *rest00 = run_attend_back(
        z, core_id, [image_tokens], upper, params, [gx00, qkv0, probs0, mix0], small00, rest01,
        True,
    )
    rest00[0], feed0.value = tie(rest00[0], feed0.value)
    reduction1.gather(False)
    reduction1.gather(True)
    arrived1 = lax.ppermute(reduction1.value, "pipe", [(0, 1)])
    rest0 = Reduction(*rest00)
    dx00 = run_input(z, core_id, [image_tokens], upper, params, [gx00, dq00])
    rest0.value, y00, y01, y10, y11, dx10, dx11, halo1 = tie(
        rest0.value, y00, y01, y10, y11, dx10, dx11, halo1
    )
    hidden_out = jnp.concatenate([y00, y01], 0)
    final = jnp.concatenate([halo1[3:], y10, y11[:4]], 0)
    entry_grad = jnp.concatenate([halo1[:3], dx10, dx11[:4]], 0)
    image_grad = jnp.concatenate([dx00, dx01], 0)
    block_outputs = arranged(hidden_out, final, sent(hidden_out, final))
    input_grads = arranged(image_grad, entry_grad, sent(image_grad, entry_grad))

    rest0.scatter(True)
    rest0.value, block_outputs, input_grads = tie(rest0.value, block_outputs, input_grads)
    reduction = feed0.join(rest0)
    reduction.scatter(False)
    reduction.gather(False)
    reduction.gather(True)

    arrived0 = lax.ppermute(reduction.value, "pipe", [(1, 0)])
    (t_triple, t_attend, t_widen, t_narrow, t_gain1, t_shift1, t_query_b, t_value_b,
     t_attend_b, t_gain2, t_shift2, t_widen_b, t_narrow_b, pair) = run_unpack(
        z, core_id, reduction.value, arrived0, reduction1.value, arrived1
    )

    return (
        block_outputs,
        input_grads,
        t_gain1,
        t_shift1,
        t_triple,
        t_query_b,
        t_value_b,
        table_slope(pair, z, heads)[None],
        t_attend,
        t_attend_b,
        t_gain2,
        t_shift2,
        t_widen,
        t_widen_b,
        t_narrow,
        t_narrow_b,
    )


def solution(mesh):
    param_specs = [
        P("pipe", None),
        P("pipe", None),
        P("pipe", None, None),
        P("pipe", None),
        P("pipe", None),
        P("pipe", None, None),
        P("pipe", None, None),
        P("pipe", None),
        P("pipe", None),
        P("pipe", None),
        P("pipe", None, None),
        P("pipe", None),
        P("pipe", None, None),
        P("pipe", None),
    ]
    in_specs = (P(None, "rows", None, None),) * 2 + tuple(param_specs)
    out_specs = (P("pipe", None, "rows", None, None),) * 2 + tuple(param_specs)
    return jax.shard_map(
        on_device, mesh=mesh, in_specs=in_specs, out_specs=out_specs, check_vma=False
    )
```

```python
from functools import partial

import jax
import jax.numpy as jnp
import numpy as np
from jax import lax
from jax.experimental import pallas as pl
from jax.experimental.pallas import tpu as pltpu
from jax.sharding import PartitionSpec as P

f32 = jnp.float32
bf16 = jnp.bfloat16
epsilon = 1e-05
masked_score = -1e30
vmem_bytes = 60 * 1024 * 1024
cells = 56
tall = 64

gain1_row, shift1_row, query_bias_row, value_bias_row = 0, 1, 2, 4
attend_bias_row, gain2_row, shift2_row, narrow_bias_row, widen_bias_row = 5, 6, 7, 8, 9
s_gain1, s_shift1, s_attend_b, s_gain2, s_shift2, s_narrow_b, s_widen_b = 3, 4, 5, 6, 7, 8, 9
small_rows = 16


def mm(left, right):
    return lax.dot_general(left, right, (((1,), (0,)), ((), ())), preferred_element_type=f32)


def mm_t(left, right):
    return lax.dot_general(left, right, (((1,), (1,)), ((), ())), preferred_element_type=f32)


def t_mm(left, right):
    return lax.dot_general(left, right, (((0,), (0,)), ((), ())), preferred_element_type=f32)


def normed_parts(values):
    center = values - jnp.mean(values, -1, keepdims=True)
    spread = jnp.mean(center * center, -1, keepdims=True)
    scale = lax.rsqrt(spread + epsilon)
    return center * scale, scale


def norm_back(grad, hat, scale, gain):
    pulled = grad * gain
    return scale * (
        pulled
        - jnp.mean(pulled, -1, keepdims=True)
        - hat * jnp.mean(pulled * hat, -1, keepdims=True)
    )


def gelu_parts(value):
    below = 0.5 + 0.5 * lax.erf(value * 0.5**0.5)
    bell = jnp.exp(value * value * -0.5)
    return value * below, below + value * bell * (2.0 * np.pi) ** -0.5


def row_sum(values):
    return jnp.sum(values, 0, keepdims=True)


def head_masks(depth):
    place = lax.broadcasted_iota(jnp.int32, (1, 128), 1) // depth
    return [(place == h) for h in range(128 // depth)]


def spread_heads(part, masks):
    return jnp.concatenate([part * m.astype(bf16) for m in masks], 0)


def collect_heads(high, masks):
    rows = high.shape[0] // len(masks)
    out = high[:rows]
    for h in range(1, len(masks)):
        out = jnp.where(masks[h], high[h * rows : (h + 1) * rows], out)
    return out


def pad_rows(values, rows):
    return jnp.concatenate(
        [values, jnp.zeros((rows - values.shape[0], values.shape[1]), values.dtype)], 0
    )


def spread_matrix(cols, roll_by):
    place = lax.broadcasted_iota(jnp.int32, (cols // 7 * 8, cols), 0)
    column = lax.broadcasted_iota(jnp.int32, (cols // 7 * 8, cols), 1)
    w = place & 7
    target = (place >> 3) * 7 + w + roll_by
    target = jnp.where(target >= cols, target - cols, target)
    return jnp.where((target == column) & (w < 7), 1.0, 0.0).astype(bf16)


def image_to_windows(image, spread, out):
    for u in range(7):
        part = mm(spread, image[u])
        out[:, u * 8 : (u + 1) * 8, :] = part.reshape(-1, 8, part.shape[-1])


def windows_to_image(windows, spread, image, rim=None, first=0):
    wins, _, feats = windows.shape
    for u in range(7):
        part = windows[:, u * 8 : (u + 1) * 8, :].reshape(wins * 8, feats).astype(bf16)
        row = t_mm(spread, part).astype(bf16)
        image[u] = row
        if rim is not None and first <= u < first + 3:
            rim[u - first] = row


def by_rows(rows, parts, step):
    size = rows // parts

    def body(i, carry):
        step(i, pl.ds(pl.multiple_of(i * size, size), size))
        return carry

    lax.fori_loop(0, parts, body, 0)


class Copies:
    def __init__(self, core_ref, block, sems):
        self.core = core_ref[0]
        self.mine = self.core == block
        self.sems = sems
        self.count = 0
        self.writes = []

    def next(self):
        self.count += 1
        return self.sems.at[self.count - 1]

    def start(self, source, target):
        copy = pltpu.make_async_copy(source, target, self.next())
        copy.start()
        return copy

    def pick(self, pair, target):
        own, other = pair
        sem = self.next()

        @pl.when(self.mine)
        def _():
            pltpu.make_async_copy(own.at[0], target, sem).start()

        @pl.when(jnp.logical_not(self.mine))
        def _():
            pltpu.make_async_copy(other.at[0], target, sem).start()

        return pltpu.make_async_copy(own.at[0], target, sem)

    def rows(self, refs, plan, target):
        at = 0
        copies = []
        for which, batched, first, size in plan:
            source = refs[which].at[self.core] if batched else refs[which]
            copies.append(
                self.start(source.at[pl.ds(first, size)], target.at[pl.ds(at, size)])
            )
            at += size
        return copies

    def write(self, source, target):
        self.writes.append(self.start(source, target))

    def write_rows(self, source, at, outs):
        size = source.shape[0]
        if len(outs) == 1:
            self.write(source, outs[0].at[pl.ds(at, size)])
            return
        half = outs[0].shape[0]
        low = at
        while low < at + size:
            which = low // half
            high = min(at + size, (which + 1) * half)
            part = source.at[pl.ds(low - at, high - low)]
            keep, send = (out.at[pl.ds(low - which * half, high - low)] for out in outs)
            sem = self.next()
            pl.when(self.core == which)(pltpu.make_async_copy(part, keep, sem).start)
            pl.when(self.core != which)(pltpu.make_async_copy(part, send, sem).start)
            self.writes.append(pltpu.make_async_copy(part, keep, sem))
            low = high

    def finish(self):
        for copy in self.writes:
            copy.wait()

    def small(self, own, other):
        return jnp.where(self.mine, own[...], other[...])


def wait_all(copies):
    for copy in copies:
        copy.wait()


def stage_norm(xs, gain, shift, n1, kept=None):
    wins, _, feats = xs.shape

    def step(i, span):
        hat, scale = normed_parts(xs[pl.ds(i * 4, 4)].reshape(4 * cells, feats))
        if n1 is not None:
            n1[span, :] = (hat * gain + shift).astype(bf16)
        if kept is not None:
            kept[0][span, :] = hat.astype(bf16)
            kept[1][span, :] = scale

    by_rows(wins * cells, wins // 4, step)


def stage_triple(n1, triple, small, qkv):
    wins, _, width = qkv.shape
    feats = width // 3
    qkv[:, cells:, :] = jnp.zeros((wins, tall - cells, width), bf16)
    offsets = (query_bias_row, None, value_bias_row)
    for j in range(3):
        lanes = slice(j * feats, (j + 1) * feats)
        part = mm(n1[...], triple[:, lanes])
        if offsets[j] is not None:
            part = part + small[offsets[j] : offsets[j] + 1]
        qkv[:, :cells, lanes] = part.reshape(wins, cells, feats).astype(bf16)


def stage_attend(qkv, bias, probs, mixed, depth, shifted):
    wins, _, width = qkv.shape
    feats = width // 3
    masks = head_masks(depth)
    scale = depth**-0.5

    def step(w, carry):
        kind = jnp.maximum(w - (wins - 3), 0) if shifted else 0
        for g in range(feats // 128):
            at = g * 128
            q = qkv[w, :, at : at + 128]
            k = qkv[w, :, feats + at : feats + at + 128]
            v = qkv[w, :, 2 * feats + at : 2 * feats + at + 128]
            scores = mm_t(k, spread_heads(q, masks))[:cells] * scale + bias[kind, g]
            powers = jnp.exp(scores - jnp.max(scores, 0, keepdims=True))
            weights = powers * (1.0 / jnp.sum(powers, 0, keepdims=True))
            low = pad_rows(weights, tall).astype(bf16)
            probs[w, g] = low
            mixed[w, :, at : at + 128] = collect_heads(t_mm(low, v), masks)[:cells]
        return carry

    lax.fori_loop(0, wins, step, 0, unroll=16)


def forward_stages(z, block, copies, c, small, bias_parts, picks, x_waits):
    rows, feats = c.x1.shape
    base, mask = bias_parts
    base = base[...].astype(f32)
    if block == 1:
        for kind in range(3):
            for g in range(z.groups):
                c.bias[kind, g] = base[g] + jnp.concatenate(
                    [mask[kind]] * (z.lanes // tall), 1
                )
    else:
        c.bias[0] = base
    wait_all(x_waits)
    image_to_windows(c.x_rows, c.spread, c.xs)
    gain1 = small[gain1_row : gain1_row + 1]
    shift1 = small[shift1_row : shift1_row + 1]
    kept = (c.hat1, c.scale1) if hasattr(c, "hat1") else None
    stage_norm(c.xs, gain1, shift1, c.n1, kept)
    picks[0].wait()
    stage_triple(c.n1, c.triple, small, c.qkv)
    yield
    stage_attend(c.qkv, c.bias, c.probs, c.mixed, z.depth, block == 1)
    c.low_mix[...] = c.mixed[...].reshape(rows, feats).astype(bf16)
    yield
    picks[1].wait()
    c.x1[...] = (
        c.xs[...].reshape(rows, feats)
        + mm(c.low_mix[...], c.attend[...])
        + small[attend_bias_row : attend_bias_row + 1]
    )
    yield
    second_norm(small, c)
    picks[2].wait()
    part = z.hidden // z.parts
    for j in range(z.parts):
        lanes = slice(j * part, (j + 1) * part)
        offset = jnp.concatenate(
            [
                small[widen_bias_row + i : widen_bias_row + i + 1]
                for i in range(j * part // feats, (j + 1) * part // feats)
            ],
            1,
        )
        value, pull = gelu_parts(mm(c.n2[...], c.widen[:, lanes]) + offset)
        c.act[:, lanes] = value.astype(bf16)
        c.slope[:, lanes] = pull.astype(bf16)
    yield
    picks[3].wait()
    c.total[...] = (
        c.x1[...]
        + mm(c.act[...], c.narrow[...])
        + small[narrow_bias_row : narrow_bias_row + 1]
    ).reshape(c.total.shape)


def second_norm(small, c):
    gain2 = small[gain2_row : gain2_row + 1]
    shift2 = small[shift2_row : shift2_row + 1]

    def norm_step(i, span):
        hat, scale = normed_parts(c.x1[span, :])
        c.n2[span, :] = (hat * gain2 + shift2).astype(bf16)
        if hasattr(c, "hat2"):
            c.hat2[span, :] = hat.astype(bf16)
            c.scale2[span, :] = scale

    by_rows(c.x1.shape[0], 4, norm_step)


def feed_back_stages(z, copies, c, small, waits, prev, outs, o_small):
    rows, feats = c.x1.shape
    w_dy, w_narrow, w_slope, w_widen, w_x1, w_act, w_prev = waits
    wait_all(w_dy)
    image_to_windows(c.dy_rows, c.spread, c.total)
    c.dy[...] = c.total[...].reshape(rows, feats).astype(bf16)
    sums = {s_narrow_b: row_sum(c.total[...].reshape(rows, feats))}
    part = z.hidden // z.parts
    wait_all(w_narrow + w_slope)
    for j in range(z.parts):
        lanes = slice(j * part, (j + 1) * part)
        grad = mm_t(c.dy[...], c.narrow[lanes, :]) * c.slope[:, lanes].astype(f32)
        total = row_sum(grad)
        for i in range(part // feats):
            sums[s_widen_b + j * part // feats + i] = total[:, i * feats : (i + 1) * feats]
        c.dh[:, lanes] = grad.astype(bf16)
    wait_all(w_widen + w_x1)
    if w_x1:
        second_norm(small, c)
    c.dn2[...] = mm_t(c.dh[...], c.widen[...])
    gain2 = small[gain2_row : gain2_row + 1]

    def norm_step(i, span):
        hat, scale = c.hat2[span, :].astype(f32), c.scale2[span, :]
        grad = c.dn2[span, :]
        o_small[s_gain2 : s_gain2 + 1] += row_sum(grad * hat)
        o_small[s_shift2 : s_shift2 + 1] += row_sum(grad)
        c.gx1[span, :] = c.dy[span, :].astype(f32) + norm_back(grad, hat, scale, gain2)

    for at, value in sums.items():
        o_small[at : at + 1] += value
    by_rows(rows, 4, norm_step)
    yield
    wait_all(w_prev)

    def put(at, value):
        span = slice(at, at + feats)
        if prev is not None:
            value = value + prev[span, :].astype(f32)
        c.mats[span, :] = value.astype(bf16)

    for j in range(z.hidden // feats):
        put(j * feats, t_mm(c.n2[...], c.dh[:, j * feats : (j + 1) * feats]))
    half = c.mats.shape[0] // 2
    copies.write_rows(c.mats.at[pl.ds(0, half)], 0, outs)
    wait_all(w_act)
    for j in range(z.hidden // feats):
        put(z.hidden + j * feats, t_mm(c.act[:, j * feats : (j + 1) * feats], c.dy[...]))
    copies.write_rows(c.mats.at[pl.ds(half, half)], half, outs)


def attend_back_stages(z, copies, c, small, waits, prev, outs, first_row, smalls):
    w_gx1, w_attend, w_mix, w_qkv, w_x, w_triple, w_prev = waits
    wins, _, feats = c.xs.shape
    rows = wins * cells
    depth = z.depth
    masks = head_masks(depth)
    scale = depth**-0.5
    mats = 4 * feats
    qkv, probs, gmix, gqkv, pair = c.qkv, c.probs, c.gmix, c.gqkv, c.pair
    wait_all(w_gx1)
    c.da[...] = c.gx1[...].astype(bf16)
    attend_b = row_sum(c.gx1[...])
    wait_all(w_attend)
    gmix[:, cells:, :] = jnp.zeros((wins, tall - cells, feats), bf16)
    gmix[:, :cells, :] = mm_t(c.da[...], c.attend[...]).reshape(wins, cells, feats).astype(bf16)
    pair[...] = jnp.zeros_like(pair)
    wait_all(w_qkv)

    def step(w, carry):
        for g in range(feats // 128):
            at = g * 128
            q = qkv[w, :, at : at + 128]
            k = qkv[w, :, feats + at : feats + at + 128]
            v = qkv[w, :, 2 * feats + at : 2 * feats + at + 128]
            wide = spread_heads(gmix[w, :, at : at + 128], masks)
            low = probs[w, g]
            high = low.astype(f32)[:cells]
            pulled = mm_t(v, wide)[:cells] * high
            ds = pulled - high * jnp.sum(pulled, 0, keepdims=True)
            pair[g] += ds
            ds = pad_rows(ds, tall).astype(bf16)
            gqkv[w, :, 2 * feats + at : 2 * feats + at + 128] = mm(low, wide)[:cells]
            gqkv[w, :, feats + at : feats + at + 128] = (
                mm(ds, spread_heads(q, masks))[:cells] * scale
            )
            gqkv[w, :, at : at + 128] = collect_heads(t_mm(ds, k), masks)[:cells] * scale
        return carry

    lax.fori_loop(0, wins, step, 0, unroll=16)
    gain1 = small[gain1_row : gain1_row + 1]
    shift1 = small[shift1_row : shift1_row + 1]
    if w_x:
        wait_all(w_x)
        image_to_windows(c.x_rows, c.spread, c.xs)
        stage_norm(c.xs, None, None, None, (c.hat1, c.scale1))
    wait_all(w_triple + w_mix + w_prev)

    def put(at, size, value):
        if prev is not None:
            value = value + prev[at : at + size, :].astype(f32)
        c.rest[at : at + size, :] = value.astype(bf16)

    put(3 * feats, feats, t_mm(c.low_mix[...], c.da[...]))
    columns = jnp.concatenate([gain1, shift1, jnp.zeros((6, feats), f32)], 0).T
    gain_column, shift_column = columns[:, 0:1], columns[:, 1:2]
    sums = []
    gain_grad = jnp.zeros((feats, 1), f32)
    shift_grad = jnp.zeros((8, feats), f32)
    for j in range(3):
        lanes = slice(j * feats, (j + 1) * feats)
        part = gqkv[:, :, lanes].reshape(rows, feats)
        total = row_sum(part)
        sums.append(total)
        c.dq[:, lanes] = part.astype(bf16)
        both = t_mm(c.hat1[...], c.dq[:, lanes])
        put(j * feats, feats, gain_column * both + shift_column * total)
        gain_grad += jnp.sum(both * c.triple[:, lanes].astype(f32), -1, keepdims=True)
        top = total.astype(bf16)
        rest = (total - top.astype(f32)).astype(bf16)
        shift_grad += mm_t(
            jnp.concatenate([top.astype(f32), rest.astype(f32), jnp.zeros((6, feats), f32)], 0)
            .astype(bf16),
            c.triple[:, lanes],
        )
    sums.append(jnp.broadcast_to(gain_grad, (feats, 8)).T[0:1])
    sums.append(shift_grad[0:1] + shift_grad[1:2])
    sums.append(attend_b)
    put(
        mats,
        small_rows,
        smalls[...] + jnp.concatenate(sums + [jnp.zeros((small_rows - 6, feats), f32)], 0),
    )
    flat = pair[...].reshape(z.groups * cells, z.lanes)
    cut = flat.shape[0] * z.lanes // feats
    more = flat[cut:]
    put(
        mats + small_rows,
        cut,
        jnp.concatenate([flat[:cut], jnp.concatenate([more[:, :128], more[:, 128:]], 0)], 1),
    )
    end = mats + small_rows + cut
    c.rest[end:, :] = jnp.zeros((c.rest.shape[0] - end, feats), bf16)
    copies.write_rows(c.rest, first_row, outs)


def input_stages(z, c, small):
    wins, _, feats = c.xs.shape
    gain1 = small[gain1_row : gain1_row + 1]
    c.dn2[...] = mm_t(c.dq[...], c.triple[...])

    def norm_step(i, span):
        wide = pl.ds(i * 4, 4)
        hat, scale = c.hat1[span, :].astype(f32), c.scale1[span, :]
        out = c.gx1[span, :] + norm_back(c.dn2[span, :], hat, scale, gain1)
        c.xs[wide] = out.reshape(4, cells, feats)

    by_rows(wins * cells, wins // 4, norm_step)


class Refs:
    def __init__(self, refs, names):
        self.refs = list(refs)
        for name in names:
            setattr(self, name, self.refs.pop(0))

    def several(self, number):
        return [self.refs.pop(0) for _ in range(number)]

    def pairs(self, number):
        return [tuple(self.several(2)) for _ in range(number)]

    def name(self, names):
        for name in names:
            setattr(self, name, self.refs.pop(0))


def forward_kernel(z, n_x, x_plan, scratch, core_ref, *refs):
    c = Refs(refs, ())
    x_refs = c.several(n_x)
    c.name(("own", "other", "base"))
    big = c.pairs(4)
    c.name(("y", "rim", "o_qkv", "o_probs", "o_mix", "o_x1", "o_act", "o_slope"))
    c.name(scratch)
    copies = Copies(core_ref, 0, c.sems)
    x_waits = copies.rows(x_refs, x_plan, c.x_rows)
    picks = [copies.pick(p, to) for p, to in zip(big, (c.triple, c.attend, c.widen, c.narrow))]
    small = copies.small(c.own, c.other)
    c.spread = spread_matrix(z.cols, 0)
    stages = forward_stages(z, 0, copies, c, small, (c.base, None), picks, x_waits)
    next(stages)
    copies.write(c.qkv, c.o_qkv)
    next(stages)
    copies.write(c.probs, c.o_probs)
    copies.write(c.low_mix, c.o_mix)
    next(stages)
    copies.write(c.x1, c.o_x1)
    next(stages)
    copies.write(c.act, c.o_act)
    copies.write(c.slope, c.o_slope)
    for _ in stages:
        pass
    windows_to_image(c.total, c.spread, c.y, c.rim, 0)
    copies.finish()


def both_kernel(z, n_x, x_plan, n_dy, dy_plan, chained, scratch, core_ref, *refs):
    c = Refs(refs, ())
    x_refs = c.several(n_x)
    dy_refs = c.several(n_dy)
    c.name(("own", "other", "base", "mask"))
    big = c.pairs(4)
    prev = c.several(1) if chained else None
    c.name(("y", "dx", "rim"))
    outs = c.several(2 if chained else 1)
    c.name(scratch)
    copies = Copies(core_ref, 1, c.sems)
    x_waits = copies.rows(x_refs, x_plan, c.x_rows)
    picks = [copies.pick(p, to) for p, to in zip(big, (c.triple, c.attend, c.widen, c.narrow))]
    dy_waits = copies.rows(dy_refs, dy_plan, c.dy_rows)
    prev_waits = [[], []]
    if chained:
        parts = ((0, c.prev_mats), (z.feed_rows, c.prev_rest))
        prev_waits = [
            [copies.start(prev[0].at[pl.ds(at, to.shape[0])], to)] for at, to in parts
        ]
    prev_refs = (c.prev_mats, c.prev_rest) if chained else (None, None)
    small = copies.small(c.own, c.other)
    c.spread = spread_matrix(z.cols, 3)
    c.smalls[...] = jnp.zeros_like(c.smalls)
    for _ in forward_stages(z, 1, copies, c, small, (c.base, c.mask), picks, x_waits):
        pass
    windows_to_image(c.total, c.spread, c.y, c.rim.at[pl.ds(3, 3)], 4)
    waits = (dy_waits, [], [], [], [], [], prev_waits[0])
    for _ in feed_back_stages(z, copies, c, small, waits, prev_refs[0], outs, c.smalls):
        pass
    waits = ([], [], [], [], [], [], prev_waits[1])
    attend_back_stages(z, copies, c, small, waits, prev_refs[1], outs, z.feed_rows, c.smalls)
    input_stages(z, c, small)
    windows_to_image(c.xs, c.spread, c.dx, c.rim.at[pl.ds(0, 3)], 4)
    copies.finish()


def feed_back_kernel(z, n_dy, dy_plan, chained, scratch, core_ref, *refs):
    c = Refs(refs, ())
    dy_refs = c.several(n_dy)
    c.name(("own", "other"))
    big = c.pairs(2)
    kept = c.several(3)
    prev = c.several(2) if chained else None
    c.name(("o_gx1", "o_small"))
    outs = c.several(2 if chained else 1)
    c.name(scratch)
    copies = Copies(core_ref, 0, c.sems)
    w_dy = copies.rows(dy_refs, dy_plan, c.dy_rows)
    w_narrow = copies.pick(big[1], c.narrow)
    w_slope = copies.start(kept[2], c.slope)
    w_widen = copies.pick(big[0], c.widen)
    w_x1 = copies.start(kept[0], c.x1)
    w_act = copies.start(kept[1], c.act)
    w_prev = [copies.start(prev[0], c.prev_mats)] if chained else []
    small = copies.small(c.own, c.other)
    c.spread = spread_matrix(z.cols, 0)
    c.o_small[...] = prev[1][...] if chained else jnp.zeros_like(c.o_small)
    waits = (w_dy, [w_narrow], [w_slope], [w_widen], [w_x1], [w_act], w_prev)
    stages = feed_back_stages(
        z, copies, c, small, waits, c.prev_mats if chained else None, outs, c.o_small
    )
    next(stages)
    copies.write(c.gx1, c.o_gx1)
    for _ in stages:
        pass
    copies.finish()


def attend_back_kernel(z, n_x, x_plan, chained, last, scratch, core_ref, *refs):
    c = Refs(refs, ())
    x_refs = c.several(n_x)
    c.name(("own", "other"))
    big = c.pairs(2)
    kept = c.several(4)
    c.name(("smalls",))
    prev = c.several(1) if chained else None
    c.name(("out",))
    outs = c.several(2 if chained else 1)
    c.name(scratch)
    copies = Copies(core_ref, 0, c.sems)
    w_gx1 = copies.start(kept[0], c.gx1)
    w_attend = copies.pick(big[1], c.attend)
    w_qkv = [copies.start(kept[1], c.qkv), copies.start(kept[2], c.probs)]
    w_x = copies.rows(x_refs, x_plan, c.x_rows)
    w_mix = copies.start(kept[3], c.low_mix)
    w_triple = copies.pick(big[0], c.triple)
    w_prev = [copies.start(prev[0], c.prev_rest)] if chained else []
    small = copies.small(c.own, c.other)
    c.spread = spread_matrix(z.cols, 0)
    waits = ([w_gx1], [w_attend], [w_mix], w_qkv, w_x, [w_triple], w_prev)
    attend_back_stages(
        z, copies, c, small, waits, c.prev_rest if chained else None, outs, 0, c.smalls
    )
    if last:
        copies.write(c.dq, c.out)
    else:
        input_stages(z, c, small)
        windows_to_image(c.xs, c.spread, c.out)
    copies.finish()


def input_kernel(z, n_x, x_plan, scratch, core_ref, *refs):
    c = Refs(refs, ())
    x_refs = c.several(n_x)
    c.name(("own", "other"))
    big = c.pairs(1)
    kept = c.several(2)
    c.name(("out",))
    c.name(scratch)
    copies = Copies(core_ref, 0, c.sems)
    w_dq = copies.start(kept[1], c.dq)
    w_triple = copies.pick(big[0], c.triple)
    w_x = copies.rows(x_refs, x_plan, c.x_rows)
    w_gx1 = copies.start(kept[0], c.gx1)
    small = copies.small(c.own, c.other)
    c.spread = spread_matrix(z.cols, 0)
    wait_all(w_x)
    image_to_windows(c.x_rows, c.spread, c.xs)
    stage_norm(c.xs, None, None, None, (c.hat1, c.scale1))
    wait_all([w_dq, w_triple, w_gx1])
    input_stages(z, c, small)
    windows_to_image(c.xs, c.spread, c.out)
    copies.finish()


def unpack_kernel(z, scratch, core_ref, *refs):
    c = Refs(refs, ("value0", "arrived0", "value1", "arrived1"))
    c.name(("triple", "attend", "widen", "narrow", "gain1", "shift1", "query_b", "value_b",
            "attend_b", "gain2", "shift2", "widen_b", "narrow_b", "pair"))
    c.name(scratch)
    copies = Copies(core_ref, 0, c.sems)
    feats, hidden = z.feats, z.hidden
    waits = [[], [], []]

    def fetch(stage, at, size, from0, from1):
        target = c.all_rows.at[pl.ds(at, size)]
        sem = copies.next()
        copy0, copy1 = (
            pltpu.make_async_copy(ref.at[pl.ds(row, size)], target, sem)
            for ref, row in (from0, from1)
        )
        pl.when(copies.mine)(copy0.start)
        pl.when(jnp.logical_not(copies.mine))(copy1.start)
        waits[stage].append(copy1)

    total = z.feed_rows + z.attend_rows
    quarters = (z.feed_rows // 8, z.attend_rows // 8)
    piece = sum(quarters)
    for half, source0 in enumerate((c.value0, c.arrived0)):
        for which, quarter in enumerate(quarters):
            for i in range(4):
                at = which * z.feed_rows + (half * 4 + i) * quarter
                row0 = i * piece + which * quarters[0]
                cuts = [at, at + quarter]
                if at < total // 2 < at + quarter:
                    cuts.insert(1, total // 2)
                for low, high in zip(cuts, cuts[1:]):
                    if low < total // 2:
                        from1 = (c.arrived1, low)
                    else:
                        from1 = (c.value1, low - total // 2)
                    stage = 2 if which else half
                    fetch(stage, low, high - low, (source0, row0 + low - at), from1)

    def rows(first, size):
        return c.all_rows[first : first + size, :].astype(f32)

    wait_all(waits[0])
    for j in range(hidden // feats):
        c.v_widen[:, j * feats : (j + 1) * feats] = rows(j * feats, feats)
    copies.write(c.v_widen, c.widen.at[0])
    wait_all(waits[1])
    c.v_narrow[...] = rows(hidden, hidden)
    copies.write(c.v_narrow, c.narrow.at[0])
    wait_all(waits[2])
    at = z.feed_rows
    for j in range(3):
        c.v_triple[:, j * feats : (j + 1) * feats] = rows(at + j * feats, feats)
    copies.write(c.v_triple, c.triple.at[0])
    c.v_attend[...] = rows(at + 3 * feats, feats)
    copies.write(c.v_attend, c.attend.at[0])
    at += 4 * feats
    smalls = rows(at, small_rows)
    for ref, row in ((c.query_b, 0), (c.value_b, 2), (c.gain1, s_gain1), (c.shift1, s_shift1),
                     (c.attend_b, s_attend_b), (c.gain2, s_gain2), (c.shift2, s_shift2),
                     (c.narrow_b, s_narrow_b)):
        ref[...] = smalls[row : row + 1]
    for j in range(hidden // feats):
        row = s_widen_b + j
        c.widen_b[:, j * feats : (j + 1) * feats] = smalls[row : row + 1]
    at += small_rows
    cut = z.groups * cells * z.lanes // feats
    flat = rows(at, cut)
    left = z.groups * cells - cut
    more = flat[:, z.lanes :]
    c.pair[...] = jnp.concatenate(
        [flat[:, : z.lanes], jnp.concatenate([more[:left], more[left:]], 1)], 0
    ).reshape(c.pair.shape)
    copies.finish()


class Sizes:
    def __init__(self, own_rows, cols, feats, hidden, heads):
        self.steps = own_rows // 7
        self.cols = cols
        self.feats = feats
        self.hidden = hidden
        self.wins = cols // 7
        self.rows = self.wins * cells
        self.depth = feats // heads
        self.groups = feats // 128
        self.lanes = 128 // self.depth * tall
        self.parts = 2
        self.feed_rows = 2 * hidden
        rows = self.feed_rows + 4 * feats + small_rows + self.groups * cells * self.lanes // feats
        self.attend_rows = -(-rows // 256) * 256 - self.feed_rows


def in_vmem(item):
    return pl.BlockSpec(item.shape, lambda i, c: (0,) * item.ndim)


hbm = pl.BlockSpec(memory_space=pl.ANY)


def shaped(shape, kind):
    return jax.ShapeDtypeStruct(shape, kind)


def scratch_table(z):
    feats, hidden, rows, wins = z.feats, z.hidden, z.rows, z.wins
    image = ((7, z.cols, feats), bf16)
    wide = ((wins, cells, feats), f32)
    low = ((rows, feats), bf16)
    high = ((rows, feats), f32)
    deep = ((rows, hidden), bf16)
    return {
        "triple": ((feats, 3 * feats), bf16),
        "attend": ((feats, feats), bf16),
        "widen": ((feats, hidden), bf16),
        "narrow": ((hidden, feats), bf16),
        "x_rows": image,
        "dy_rows": image,
        "xs": wide,
        "n1": low,
        "hat1": low,
        "hat2": low,
        "scale1": ((rows, 1), f32),
        "scale2": ((rows, 1), f32),
        "qkv": ((wins, tall, 3 * feats), bf16),
        "bias": ((3, z.groups, cells, z.lanes), f32),
        "probs": ((wins, z.groups, tall, z.lanes), bf16),
        "mixed": wide,
        "low_mix": low,
        "x1": high,
        "n2": low,
        "act": deep,
        "slope": deep,
        "total": wide,
        "dy": low,
        "dh": deep,
        "dn2": high,
        "gx1": high,
        "mats": ((z.feed_rows, feats), bf16),
        "prev_mats": ((z.feed_rows, feats), bf16),
        "smalls": ((small_rows, feats), f32),
        "da": low,
        "gmix": ((wins, tall, feats), bf16),
        "gqkv": ((wins, cells, 3 * feats), f32),
        "dq": ((rows, 3 * feats), bf16),
        "pair": ((z.groups, cells, z.lanes), f32),
        "rest": ((z.attend_rows, feats), bf16),
        "prev_rest": ((z.attend_rows, feats), bf16),
        "all_rows": ((z.feed_rows + z.attend_rows, feats), bf16),
        "v_triple": ((feats, 3 * feats), f32),
        "v_attend": ((feats, feats), f32),
        "v_widen": ((feats, hidden), f32),
        "v_narrow": ((hidden, feats), f32),
    }


def call(kernel, z, core, inputs, outputs, scratch, passes):
    inputs = [item if isinstance(item, tuple) else (item, hbm) for item in inputs]
    out_specs = [
        hbm if manual else pl.BlockSpec(shape, lambda i, c, n=len(shape): (0,) * n)
        for shape, _, manual in outputs
    ]
    table = scratch_table(z)
    return pl.pallas_call(
        partial(kernel, scratch + ("sems",)),
        grid_spec=pltpu.PrefetchScalarGridSpec(
            num_scalar_prefetch=1,
            grid=(1,),
            in_specs=[spec for _, spec in inputs],
            out_specs=out_specs,
            scratch_shapes=[pltpu.VMEM(*table[name]) for name in scratch]
            + [pltpu.SemaphoreType.DMA((24,))],
        ),
        out_shape=[shaped(shape, kind) for shape, kind, _ in outputs],
        compiler_params=pltpu.CompilerParams(
            dimension_semantics=("arbitrary",), vmem_limit_bytes=vmem_bytes
        ),
        cost_estimate=pl.CostEstimate(
            flops=int(passes * 20 * z.rows * z.feats * (4 * z.feats + 2 * z.hidden)),
            bytes_accessed=int(passes * 300_000_000),
            transcendentals=0,
        ),
    )(core, *(item for item, _ in inputs))


def gradient_outputs(z, rows, chained):
    return [((rows // 2, z.feats), bf16, True)] * 2 if chained else [((rows, z.feats), bf16, True)]


def resident(items):
    return [(item, in_vmem(item)) for item in items]


def flat_pairs(pairs):
    return [item for pair in pairs for item in pair]


forward_scratch = (
    "triple", "attend", "widen", "narrow", "x_rows", "xs", "n1", "qkv", "bias", "probs", "mixed",
    "low_mix", "x1", "n2", "act", "slope", "total",
)
back_scratch = ("dy_rows", "dy", "dh", "dn2", "gx1", "mats", "hat2", "scale2")
attend_back_scratch = ("da", "gmix", "gqkv", "dq", "pair", "rest", "hat1", "scale1")


def run_forward(z, core, xs, x_plan, params, base):
    inputs = list(xs) + resident(params["small"] + [base]) + flat_pairs(params["big"])
    table = scratch_table(z)
    rim = ((3, z.cols, z.feats), bf16, False)
    outputs = [(*table["x_rows"], False), rim] + [
        (*table[name], True) for name in ("qkv", "probs", "low_mix", "x1", "act", "slope")
    ]
    kernel = partial(bind, forward_kernel, (z, len(xs), x_plan))
    return call(kernel, z, core, inputs, outputs, forward_scratch, 1.2)


def bind(kernel, arguments, scratch, *refs):
    kernel(*arguments, scratch, *refs)


def run_both(z, core, xs, x_plan, dys, dy_plan, params, base, mask, prev):
    inputs = list(xs) + list(dys) + resident(params["small"] + [base, mask])
    inputs += flat_pairs(params["big"]) + ([] if prev is None else [prev])
    table = scratch_table(z)
    image = (*table["x_rows"], False)
    outputs = [image, image, ((6, z.cols, z.feats), bf16, False)]
    outputs += gradient_outputs(z, z.feed_rows + z.attend_rows, prev is not None)
    scratch = forward_scratch + back_scratch + attend_back_scratch + ("smalls",)
    if prev is not None:
        scratch += ("prev_mats", "prev_rest")
    arguments = (z, len(xs), x_plan, len(dys), dy_plan, prev is not None)
    return call(partial(bind, both_kernel, arguments), z, core, inputs, outputs, scratch, 4.0)


def run_feed_back(z, core, dys, dy_plan, params, kept, prev):
    inputs = list(dys) + resident(params["small"]) + flat_pairs(params["big"][2:]) + list(kept)
    if prev:
        inputs += [prev[0]] + resident(prev[1:])
    table = scratch_table(z)
    outputs = [(*table["gx1"], True), (*table["smalls"], False)]
    outputs += gradient_outputs(z, z.feed_rows, bool(prev))
    scratch = back_scratch + ("widen", "narrow", "x1", "n2", "act", "slope", "total")
    if prev:
        scratch += ("prev_mats",)
    arguments = (z, len(dys), dy_plan, bool(prev))
    return call(
        partial(bind, feed_back_kernel, arguments), z, core, inputs, outputs, scratch, 1.2
    )


def run_attend_back(z, core, xs, x_plan, params, kept, smalls, prev, last):
    inputs = list(xs) + resident(params["small"]) + flat_pairs(params["big"][:2]) + list(kept)
    inputs += resident([smalls])
    if prev is not None:
        inputs.append(prev)
    table = scratch_table(z)
    outputs = [(*table["dq"], True) if last else (*table["x_rows"], False)]
    outputs += gradient_outputs(z, z.attend_rows, prev is not None)
    scratch = attend_back_scratch + (
        "triple", "attend", "x_rows", "xs", "qkv", "probs", "low_mix", "gx1", "dn2",
    )
    if prev is not None:
        scratch += ("prev_rest",)
    arguments = (z, len(xs), x_plan, prev is not None, last)
    return call(
        partial(bind, attend_back_kernel, arguments), z, core, inputs, outputs, scratch, 1.5
    )


def run_input(z, core, xs, x_plan, params, kept):
    inputs = list(xs) + resident(params["small"]) + flat_pairs(params["big"][:1]) + list(kept)
    scratch = ("triple", "x_rows", "xs", "gx1", "dq", "dn2", "hat1", "scale1")
    arguments = (z, len(xs), x_plan)
    outputs = [(*scratch_table(z)["x_rows"], False)]
    return call(partial(bind, input_kernel, arguments), z, core, inputs, outputs, scratch, 0.4)[0]


def run_unpack(z, core, value0, arrived0, value1, arrived1):
    feats, hidden = z.feats, z.hidden
    outputs = [
        ((1, feats, 3 * feats), f32, True),
        ((1, feats, feats), f32, True),
        ((1, feats, hidden), f32, True),
        ((1, hidden, feats), f32, True),
    ]
    outputs += [((1, feats), f32, False)] * 7
    outputs += [((1, hidden), f32, False), ((1, feats), f32, False)]
    outputs.append((*scratch_table(z)["pair"], False))
    scratch = ("all_rows", "v_triple", "v_attend", "v_widen", "v_narrow")
    kernel = partial(bind, unpack_kernel, (z,))
    return call(kernel, z, core, [value0, arrived0, value1, arrived1], outputs, scratch, 0.2)


def pair_index():
    place = np.arange(tall)
    u, w = place // 8, place % 8
    real = (u < 7) & (w < 7)
    index = (u[None, :] - u[:, None] + 6) * 13 + (w[None, :] - w[:, None] + 6)
    return np.where(real[:, None] & real[None, :], index, 169)[:cells]


def pair_onehot():
    return jnp.asarray(
        np.arange(169)[:, None] == pair_index().reshape(-1)[None, :], bf16
    )


def bias_base(table, z):
    spread = lax.dot_general(
        table, pair_onehot(), (((0,), (0,)), ((), ())), preferred_element_type=f32
    )
    spread = spread.reshape(z.groups, -1, cells, tall).transpose(0, 2, 1, 3)
    real = (np.arange(cells) % 8 < 7)[None, :, None, None]
    return (
        jnp.where(real, spread, masked_score).astype(bf16).reshape(z.groups, cells, z.lanes)
    )


def region_mask(z, step, first_row, total_rows):
    place = np.arange(tall)
    u, w = np.minimum(place // 8, 6), np.minimum(place % 8, 6)
    rows = jnp.mod(first_row + step * 7 + u + 3, total_rows)
    vertical = (rows >= total_rows - 7).astype(jnp.int32) + (rows >= total_rows - 3)
    kinds = []
    for column in (0, z.wins - 2, z.wins - 1):
        at = np.mod(column * 7 + w + 3, z.cols)
        horizontal = (at >= z.cols - 7).astype(np.int32) + (at >= z.cols - 3)
        code = vertical * 3 + horizontal
        alike = code[:cells, None] == code[None, :]
        kinds.append(jnp.where(alike, 0.0, masked_score).astype(f32))
    return jnp.stack(kinds)


def table_slope(pair, z, heads):
    pair = pair.reshape(z.groups, cells, -1, tall).transpose(1, 3, 0, 2).reshape(-1, heads)
    return mm(pair_onehot(), pair.astype(bf16))


def swap_cores(item):
    return lax.ppermute(item, "pipe", [(0, 1), (1, 0)])


def take(pair, index):
    return lax.dynamic_index_in_dim(pair, index, 0, keepdims=False)


def tie(item, *others):
    return lax.optimization_barrier((item,) + others)


class Reduction:
    near = 4

    def __init__(self, kept, sent=None):
        if sent is not None:
            kept = (kept.astype(f32) + swap_cores(sent).astype(f32)).astype(bf16)
        self.value = kept

    def partners(self, near):
        count, place = lax.axis_size("rows"), lax.axis_index("rows")
        size, unit = (self.near, 1) if near else (count // self.near, self.near)
        mine = (place // unit) % size
        return size, mine, [[(i, i ^ (d * unit)) for i in range(count)] for d in range(1, size)]

    def scatter(self, near):
        size, mine, routes = self.partners(near)
        parts = self.value.reshape((size, -1) + self.value.shape[1:])
        arrived = [
            lax.ppermute(take(parts, mine ^ d), "rows", route)
            for d, route in enumerate(routes, 1)
        ]
        total = take(parts, mine).astype(f32)
        for item in arrived:
            total = total + item.astype(f32)
        self.value = total.astype(bf16)

    def gather(self, near):
        size, mine, routes = self.partners(near)
        arrived = [lax.ppermute(self.value, "rows", route) for route in routes]
        parts = jnp.zeros((size,) + self.value.shape, bf16)
        for d, item in enumerate([self.value] + arrived):
            parts = lax.dynamic_update_index_in_dim(parts, item, mine ^ d, 0)
        self.value = parts.reshape((-1,) + self.value.shape[1:])

    def join(self, other):
        return Reduction(jnp.concatenate([self.value, other.value], 0))


def on_device(
    image_tokens,
    out_grad,
    first_gain,
    first_shift,
    triple_weight,
    query_bias,
    value_bias,
    bias_table,
    attend_weight,
    attend_bias,
    second_gain,
    second_shift,
    widen_weight,
    widen_bias,
    narrow_weight,
    narrow_bias,
):
    core = lax.axis_index("pipe")
    core_id = core.astype(jnp.int32).reshape(1)
    count = lax.axis_size("rows")
    place = lax.axis_index("rows")
    batches, own_rows, cols, feats = image_tokens.shape
    heads = bias_table.shape[2]
    hidden = widen_weight.shape[2]
    z = Sizes(own_rows, cols, feats, hidden, heads)
    total_rows = own_rows * count
    first_row = place * own_rows

    small = jnp.concatenate(
        [
            first_gain,
            first_shift,
            query_bias,
            jnp.zeros_like(query_bias),
            value_bias,
            attend_bias,
            second_gain,
            second_shift,
            narrow_bias,
            widen_bias.reshape(-1, feats),
            jnp.zeros((small_rows - 9 - hidden // feats, feats), bf16),
        ],
        0,
    ).astype(f32)
    tables = [bias_table[0], swap_cores(bias_table[0])]
    first = core == 0
    big = (triple_weight, attend_weight, widen_weight, narrow_weight)
    params = {
        "small": [small, swap_cores(small)],
        "big": [(item, swap_cores(item)) for item in big],
    }
    to_previous = [((i + 1) % count, i) for i in range(count)]
    to_next = [(i, (i + 1) % count) for i in range(count)]
    base0 = bias_base(jnp.where(first, tables[0], tables[1]), z)

    upper = [(0, True, 0, 7)]
    lower = [(0, True, 7, 7)]

    y00, y0_rim, *kept0 = run_forward(z, core_id, [image_tokens], upper, params, base0)
    y0_halo = lax.ppermute(y0_rim, "rows", to_previous)
    late_grad, late_row, late_table, _ = tie(
        out_grad, first_row, jnp.where(first, tables[1], tables[0]), y00
    )
    grad_top = lax.dynamic_slice(late_grad, (core, 0, 0, 0), (1, 3) + late_grad.shape[2:])
    grad_halo = lax.ppermute(grad_top[0], "rows", to_previous)
    masks = [region_mask(z, step, late_row, total_rows) for step in range(2)]
    base1 = bias_base(late_table, z)
    y01, _, *kept1 = run_forward(z, core_id, [image_tokens], lower, params, base0)
    (qkv0, probs0, mix0, x10, act0, slope0) = kept0
    (qkv1, probs1, mix1, x11, act1, slope1) = kept1

    y10, dx10, _, all10 = run_both(
        z, core_id, [y00, y01], [(0, False, 3, 4), (1, False, 0, 3)], [out_grad],
        [(0, True, 3, 7)], params, base1, masks[0], None,
    )
    y11, dx11, rim1, *all11 = run_both(
        z, core_id, [y01, y0_halo], [(0, False, 3, 4), (1, False, 0, 3)],
        [out_grad, grad_halo], [(0, True, 10, 4), (1, False, 0, 3)], params, base1, masks[1],
        all10,
    )
    halo1 = lax.ppermute(rim1, "rows", to_next)

    def sent(block0, block1):
        return swap_cores(jnp.where(first, block1, block0))

    def arranged(block0, block1, other):
        return jnp.where(first, jnp.stack([block0, other]), jnp.stack([other, block1]))[None]

    reduction1 = Reduction(*all11)

    gx01, small01, mats01 = run_feed_back(
        z, core_id, [dx10, dx11], [(0, False, 4, 3), (1, False, 0, 4)], params,
        [x11, act1, slope1], None,
    )
    halo1, reduction1.value = tie(halo1, reduction1.value)
    reduction1.scatter(True)
    gx00, small00, *mats00 = run_feed_back(
        z, core_id, [halo1, dx10], [(0, False, 0, 3), (1, False, 0, 4)], params,
        [x10, act0, slope0], (mats01, small01),
    )
    gx01, reduction1.value = tie(gx01, reduction1.value)
    reduction1.scatter(False)
    feed0 = Reduction(*mats00)
    dx01, rest01 = run_attend_back(
        z, core_id, [image_tokens], lower, params, [gx01, qkv1, probs1, mix1],
        jnp.zeros((small_rows, feats), f32), None, False,
    )
    gx00, reduction1.value, feed0.value = tie(gx00, reduction1.value, feed0.value)
    feed0.scatter(True)
    dq00, *rest00 = run_attend_back(
        z, core_id, [image_tokens], upper, params, [gx00, qkv0, probs0, mix0], small00, rest01,
        True,
    )
    rest00[0], feed0.value = tie(rest00[0], feed0.value)
    reduction1.gather(False)
    reduction1.gather(True)
    arrived1 = lax.ppermute(reduction1.value, "pipe", [(0, 1)])
    rest0 = Reduction(*rest00)
    dx00 = run_input(z, core_id, [image_tokens], upper, params, [gx00, dq00])
    rest0.value, y00, y01, y10, y11, dx10, dx11, halo1 = tie(
        rest0.value, y00, y01, y10, y11, dx10, dx11, halo1
    )
    hidden_out = jnp.concatenate([y00, y01], 0)
    final = jnp.concatenate([halo1[3:], y10, y11[:4]], 0)
    entry_grad = jnp.concatenate([halo1[:3], dx10, dx11[:4]], 0)
    image_grad = jnp.concatenate([dx00, dx01], 0)
    block_outputs = arranged(hidden_out, final, sent(hidden_out, final))
    input_grads = arranged(image_grad, entry_grad, sent(image_grad, entry_grad))

    rest0.scatter(True)
    rest0.value, block_outputs, input_grads = tie(rest0.value, block_outputs, input_grads)
    reduction = feed0.join(rest0)
    reduction.scatter(False)
    reduction.gather(False)
    reduction.gather(True)

    arrived0 = lax.ppermute(reduction.value, "pipe", [(1, 0)])
    (t_triple, t_attend, t_widen, t_narrow, t_gain1, t_shift1, t_query_b, t_value_b,
     t_attend_b, t_gain2, t_shift2, t_widen_b, t_narrow_b, pair) = run_unpack(
        z, core_id, reduction.value, arrived0, reduction1.value, arrived1
    )

    return (
        block_outputs,
        input_grads,
        t_gain1,
        t_shift1,
        t_triple,
        t_query_b,
        t_value_b,
        table_slope(pair, z, heads)[None],
        t_attend,
        t_attend_b,
        t_gain2,
        t_shift2,
        t_widen,
        t_widen_b,
        t_narrow,
        t_narrow_b,
    )


def solution(mesh):
    param_specs = [
        P("pipe", None),
        P("pipe", None),
        P("pipe", None, None),
        P("pipe", None),
        P("pipe", None),
        P("pipe", None, None),
        P("pipe", None, None),
        P("pipe", None),
        P("pipe", None),
        P("pipe", None),
        P("pipe", None, None),
        P("pipe", None),
        P("pipe", None, None),
        P("pipe", None),
    ]
    in_specs = (P(None, "rows", None, None),) * 2 + tuple(param_specs)
    out_specs = (P("pipe", None, "rows", None, None),) * 2 + tuple(param_specs)
    return jax.shard_map(
        on_device, mesh=mesh, in_specs=in_specs, out_specs=out_specs, check_vma=False
    )
```

```python
from functools import partial

import jax
import jax.numpy as jnp
import numpy as np
from jax import lax
from jax.experimental import pallas as pl
from jax.experimental.pallas import tpu as pltpu
from jax.sharding import PartitionSpec as P

f32 = jnp.float32
bf16 = jnp.bfloat16
epsilon = 1e-05
masked_score = -1e30
vmem_bytes = 60 * 1024 * 1024
cells = 56
tall = 64

gain1_row, shift1_row, query_bias_row, value_bias_row = 0, 1, 2, 4
attend_bias_row, gain2_row, shift2_row, narrow_bias_row, widen_bias_row = 5, 6, 7, 8, 9
s_gain1, s_shift1, s_attend_b, s_gain2, s_shift2, s_narrow_b, s_widen_b = 3, 4, 5, 6, 7, 8, 9
small_rows = 16


def mm(left, right):
    return lax.dot_general(left, right, (((1,), (0,)), ((), ())), preferred_element_type=f32)


def mm_t(left, right):
    return lax.dot_general(left, right, (((1,), (1,)), ((), ())), preferred_element_type=f32)


def t_mm(left, right):
    return lax.dot_general(left, right, (((0,), (0,)), ((), ())), preferred_element_type=f32)


def normed_parts(values):
    center = values - jnp.mean(values, -1, keepdims=True)
    spread = jnp.mean(center * center, -1, keepdims=True)
    scale = lax.rsqrt(spread + epsilon)
    return center * scale, scale


def norm_back(grad, hat, scale, gain):
    pulled = grad * gain
    return scale * (
        pulled
        - jnp.mean(pulled, -1, keepdims=True)
        - hat * jnp.mean(pulled * hat, -1, keepdims=True)
    )


def gelu_parts(value):
    below = 0.5 + 0.5 * lax.erf(value * 0.5**0.5)
    bell = jnp.exp(value * value * -0.5)
    return value * below, below + value * bell * (2.0 * np.pi) ** -0.5


def row_sum(values):
    return jnp.sum(values, 0, keepdims=True)


def head_masks(depth):
    place = lax.broadcasted_iota(jnp.int32, (1, 128), 1) // depth
    return [(place == h) for h in range(128 // depth)]


def spread_heads(part, masks):
    return jnp.concatenate([part * m.astype(bf16) for m in masks], 0)


def collect_heads(high, masks):
    rows = high.shape[0] // len(masks)
    out = high[:rows]
    for h in range(1, len(masks)):
        out = jnp.where(masks[h], high[h * rows : (h + 1) * rows], out)
    return out


def pad_rows(values, rows):
    return jnp.concatenate(
        [values, jnp.zeros((rows - values.shape[0], values.shape[1]), values.dtype)], 0
    )


def spread_matrix(cols, roll_by):
    place = lax.broadcasted_iota(jnp.int32, (cols // 7 * 8, cols), 0)
    column = lax.broadcasted_iota(jnp.int32, (cols // 7 * 8, cols), 1)
    w = place & 7
    target = (place >> 3) * 7 + w + roll_by
    target = jnp.where(target >= cols, target - cols, target)
    return jnp.where((target == column) & (w < 7), 1.0, 0.0).astype(bf16)


def image_to_windows(image, spread, out):
    for u in range(7):
        part = mm(spread, image[u])
        out[:, u * 8 : (u + 1) * 8, :] = part.reshape(-1, 8, part.shape[-1])


def windows_to_image(windows, spread, image, rim=None, first=0):
    wins, _, feats = windows.shape
    for u in range(7):
        part = windows[:, u * 8 : (u + 1) * 8, :].reshape(wins * 8, feats).astype(bf16)
        row = t_mm(spread, part).astype(bf16)
        image[u] = row
        if rim is not None and first <= u < first + 3:
            rim[u - first] = row


def by_rows(rows, parts, step):
    size = rows // parts

    def body(i, carry):
        step(i, pl.ds(pl.multiple_of(i * size, size), size))
        return carry

    lax.fori_loop(0, parts, body, 0, unroll=2)


class Copies:
    def __init__(self, core_ref, block, sems):
        self.core = core_ref[0]
        self.mine = self.core == block
        self.sems = sems
        self.count = 0
        self.writes = []

    def next(self):
        self.count += 1
        return self.sems.at[self.count - 1]

    def start(self, source, target):
        copy = pltpu.make_async_copy(source, target, self.next())
        copy.start()
        return copy

    def pick(self, pair, target):
        own, other = pair
        sem = self.next()

        @pl.when(self.mine)
        def _():
            pltpu.make_async_copy(own.at[0], target, sem).start()

        @pl.when(jnp.logical_not(self.mine))
        def _():
            pltpu.make_async_copy(other.at[0], target, sem).start()

        return pltpu.make_async_copy(own.at[0], target, sem)

    def rows(self, refs, plan, target):
        at = 0
        copies = []
        for which, batched, first, size in plan:
            source = refs[which].at[self.core] if batched else refs[which]
            copies.append(
                self.start(source.at[pl.ds(first, size)], target.at[pl.ds(at, size)])
            )
            at += size
        return copies

    def write(self, source, target):
        self.writes.append(self.start(source, target))

    def write_rows(self, source, at, outs):
        size = source.shape[0]
        if len(outs) == 1:
            self.write(source, outs[0].at[pl.ds(at, size)])
            return
        half = outs[0].shape[0]
        low = at
        while low < at + size:
            which = low // half
            high = min(at + size, (which + 1) * half)
            part = source.at[pl.ds(low - at, high - low)]
            keep, send = (out.at[pl.ds(low - which * half, high - low)] for out in outs)
            sem = self.next()
            pl.when(self.core == which)(pltpu.make_async_copy(part, keep, sem).start)
            pl.when(self.core != which)(pltpu.make_async_copy(part, send, sem).start)
            self.writes.append(pltpu.make_async_copy(part, keep, sem))
            low = high

    def finish(self):
        for copy in self.writes:
            copy.wait()

    def small(self, own, other):
        return jnp.where(self.mine, own[...], other[...])


def wait_all(copies):
    for copy in copies:
        copy.wait()


def stage_norm(xs, gain, shift, n1, kept=None):
    wins, _, feats = xs.shape

    def step(i, span):
        hat, scale = normed_parts(xs[pl.ds(i * 4, 4)].reshape(4 * cells, feats))
        if n1 is not None:
            n1[span, :] = (hat * gain + shift).astype(bf16)
        if kept is not None:
            kept[0][span, :] = hat.astype(bf16)
            kept[1][span, :] = scale

    by_rows(wins * cells, wins // 4, step)


def stage_triple(n1, triple, small, qkv):
    wins, _, width = qkv.shape
    feats = width // 3
    qkv[:, cells:, :] = jnp.zeros((wins, tall - cells, width), bf16)
    offsets = (query_bias_row, None, value_bias_row)
    for j in range(3):
        lanes = slice(j * feats, (j + 1) * feats)
        part = mm(n1[...], triple[:, lanes])
        if offsets[j] is not None:
            part = part + small[offsets[j] : offsets[j] + 1]
        qkv[:, :cells, lanes] = part.reshape(wins, cells, feats).astype(bf16)


def stage_attend(qkv, bias, probs, mixed, depth, shifted):
    wins, _, width = qkv.shape
    feats = width // 3
    masks = head_masks(depth)
    scale = depth**-0.5

    def step(w, carry):
        kind = jnp.maximum(w - (wins - 3), 0) if shifted else 0
        for g in range(feats // 128):
            at = g * 128
            q = qkv[w, :, at : at + 128]
            k = qkv[w, :, feats + at : feats + at + 128]
            v = qkv[w, :, 2 * feats + at : 2 * feats + at + 128]
            scores = mm_t(k, spread_heads(q, masks))[:cells] * scale + bias[kind, g]
            powers = jnp.exp(scores - jnp.max(scores, 0, keepdims=True))
            weights = powers * (1.0 / jnp.sum(powers, 0, keepdims=True))
            low = pad_rows(weights, tall).astype(bf16)
            probs[w, g] = low
            mixed[w, :, at : at + 128] = collect_heads(t_mm(low, v), masks)[:cells]
        return carry

    lax.fori_loop(0, wins, step, 0, unroll=16)


def forward_stages(z, block, copies, c, small, bias_parts, picks, x_waits):
    rows, feats = c.x1.shape
    base, mask = bias_parts
    base = base[...].astype(f32)
    if block == 1:
        for kind in range(3):
            for g in range(z.groups):
                c.bias[kind, g] = base[g] + jnp.concatenate(
                    [mask[kind]] * (z.lanes // tall), 1
                )
    else:
        c.bias[0] = base
    wait_all(x_waits)
    image_to_windows(c.x_rows, c.spread, c.xs)
    gain1 = small[gain1_row : gain1_row + 1]
    shift1 = small[shift1_row : shift1_row + 1]
    kept = (c.hat1, c.scale1) if hasattr(c, "hat1") else None
    stage_norm(c.xs, gain1, shift1, c.n1, kept)
    picks[0].wait()
    stage_triple(c.n1, c.triple, small, c.qkv)
    yield
    stage_attend(c.qkv, c.bias, c.probs, c.mixed, z.depth, block == 1)
    c.low_mix[...] = c.mixed[...].reshape(rows, feats).astype(bf16)
    yield
    picks[1].wait()
    c.x1[...] = (
        c.xs[...].reshape(rows, feats)
        + mm(c.low_mix[...], c.attend[...])
        + small[attend_bias_row : attend_bias_row + 1]
    )
    yield
    second_norm(small, c)
    picks[2].wait()
    part = z.hidden // z.parts
    for j in range(z.parts):
        lanes = slice(j * part, (j + 1) * part)
        offset = jnp.concatenate(
            [
                small[widen_bias_row + i : widen_bias_row + i + 1]
                for i in range(j * part // feats, (j + 1) * part // feats)
            ],
            1,
        )
        value, pull = gelu_parts(mm(c.n2[...], c.widen[:, lanes]) + offset)
        c.act[:, lanes] = value.astype(bf16)
        c.slope[:, lanes] = pull.astype(bf16)
    yield
    picks[3].wait()
    c.total[...] = (
        c.x1[...]
        + mm(c.act[...], c.narrow[...])
        + small[narrow_bias_row : narrow_bias_row + 1]
    ).reshape(c.total.shape)


def second_norm(small, c):
    gain2 = small[gain2_row : gain2_row + 1]
    shift2 = small[shift2_row : shift2_row + 1]

    def norm_step(i, span):
        hat, scale = normed_parts(c.x1[span, :])
        c.n2[span, :] = (hat * gain2 + shift2).astype(bf16)
        if hasattr(c, "hat2"):
            c.hat2[span, :] = hat.astype(bf16)
            c.scale2[span, :] = scale

    by_rows(c.x1.shape[0], 4, norm_step)


def feed_back_stages(z, copies, c, small, waits, prev, outs, o_small):
    rows, feats = c.x1.shape
    w_dy, w_narrow, w_slope, w_widen, w_x1, w_act, w_prev = waits
    wait_all(w_dy)
    image_to_windows(c.dy_rows, c.spread, c.total)
    c.dy[...] = c.total[...].reshape(rows, feats).astype(bf16)
    sums = {s_narrow_b: row_sum(c.total[...].reshape(rows, feats))}
    part = z.hidden // z.parts
    wait_all(w_narrow + w_slope)
    for j in range(z.parts):
        lanes = slice(j * part, (j + 1) * part)
        grad = mm_t(c.dy[...], c.narrow[lanes, :]) * c.slope[:, lanes].astype(f32)
        total = row_sum(grad)
        for i in range(part // feats):
            sums[s_widen_b + j * part // feats + i] = total[:, i * feats : (i + 1) * feats]
        c.dh[:, lanes] = grad.astype(bf16)
    wait_all(w_widen + w_x1)
    if w_x1:
        second_norm(small, c)
    c.dn2[...] = mm_t(c.dh[...], c.widen[...])
    gain2 = small[gain2_row : gain2_row + 1]

    def norm_step(i, span):
        hat, scale = c.hat2[span, :].astype(f32), c.scale2[span, :]
        grad = c.dn2[span, :]
        o_small[s_gain2 : s_gain2 + 1] += row_sum(grad * hat)
        o_small[s_shift2 : s_shift2 + 1] += row_sum(grad)
        c.gx1[span, :] = c.dy[span, :].astype(f32) + norm_back(grad, hat, scale, gain2)

    for at, value in sums.items():
        o_small[at : at + 1] += value
    by_rows(rows, 4, norm_step)
    yield
    wait_all(w_prev)

    def put(at, value):
        span = slice(at, at + feats)
        if prev is not None:
            value = value + prev[span, :].astype(f32)
        c.mats[span, :] = value.astype(bf16)

    for j in range(z.hidden // feats):
        put(j * feats, t_mm(c.n2[...], c.dh[:, j * feats : (j + 1) * feats]))
    half = c.mats.shape[0] // 2
    copies.write_rows(c.mats.at[pl.ds(0, half)], 0, outs)
    wait_all(w_act)
    for j in range(z.hidden // feats):
        put(z.hidden + j * feats, t_mm(c.act[:, j * feats : (j + 1) * feats], c.dy[...]))
    copies.write_rows(c.mats.at[pl.ds(half, half)], half, outs)


def attend_back_stages(z, copies, c, small, waits, prev, outs, first_row, smalls):
    w_gx1, w_attend, w_mix, w_qkv, w_x, w_triple, w_prev = waits
    wins, _, feats = c.xs.shape
    rows = wins * cells
    depth = z.depth
    masks = head_masks(depth)
    scale = depth**-0.5
    mats = 4 * feats
    qkv, probs, gmix, gqkv, pair = c.qkv, c.probs, c.gmix, c.gqkv, c.pair
    wait_all(w_gx1)
    c.da[...] = c.gx1[...].astype(bf16)
    attend_b = row_sum(c.gx1[...])
    wait_all(w_attend)
    gmix[:, cells:, :] = jnp.zeros((wins, tall - cells, feats), bf16)
    gmix[:, :cells, :] = mm_t(c.da[...], c.attend[...]).reshape(wins, cells, feats).astype(bf16)
    pair[...] = jnp.zeros_like(pair)
    wait_all(w_qkv)

    def step(w, carry):
        for g in range(feats // 128):
            at = g * 128
            q = qkv[w, :, at : at + 128]
            k = qkv[w, :, feats + at : feats + at + 128]
            v = qkv[w, :, 2 * feats + at : 2 * feats + at + 128]
            wide = spread_heads(gmix[w, :, at : at + 128], masks)
            low = probs[w, g]
            high = low.astype(f32)[:cells]
            pulled = mm_t(v, wide)[:cells] * high
            ds = pulled - high * jnp.sum(pulled, 0, keepdims=True)
            pair[g] += ds
            ds = pad_rows(ds, tall).astype(bf16)
            gqkv[w, :, 2 * feats + at : 2 * feats + at + 128] = mm(low, wide)[:cells]
            gqkv[w, :, feats + at : feats + at + 128] = (
                mm(ds, spread_heads(q, masks))[:cells] * scale
            )
            gqkv[w, :, at : at + 128] = collect_heads(t_mm(ds, k), masks)[:cells] * scale
        return carry

    lax.fori_loop(0, wins, step, 0, unroll=16)
    gain1 = small[gain1_row : gain1_row + 1]
    shift1 = small[shift1_row : shift1_row + 1]
    if w_x:
        wait_all(w_x)
        image_to_windows(c.x_rows, c.spread, c.xs)
        stage_norm(c.xs, None, None, None, (c.hat1, c.scale1))
    wait_all(w_triple + w_mix + w_prev)

    def put(at, size, value):
        if prev is not None:
            value = value + prev[at : at + size, :].astype(f32)
        c.rest[at : at + size, :] = value.astype(bf16)

    put(3 * feats, feats, t_mm(c.low_mix[...], c.da[...]))
    columns = jnp.concatenate([gain1, shift1, jnp.zeros((6, feats), f32)], 0).T
    gain_column, shift_column = columns[:, 0:1], columns[:, 1:2]
    sums = []
    gain_grad = jnp.zeros((feats, 1), f32)
    shift_grad = jnp.zeros((8, feats), f32)
    for j in range(3):
        lanes = slice(j * feats, (j + 1) * feats)
        part = gqkv[:, :, lanes].reshape(rows, feats)
        total = row_sum(part)
        sums.append(total)
        c.dq[:, lanes] = part.astype(bf16)
        both = t_mm(c.hat1[...], c.dq[:, lanes])
        put(j * feats, feats, gain_column * both + shift_column * total)
        gain_grad += jnp.sum(both * c.triple[:, lanes].astype(f32), -1, keepdims=True)
        top = total.astype(bf16)
        rest = (total - top.astype(f32)).astype(bf16)
        shift_grad += mm_t(
            jnp.concatenate([top.astype(f32), rest.astype(f32), jnp.zeros((6, feats), f32)], 0)
            .astype(bf16),
            c.triple[:, lanes],
        )
    sums.append(jnp.broadcast_to(gain_grad, (feats, 8)).T[0:1])
    sums.append(shift_grad[0:1] + shift_grad[1:2])
    sums.append(attend_b)
    put(
        mats,
        small_rows,
        smalls[...] + jnp.concatenate(sums + [jnp.zeros((small_rows - 6, feats), f32)], 0),
    )
    flat = pair[...].reshape(z.groups * cells, z.lanes)
    cut = flat.shape[0] * z.lanes // feats
    more = flat[cut:]
    put(
        mats + small_rows,
        cut,
        jnp.concatenate([flat[:cut], jnp.concatenate([more[:, :128], more[:, 128:]], 0)], 1),
    )
    end = mats + small_rows + cut
    c.rest[end:, :] = jnp.zeros((c.rest.shape[0] - end, feats), bf16)
    copies.write_rows(c.rest, first_row, outs)


def input_stages(z, c, small):
    wins, _, feats = c.xs.shape
    gain1 = small[gain1_row : gain1_row + 1]
    c.dn2[...] = mm_t(c.dq[...], c.triple[...])

    def norm_step(i, span):
        wide = pl.ds(i * 4, 4)
        hat, scale = c.hat1[span, :].astype(f32), c.scale1[span, :]
        out = c.gx1[span, :] + norm_back(c.dn2[span, :], hat, scale, gain1)
        c.xs[wide] = out.reshape(4, cells, feats)

    by_rows(wins * cells, wins // 4, norm_step)


class Refs:
    def __init__(self, refs, names):
        self.refs = list(refs)
        for name in names:
            setattr(self, name, self.refs.pop(0))

    def several(self, number):
        return [self.refs.pop(0) for _ in range(number)]

    def pairs(self, number):
        return [tuple(self.several(2)) for _ in range(number)]

    def name(self, names):
        for name in names:
            setattr(self, name, self.refs.pop(0))


def forward_kernel(z, n_x, x_plan, scratch, core_ref, *refs):
    c = Refs(refs, ())
    x_refs = c.several(n_x)
    c.name(("own", "other", "base"))
    big = c.pairs(4)
    c.name(("y", "rim", "o_qkv", "o_probs", "o_mix", "o_x1", "o_act", "o_slope"))
    c.name(scratch)
    copies = Copies(core_ref, 0, c.sems)
    x_waits = copies.rows(x_refs, x_plan, c.x_rows)
    picks = [copies.pick(p, to) for p, to in zip(big, (c.triple, c.attend, c.widen, c.narrow))]
    small = copies.small(c.own, c.other)
    c.spread = spread_matrix(z.cols, 0)
    stages = forward_stages(z, 0, copies, c, small, (c.base, None), picks, x_waits)
    next(stages)
    copies.write(c.qkv, c.o_qkv)
    next(stages)
    copies.write(c.probs, c.o_probs)
    copies.write(c.low_mix, c.o_mix)
    next(stages)
    copies.write(c.x1, c.o_x1)
    next(stages)
    copies.write(c.act, c.o_act)
    copies.write(c.slope, c.o_slope)
    for _ in stages:
        pass
    windows_to_image(c.total, c.spread, c.y, c.rim, 0)
    copies.finish()


def both_kernel(z, n_x, x_plan, n_dy, dy_plan, chained, scratch, core_ref, *refs):
    c = Refs(refs, ())
    x_refs = c.several(n_x)
    dy_refs = c.several(n_dy)
    c.name(("own", "other", "base", "mask"))
    big = c.pairs(4)
    prev = c.several(1) if chained else None
    c.name(("y", "dx", "rim"))
    outs = c.several(2 if chained else 1)
    c.name(scratch)
    copies = Copies(core_ref, 1, c.sems)
    x_waits = copies.rows(x_refs, x_plan, c.x_rows)
    picks = [copies.pick(p, to) for p, to in zip(big, (c.triple, c.attend, c.widen, c.narrow))]
    dy_waits = copies.rows(dy_refs, dy_plan, c.dy_rows)
    prev_waits = [[], []]
    if chained:
        parts = ((0, c.prev_mats), (z.feed_rows, c.prev_rest))
        prev_waits = [
            [copies.start(prev[0].at[pl.ds(at, to.shape[0])], to)] for at, to in parts
        ]
    prev_refs = (c.prev_mats, c.prev_rest) if chained else (None, None)
    small = copies.small(c.own, c.other)
    c.spread = spread_matrix(z.cols, 3)
    c.smalls[...] = jnp.zeros_like(c.smalls)
    for _ in forward_stages(z, 1, copies, c, small, (c.base, c.mask), picks, x_waits):
        pass
    windows_to_image(c.total, c.spread, c.y, c.rim.at[pl.ds(3, 3)], 4)
    waits = (dy_waits, [], [], [], [], [], prev_waits[0])
    for _ in feed_back_stages(z, copies, c, small, waits, prev_refs[0], outs, c.smalls):
        pass
    waits = ([], [], [], [], [], [], prev_waits[1])
    attend_back_stages(z, copies, c, small, waits, prev_refs[1], outs, z.feed_rows, c.smalls)
    input_stages(z, c, small)
    windows_to_image(c.xs, c.spread, c.dx, c.rim.at[pl.ds(0, 3)], 4)
    copies.finish()


def feed_back_kernel(z, n_dy, dy_plan, chained, scratch, core_ref, *refs):
    c = Refs(refs, ())
    dy_refs = c.several(n_dy)
    c.name(("own", "other"))
    big = c.pairs(2)
    kept = c.several(3)
    prev = c.several(2) if chained else None
    c.name(("o_gx1", "o_small"))
    outs = c.several(2 if chained else 1)
    c.name(scratch)
    copies = Copies(core_ref, 0, c.sems)
    w_dy = copies.rows(dy_refs, dy_plan, c.dy_rows)
    w_narrow = copies.pick(big[1], c.narrow)
    w_slope = copies.start(kept[2], c.slope)
    w_widen = copies.pick(big[0], c.widen)
    w_x1 = copies.start(kept[0], c.x1)
    w_act = copies.start(kept[1], c.act)
    w_prev = [copies.start(prev[0], c.prev_mats)] if chained else []
    small = copies.small(c.own, c.other)
    c.spread = spread_matrix(z.cols, 0)
    c.o_small[...] = prev[1][...] if chained else jnp.zeros_like(c.o_small)
    waits = (w_dy, [w_narrow], [w_slope], [w_widen], [w_x1], [w_act], w_prev)
    stages = feed_back_stages(
        z, copies, c, small, waits, c.prev_mats if chained else None, outs, c.o_small
    )
    next(stages)
    copies.write(c.gx1, c.o_gx1)
    for _ in stages:
        pass
    copies.finish()


def attend_back_kernel(z, n_x, x_plan, chained, last, scratch, core_ref, *refs):
    c = Refs(refs, ())
    x_refs = c.several(n_x)
    c.name(("own", "other"))
    big = c.pairs(2)
    kept = c.several(4)
    c.name(("smalls",))
    prev = c.several(1) if chained else None
    c.name(("out",))
    outs = c.several(2 if chained else 1)
    c.name(scratch)
    copies = Copies(core_ref, 0, c.sems)
    w_gx1 = copies.start(kept[0], c.gx1)
    w_attend = copies.pick(big[1], c.attend)
    w_qkv = [copies.start(kept[1], c.qkv), copies.start(kept[2], c.probs)]
    w_x = copies.rows(x_refs, x_plan, c.x_rows)
    w_mix = copies.start(kept[3], c.low_mix)
    w_triple = copies.pick(big[0], c.triple)
    w_prev = [copies.start(prev[0], c.prev_rest)] if chained else []
    small = copies.small(c.own, c.other)
    c.spread = spread_matrix(z.cols, 0)
    waits = ([w_gx1], [w_attend], [w_mix], w_qkv, w_x, [w_triple], w_prev)
    attend_back_stages(
        z, copies, c, small, waits, c.prev_rest if chained else None, outs, 0, c.smalls
    )
    if last:
        copies.write(c.dq, c.out)
    else:
        input_stages(z, c, small)
        windows_to_image(c.xs, c.spread, c.out)
    copies.finish()


def input_kernel(z, n_x, x_plan, scratch, core_ref, *refs):
    c = Refs(refs, ())
    x_refs = c.several(n_x)
    c.name(("own", "other"))
    big = c.pairs(1)
    kept = c.several(2)
    c.name(("out",))
    c.name(scratch)
    copies = Copies(core_ref, 0, c.sems)
    w_dq = copies.start(kept[1], c.dq)
    w_triple = copies.pick(big[0], c.triple)
    w_x = copies.rows(x_refs, x_plan, c.x_rows)
    w_gx1 = copies.start(kept[0], c.gx1)
    small = copies.small(c.own, c.other)
    c.spread = spread_matrix(z.cols, 0)
    wait_all(w_x)
    image_to_windows(c.x_rows, c.spread, c.xs)
    stage_norm(c.xs, None, None, None, (c.hat1, c.scale1))
    wait_all([w_dq, w_triple, w_gx1])
    input_stages(z, c, small)
    windows_to_image(c.xs, c.spread, c.out)
    copies.finish()


def unpack_kernel(z, scratch, core_ref, *refs):
    c = Refs(refs, ("value0", "arrived0", "value1", "arrived1"))
    c.name(("triple", "attend", "widen", "narrow", "gain1", "shift1", "query_b", "value_b",
            "attend_b", "gain2", "shift2", "widen_b", "narrow_b", "pair"))
    c.name(scratch)
    copies = Copies(core_ref, 0, c.sems)
    feats, hidden = z.feats, z.hidden
    waits = [[], [], []]

    def fetch(stage, at, size, from0, from1):
        target = c.all_rows.at[pl.ds(at, size)]
        sem = copies.next()
        copy0, copy1 = (
            pltpu.make_async_copy(ref.at[pl.ds(row, size)], target, sem)
            for ref, row in (from0, from1)
        )
        pl.when(copies.mine)(copy0.start)
        pl.when(jnp.logical_not(copies.mine))(copy1.start)
        waits[stage].append(copy1)

    total = z.feed_rows + z.attend_rows
    quarters = (z.feed_rows // 8, z.attend_rows // 8)
    piece = sum(quarters)
    for half, source0 in enumerate((c.value0, c.arrived0)):
        for which, quarter in enumerate(quarters):
            for i in range(4):
                at = which * z.feed_rows + (half * 4 + i) * quarter
                row0 = i * piece + which * quarters[0]
                cuts = [at, at + quarter]
                if at < total // 2 < at + quarter:
                    cuts.insert(1, total // 2)
                for low, high in zip(cuts, cuts[1:]):
                    if low < total // 2:
                        from1 = (c.arrived1, low)
                    else:
                        from1 = (c.value1, low - total // 2)
                    stage = 2 if which else half
                    fetch(stage, low, high - low, (source0, row0 + low - at), from1)

    def rows(first, size):
        return c.all_rows[first : first + size, :].astype(f32)

    wait_all(waits[0])
    for j in range(hidden // feats):
        c.v_widen[:, j * feats : (j + 1) * feats] = rows(j * feats, feats)
    copies.write(c.v_widen, c.widen.at[0])
    wait_all(waits[1])
    c.v_narrow[...] = rows(hidden, hidden)
    copies.write(c.v_narrow, c.narrow.at[0])
    wait_all(waits[2])
    at = z.feed_rows
    for j in range(3):
        c.v_triple[:, j * feats : (j + 1) * feats] = rows(at + j * feats, feats)
    copies.write(c.v_triple, c.triple.at[0])
    c.v_attend[...] = rows(at + 3 * feats, feats)
    copies.write(c.v_attend, c.attend.at[0])
    at += 4 * feats
    smalls = rows(at, small_rows)
    for ref, row in ((c.query_b, 0), (c.value_b, 2), (c.gain1, s_gain1), (c.shift1, s_shift1),
                     (c.attend_b, s_attend_b), (c.gain2, s_gain2), (c.shift2, s_shift2),
                     (c.narrow_b, s_narrow_b)):
        ref[...] = smalls[row : row + 1]
    for j in range(hidden // feats):
        row = s_widen_b + j
        c.widen_b[:, j * feats : (j + 1) * feats] = smalls[row : row + 1]
    at += small_rows
    cut = z.groups * cells * z.lanes // feats
    flat = rows(at, cut)
    left = z.groups * cells - cut
    more = flat[:, z.lanes :]
    c.pair[...] = jnp.concatenate(
        [flat[:, : z.lanes], jnp.concatenate([more[:left], more[left:]], 1)], 0
    ).reshape(c.pair.shape)
    copies.finish()


class Sizes:
    def __init__(self, own_rows, cols, feats, hidden, heads):
        self.steps = own_rows // 7
        self.cols = cols
        self.feats = feats
        self.hidden = hidden
        self.wins = cols // 7
        self.rows = self.wins * cells
        self.depth = feats // heads
        self.groups = feats // 128
        self.lanes = 128 // self.depth * tall
        self.parts = 2
        self.feed_rows = 2 * hidden
        rows = self.feed_rows + 4 * feats + small_rows + self.groups * cells * self.lanes // feats
        self.attend_rows = -(-rows // 256) * 256 - self.feed_rows


def in_vmem(item):
    return pl.BlockSpec(item.shape, lambda i, c: (0,) * item.ndim)


hbm = pl.BlockSpec(memory_space=pl.ANY)


def shaped(shape, kind):
    return jax.ShapeDtypeStruct(shape, kind)


def scratch_table(z):
    feats, hidden, rows, wins = z.feats, z.hidden, z.rows, z.wins
    image = ((7, z.cols, feats), bf16)
    wide = ((wins, cells, feats), f32)
    low = ((rows, feats), bf16)
    high = ((rows, feats), f32)
    deep = ((rows, hidden), bf16)
    return {
        "triple": ((feats, 3 * feats), bf16),
        "attend": ((feats, feats), bf16),
        "widen": ((feats, hidden), bf16),
        "narrow": ((hidden, feats), bf16),
        "x_rows": image,
        "dy_rows": image,
        "xs": wide,
        "n1": low,
        "hat1": low,
        "hat2": low,
        "scale1": ((rows, 1), f32),
        "scale2": ((rows, 1), f32),
        "qkv": ((wins, tall, 3 * feats), bf16),
        "bias": ((3, z.groups, cells, z.lanes), f32),
        "probs": ((wins, z.groups, tall, z.lanes), bf16),
        "mixed": wide,
        "low_mix": low,
        "x1": high,
        "n2": low,
        "act": deep,
        "slope": deep,
        "total": wide,
        "dy": low,
        "dh": deep,
        "dn2": high,
        "gx1": high,
        "mats": ((z.feed_rows, feats), bf16),
        "prev_mats": ((z.feed_rows, feats), bf16),
        "smalls": ((small_rows, feats), f32),
        "da": low,
        "gmix": ((wins, tall, feats), bf16),
        "gqkv": ((wins, cells, 3 * feats), f32),
        "dq": ((rows, 3 * feats), bf16),
        "pair": ((z.groups, cells, z.lanes), f32),
        "rest": ((z.attend_rows, feats), bf16),
        "prev_rest": ((z.attend_rows, feats), bf16),
        "all_rows": ((z.feed_rows + z.attend_rows, feats), bf16),
        "v_triple": ((feats, 3 * feats), f32),
        "v_attend": ((feats, feats), f32),
        "v_widen": ((feats, hidden), f32),
        "v_narrow": ((hidden, feats), f32),
    }


def call(kernel, z, core, inputs, outputs, scratch, passes):
    inputs = [item if isinstance(item, tuple) else (item, hbm) for item in inputs]
    out_specs = [
        hbm if manual else pl.BlockSpec(shape, lambda i, c, n=len(shape): (0,) * n)
        for shape, _, manual in outputs
    ]
    table = scratch_table(z)
    return pl.pallas_call(
        partial(kernel, scratch + ("sems",)),
        grid_spec=pltpu.PrefetchScalarGridSpec(
            num_scalar_prefetch=1,
            grid=(1,),
            in_specs=[spec for _, spec in inputs],
            out_specs=out_specs,
            scratch_shapes=[pltpu.VMEM(*table[name]) for name in scratch]
            + [pltpu.SemaphoreType.DMA((24,))],
        ),
        out_shape=[shaped(shape, kind) for shape, kind, _ in outputs],
        compiler_params=pltpu.CompilerParams(
            dimension_semantics=("arbitrary",), vmem_limit_bytes=vmem_bytes
        ),
        cost_estimate=pl.CostEstimate(
            flops=int(passes * 20 * z.rows * z.feats * (4 * z.feats + 2 * z.hidden)),
            bytes_accessed=int(passes * 300_000_000),
            transcendentals=0,
        ),
    )(core, *(item for item, _ in inputs))


def gradient_outputs(z, rows, chained):
    return [((rows // 2, z.feats), bf16, True)] * 2 if chained else [((rows, z.feats), bf16, True)]


def resident(items):
    return [(item, in_vmem(item)) for item in items]


def flat_pairs(pairs):
    return [item for pair in pairs for item in pair]


forward_scratch = (
    "triple", "attend", "widen", "narrow", "x_rows", "xs", "n1", "qkv", "bias", "probs", "mixed",
    "low_mix", "x1", "n2", "act", "slope", "total",
)
back_scratch = ("dy_rows", "dy", "dh", "dn2", "gx1", "mats", "hat2", "scale2")
attend_back_scratch = ("da", "gmix", "gqkv", "dq", "pair", "rest", "hat1", "scale1")


def run_forward(z, core, xs, x_plan, params, base):
    inputs = list(xs) + resident(params["small"] + [base]) + flat_pairs(params["big"])
    table = scratch_table(z)
    rim = ((3, z.cols, z.feats), bf16, False)
    outputs = [(*table["x_rows"], False), rim] + [
        (*table[name], True) for name in ("qkv", "probs", "low_mix", "x1", "act", "slope")
    ]
    kernel = partial(bind, forward_kernel, (z, len(xs), x_plan))
    return call(kernel, z, core, inputs, outputs, forward_scratch, 1.2)


def bind(kernel, arguments, scratch, *refs):
    kernel(*arguments, scratch, *refs)


def run_both(z, core, xs, x_plan, dys, dy_plan, params, base, mask, prev):
    inputs = list(xs) + list(dys) + resident(params["small"] + [base, mask])
    inputs += flat_pairs(params["big"]) + ([] if prev is None else [prev])
    table = scratch_table(z)
    image = (*table["x_rows"], False)
    outputs = [image, image, ((6, z.cols, z.feats), bf16, False)]
    outputs += gradient_outputs(z, z.feed_rows + z.attend_rows, prev is not None)
    scratch = forward_scratch + back_scratch + attend_back_scratch + ("smalls",)
    if prev is not None:
        scratch += ("prev_mats", "prev_rest")
    arguments = (z, len(xs), x_plan, len(dys), dy_plan, prev is not None)
    return call(partial(bind, both_kernel, arguments), z, core, inputs, outputs, scratch, 4.0)


def run_feed_back(z, core, dys, dy_plan, params, kept, prev):
    inputs = list(dys) + resident(params["small"]) + flat_pairs(params["big"][2:]) + list(kept)
    if prev:
        inputs += [prev[0]] + resident(prev[1:])
    table = scratch_table(z)
    outputs = [(*table["gx1"], True), (*table["smalls"], False)]
    outputs += gradient_outputs(z, z.feed_rows, bool(prev))
    scratch = back_scratch + ("widen", "narrow", "x1", "n2", "act", "slope", "total")
    if prev:
        scratch += ("prev_mats",)
    arguments = (z, len(dys), dy_plan, bool(prev))
    return call(
        partial(bind, feed_back_kernel, arguments), z, core, inputs, outputs, scratch, 1.2
    )


def run_attend_back(z, core, xs, x_plan, params, kept, smalls, prev, last):
    inputs = list(xs) + resident(params["small"]) + flat_pairs(params["big"][:2]) + list(kept)
    inputs += resident([smalls])
    if prev is not None:
        inputs.append(prev)
    table = scratch_table(z)
    outputs = [(*table["dq"], True) if last else (*table["x_rows"], False)]
    outputs += gradient_outputs(z, z.attend_rows, prev is not None)
    scratch = attend_back_scratch + (
        "triple", "attend", "x_rows", "xs", "qkv", "probs", "low_mix", "gx1", "dn2",
    )
    if prev is not None:
        scratch += ("prev_rest",)
    arguments = (z, len(xs), x_plan, prev is not None, last)
    return call(
        partial(bind, attend_back_kernel, arguments), z, core, inputs, outputs, scratch, 1.5
    )


def run_input(z, core, xs, x_plan, params, kept):
    inputs = list(xs) + resident(params["small"]) + flat_pairs(params["big"][:1]) + list(kept)
    scratch = ("triple", "x_rows", "xs", "gx1", "dq", "dn2", "hat1", "scale1")
    arguments = (z, len(xs), x_plan)
    outputs = [(*scratch_table(z)["x_rows"], False)]
    return call(partial(bind, input_kernel, arguments), z, core, inputs, outputs, scratch, 0.4)[0]


def run_unpack(z, core, value0, arrived0, value1, arrived1):
    feats, hidden = z.feats, z.hidden
    outputs = [
        ((1, feats, 3 * feats), f32, True),
        ((1, feats, feats), f32, True),
        ((1, feats, hidden), f32, True),
        ((1, hidden, feats), f32, True),
    ]
    outputs += [((1, feats), f32, False)] * 7
    outputs += [((1, hidden), f32, False), ((1, feats), f32, False)]
    outputs.append((*scratch_table(z)["pair"], False))
    scratch = ("all_rows", "v_triple", "v_attend", "v_widen", "v_narrow")
    kernel = partial(bind, unpack_kernel, (z,))
    return call(kernel, z, core, [value0, arrived0, value1, arrived1], outputs, scratch, 0.2)


def pair_index():
    place = np.arange(tall)
    u, w = place // 8, place % 8
    real = (u < 7) & (w < 7)
    index = (u[None, :] - u[:, None] + 6) * 13 + (w[None, :] - w[:, None] + 6)
    return np.where(real[:, None] & real[None, :], index, 169)[:cells]


def pair_onehot():
    return jnp.asarray(
        np.arange(169)[:, None] == pair_index().reshape(-1)[None, :], bf16
    )


def bias_base(table, z):
    spread = lax.dot_general(
        table, pair_onehot(), (((0,), (0,)), ((), ())), preferred_element_type=f32
    )
    spread = spread.reshape(z.groups, -1, cells, tall).transpose(0, 2, 1, 3)
    real = (np.arange(cells) % 8 < 7)[None, :, None, None]
    return (
        jnp.where(real, spread, masked_score).astype(bf16).reshape(z.groups, cells, z.lanes)
    )


def region_mask(z, step, first_row, total_rows):
    place = np.arange(tall)
    u, w = np.minimum(place // 8, 6), np.minimum(place % 8, 6)
    rows = jnp.mod(first_row + step * 7 + u + 3, total_rows)
    vertical = (rows >= total_rows - 7).astype(jnp.int32) + (rows >= total_rows - 3)
    kinds = []
    for column in (0, z.wins - 2, z.wins - 1):
        at = np.mod(column * 7 + w + 3, z.cols)
        horizontal = (at >= z.cols - 7).astype(np.int32) + (at >= z.cols - 3)
        code = vertical * 3 + horizontal
        alike = code[:cells, None] == code[None, :]
        kinds.append(jnp.where(alike, 0.0, masked_score).astype(f32))
    return jnp.stack(kinds)


def table_slope(pair, z, heads):
    pair = pair.reshape(z.groups, cells, -1, tall).transpose(1, 3, 0, 2).reshape(-1, heads)
    return mm(pair_onehot(), pair.astype(bf16))


def swap_cores(item):
    return lax.ppermute(item, "pipe", [(0, 1), (1, 0)])


def take(pair, index):
    return lax.dynamic_index_in_dim(pair, index, 0, keepdims=False)


def tie(item, *others):
    return lax.optimization_barrier((item,) + others)


class Reduction:
    near = 4

    def __init__(self, kept, sent=None):
        if sent is not None:
            kept = (kept.astype(f32) + swap_cores(sent).astype(f32)).astype(bf16)
        self.value = kept

    def partners(self, near):
        count, place = lax.axis_size("rows"), lax.axis_index("rows")
        size, unit = (self.near, 1) if near else (count // self.near, self.near)
        mine = (place // unit) % size
        return size, mine, [[(i, i ^ (d * unit)) for i in range(count)] for d in range(1, size)]

    def scatter(self, near):
        size, mine, routes = self.partners(near)
        parts = self.value.reshape((size, -1) + self.value.shape[1:])
        arrived = [
            lax.ppermute(take(parts, mine ^ d), "rows", route)
            for d, route in enumerate(routes, 1)
        ]
        total = take(parts, mine).astype(f32)
        for item in arrived:
            total = total + item.astype(f32)
        self.value = total.astype(bf16)

    def gather(self, near):
        size, mine, routes = self.partners(near)
        arrived = [lax.ppermute(self.value, "rows", route) for route in routes]
        parts = jnp.zeros((size,) + self.value.shape, bf16)
        for d, item in enumerate([self.value] + arrived):
            parts = lax.dynamic_update_index_in_dim(parts, item, mine ^ d, 0)
        self.value = parts.reshape((-1,) + self.value.shape[1:])

    def join(self, other):
        return Reduction(jnp.concatenate([self.value, other.value], 0))


def on_device(
    image_tokens,
    out_grad,
    first_gain,
    first_shift,
    triple_weight,
    query_bias,
    value_bias,
    bias_table,
    attend_weight,
    attend_bias,
    second_gain,
    second_shift,
    widen_weight,
    widen_bias,
    narrow_weight,
    narrow_bias,
):
    core = lax.axis_index("pipe")
    core_id = core.astype(jnp.int32).reshape(1)
    count = lax.axis_size("rows")
    place = lax.axis_index("rows")
    batches, own_rows, cols, feats = image_tokens.shape
    heads = bias_table.shape[2]
    hidden = widen_weight.shape[2]
    z = Sizes(own_rows, cols, feats, hidden, heads)
    total_rows = own_rows * count
    first_row = place * own_rows

    small = jnp.concatenate(
        [
            first_gain,
            first_shift,
            query_bias,
            jnp.zeros_like(query_bias),
            value_bias,
            attend_bias,
            second_gain,
            second_shift,
            narrow_bias,
            widen_bias.reshape(-1, feats),
            jnp.zeros((small_rows - 9 - hidden // feats, feats), bf16),
        ],
        0,
    ).astype(f32)
    tables = [bias_table[0], swap_cores(bias_table[0])]
    first = core == 0
    big = (triple_weight, attend_weight, widen_weight, narrow_weight)
    params = {
        "small": [small, swap_cores(small)],
        "big": [(item, swap_cores(item)) for item in big],
    }
    to_previous = [((i + 1) % count, i) for i in range(count)]
    to_next = [(i, (i + 1) % count) for i in range(count)]
    base0 = bias_base(jnp.where(first, tables[0], tables[1]), z)

    upper = [(0, True, 0, 7)]
    lower = [(0, True, 7, 7)]

    y00, y0_rim, *kept0 = run_forward(z, core_id, [image_tokens], upper, params, base0)
    y0_halo = lax.ppermute(y0_rim, "rows", to_previous)
    late_grad, late_row, late_table, _ = tie(
        out_grad, first_row, jnp.where(first, tables[1], tables[0]), y00
    )
    grad_top = lax.dynamic_slice(late_grad, (core, 0, 0, 0), (1, 3) + late_grad.shape[2:])
    grad_halo = lax.ppermute(grad_top[0], "rows", to_previous)
    masks = [region_mask(z, step, late_row, total_rows) for step in range(2)]
    base1 = bias_base(late_table, z)
    y01, _, *kept1 = run_forward(z, core_id, [image_tokens], lower, params, base0)
    (qkv0, probs0, mix0, x10, act0, slope0) = kept0
    (qkv1, probs1, mix1, x11, act1, slope1) = kept1

    y10, dx10, _, all10 = run_both(
        z, core_id, [y00, y01], [(0, False, 3, 4), (1, False, 0, 3)], [out_grad],
        [(0, True, 3, 7)], params, base1, masks[0], None,
    )
    y11, dx11, rim1, *all11 = run_both(
        z, core_id, [y01, y0_halo], [(0, False, 3, 4), (1, False, 0, 3)],
        [out_grad, grad_halo], [(0, True, 10, 4), (1, False, 0, 3)], params, base1, masks[1],
        all10,
    )
    halo1 = lax.ppermute(rim1, "rows", to_next)

    def sent(block0, block1):
        return swap_cores(jnp.where(first, block1, block0))

    def arranged(block0, block1, other):
        return jnp.where(first, jnp.stack([block0, other]), jnp.stack([other, block1]))[None]

    reduction1 = Reduction(*all11)

    gx01, small01, mats01 = run_feed_back(
        z, core_id, [dx10, dx11], [(0, False, 4, 3), (1, False, 0, 4)], params,
        [x11, act1, slope1], None,
    )
    halo1, reduction1.value = tie(halo1, reduction1.value)
    reduction1.scatter(True)
    gx00, small00, *mats00 = run_feed_back(
        z, core_id, [halo1, dx10], [(0, False, 0, 3), (1, False, 0, 4)], params,
        [x10, act0, slope0], (mats01, small01),
    )
    gx01, reduction1.value = tie(gx01, reduction1.value)
    reduction1.scatter(False)
    feed0 = Reduction(*mats00)
    dx01, rest01 = run_attend_back(
        z, core_id, [image_tokens], lower, params, [gx01, qkv1, probs1, mix1],
        jnp.zeros((small_rows, feats), f32), None, False,
    )
    gx00, reduction1.value, feed0.value = tie(gx00, reduction1.value, feed0.value)
    feed0.scatter(True)
    dq00, *rest00 = run_attend_back(
        z, core_id, [image_tokens], upper, params, [gx00, qkv0, probs0, mix0], small00, rest01,
        True,
    )
    rest00[0], feed0.value = tie(rest00[0], feed0.value)
    reduction1.gather(False)
    reduction1.gather(True)
    arrived1 = lax.ppermute(reduction1.value, "pipe", [(0, 1)])
    rest0 = Reduction(*rest00)
    dx00 = run_input(z, core_id, [image_tokens], upper, params, [gx00, dq00])
    rest0.value, y00, y01, y10, y11, dx10, dx11, halo1 = tie(
        rest0.value, y00, y01, y10, y11, dx10, dx11, halo1
    )
    hidden_out = jnp.concatenate([y00, y01], 0)
    final = jnp.concatenate([halo1[3:], y10, y11[:4]], 0)
    entry_grad = jnp.concatenate([halo1[:3], dx10, dx11[:4]], 0)
    image_grad = jnp.concatenate([dx00, dx01], 0)
    block_outputs = arranged(hidden_out, final, sent(hidden_out, final))
    input_grads = arranged(image_grad, entry_grad, sent(image_grad, entry_grad))

    rest0.scatter(True)
    rest0.value, block_outputs, input_grads = tie(rest0.value, block_outputs, input_grads)
    reduction = feed0.join(rest0)
    reduction.scatter(False)
    reduction.gather(False)
    reduction.gather(True)

    arrived0 = lax.ppermute(reduction.value, "pipe", [(1, 0)])
    (t_triple, t_attend, t_widen, t_narrow, t_gain1, t_shift1, t_query_b, t_value_b,
     t_attend_b, t_gain2, t_shift2, t_widen_b, t_narrow_b, pair) = run_unpack(
        z, core_id, reduction.value, arrived0, reduction1.value, arrived1
    )

    return (
        block_outputs,
        input_grads,
        t_gain1,
        t_shift1,
        t_triple,
        t_query_b,
        t_value_b,
        table_slope(pair, z, heads)[None],
        t_attend,
        t_attend_b,
        t_gain2,
        t_shift2,
        t_widen,
        t_widen_b,
        t_narrow,
        t_narrow_b,
    )


def solution(mesh):
    param_specs = [
        P("pipe", None),
        P("pipe", None),
        P("pipe", None, None),
        P("pipe", None),
        P("pipe", None),
        P("pipe", None, None),
        P("pipe", None, None),
        P("pipe", None),
        P("pipe", None),
        P("pipe", None),
        P("pipe", None, None),
        P("pipe", None),
        P("pipe", None, None),
        P("pipe", None),
    ]
    in_specs = (P(None, "rows", None, None),) * 2 + tuple(param_specs)
    out_specs = (P("pipe", None, "rows", None, None),) * 2 + tuple(param_specs)
    return jax.shard_map(
        on_device, mesh=mesh, in_specs=in_specs, out_specs=out_specs, check_vma=False
    )
```
